32 devices in a mesh: dom: 8 (over z, y), rep: 4 (over x, core).
Axes of the slice: x: 2, y: 2, z: 4, core: 2. Of those that a mesh axis runs over, the one named last changes fastest.
Arguments:
- coords: float32 [8, 3, 8192], P('dom'), may hold values from -6 to 6
- disp: float32 [8, 3, 8192], P('dom'), may hold values from -4 to 4
- mass: float32 [8, 8192], P('dom'), may hold values from 0.5 to 4
- stiffness: float32 [24, 24], replicated, may hold values from -1.25 to 1.25
- elem_nodes: int32 [8, 8, 4096], P('dom', None, 'rep'), may hold values from 0 to 8191
- modulus: float32 [8, 4096], P('dom', 'rep'), may hold values from 0.3 to 3
- surf_nodes: int32 [8, 128, 128], P('dom'), may hold values from 0 to 8191
- block_region: int32 [8, 128], P('dom'), may hold values from 0 to 7, as said below
- face_pos: float32 [8, 64, 3, 128], P('dom'), may hold values from -6 to 6
- face_normal: float32 [8, 64, 3, 128], P('dom'), may hold values from -6 to 6
- tile_slot: int32 [8, 32], P('dom', 'rep'), may hold values from 0 to 255, as said below
- tile_face: int32 [8, 32], P('dom', 'rep'), may hold values from 0 to 63
- tile_weight: bfloat16 [8, 32, 128, 128], P('dom', 'rep'), may hold values from -0.5 to 0.5
- shared_lo: int32 [8, 512], P('dom'), may hold values from 0 to 8191
- shared_hi: int32 [8, 512], P('dom'), may hold values from 0 to 8191
Outputs:
- accel: float32 [8, 3, 8192], P('dom')
The draws below stay inside these ranges and needn't reach their ends.
Inputs may be any that keep to these rules, and one draw needn't show every extreme that they name: `block_region`: each partition's blocks come in runs of 32: blocks b with equal b // 32 share a box, and the 4 runs go to distinct boxes, so a partition sends at most 32 blocks to one box. Partition s always sends a run to each of the boxes s + 1, s - 1 and s + 8 // 2 (counted round). `tile_slot`: slot source * 32 + c with c < 32, where the source partition sends blocks to this box.
All inputs are finite; a program needn't handle non-finite values.
Results may differ from the reference program's by a relative error of at most 0.0065.
Values may be sent and summed in bfloat16 or wider, within the bound.
No kernel may reach another device: no remote copies, remote signals or barrier semaphores. Data moves between devices by JAX's collectives and lax.ppermute only.
A program may use at most 64 MiB of HBM per device.

```python
import math
import jax
import jax.numpy as jnp
from jax import lax

BLOCK = 128
NP = 8192
SB = 128
FB = 64
SH = 512
DOMAIN_PARTS = 8
CAP = 32
NE = 4096
TILES = 32


def chosen_boxes(key):
    parts_index = jnp.arange(DOMAIN_PARTS, dtype=jnp.int32)
    offset = (parts_index[None, :] - parts_index[:, None]) % DOMAIN_PARTS
    forced = (offset == 1) | (offset == DOMAIN_PARTS - 1) | (offset == DOMAIN_PARTS // 2)
    forced_reward = jnp.where(forced, 2 ** 15, 0).astype(jnp.int32)
    busiest_rank = jax.random.permutation(jax.random.fold_in(key, 101), DOMAIN_PARTS)
    extra_reward = jnp.where(busiest_rank < max(DOMAIN_PARTS // 8, 1), 2 ** 14, 0).astype(jnp.int32)
    box_rating = jax.random.randint(jax.random.fold_in(key, 102), (DOMAIN_PARTS, DOMAIN_PARTS), 0, 2 ** 14)
    unique_boxes = (box_rating + extra_reward[None, :] + forced_reward) * DOMAIN_PARTS + parts_index[None, :]
    return lax.top_k(unique_boxes, SB // CAP)[1].astype(jnp.int32)


def draw_block_region(key, part):
    chosen = chosen_boxes(key)
    return jnp.repeat(chosen, CAP, axis=1).astype(jnp.int32)


def draw_tile_slot(key, part):
    chosen = chosen_boxes(key)
    key = jax.random.fold_in(key, 2)
    boxes = jnp.arange(DOMAIN_PARTS, dtype=jnp.int32)
    live = jnp.any(chosen[None, :, :] == boxes[:, None, None], axis=2)
    box_rating = jax.random.randint(jax.random.fold_in(key, 3), (DOMAIN_PARTS, TILES, DOMAIN_PARTS), 0, 2 ** 14)
    unique_boxes = box_rating * DOMAIN_PARTS + boxes[None, None, :]
    masked = jnp.where(live[:, None, :], unique_boxes, -1)
    anywhere = lax.top_k(masked, 1)[1][..., 0].astype(jnp.int32)
    kind = jax.random.randint(jax.random.fold_in(key, 5), (DOMAIN_PARTS, TILES), 0, 4)
    home = boxes[:, None]
    below = (home - 1) % DOMAIN_PARTS
    above = (home + 1) % DOMAIN_PARTS
    across = (home - DOMAIN_PARTS // 2) % DOMAIN_PARTS
    source = jnp.where(kind == 0, below, jnp.where(kind == 1, above, jnp.where(kind == 2, across, anywhere)))
    within = jax.random.randint(jax.random.fold_in(key, 4), (DOMAIN_PARTS, TILES), 0, CAP)
    return (source * CAP + within).astype(jnp.int32)


def plant(values, own_key, low, largest):
    longest = values.shape.index(max(values.shape))
    spots = []
    for shift in (0, 1):
        where = [jax.random.randint(jax.random.fold_in(own_key, axis), (), 0, length) for axis, length in enumerate(values.shape)]
        where[longest] = (where[longest] + shift) % values.shape[longest]
        spots.append(tuple(where))
    return values.at[spots[0]].set(low).at[spots[1]].set(largest)


def steps_of(rng, shape, split, low, largest):
    level, own = 1.0, jax.random.fold_in(rng, 6)
    for dim, blocks in split:
        steps = jnp.exp(jax.random.uniform(jax.random.fold_in(own, dim), (blocks,), jnp.float32, low / len(split), largest / len(split)))
        level = level * jnp.repeat(steps, shape[dim] // blocks).reshape([-1 if axis == dim else 1 for axis in range(len(shape))])
    return level


def normal_values(stream_key, shape, deviation, limit, shards=(), kind=jnp.bfloat16):
    drawn = deviation * jax.random.normal(stream_key, shape, jnp.float32)
    if shards:
        drawn = drawn * steps_of(stream_key, shape, shards, -0.22, 0.18)
    return jnp.clip(drawn, -limit, limit).astype(kind)


def setup_inputs(seed: int = 0) -> dict:
    key_list = jax.random.split(jax.random.key(seed), 16)
    return {
        "coords": normal_values(key_list[0], (DOMAIN_PARTS, 3, NP), 1.0, 6.0, ((0, 8),), jnp.float32),
        "disp": normal_values(key_list[1], (DOMAIN_PARTS, 3, NP), 0.5, 4.0, ((0, 8),), jnp.float32),
        "mass": jnp.clip(jnp.exp(math.log(4.0) - 2.0794415 * jax.random.uniform(key_list[2], (DOMAIN_PARTS, NP), jnp.float32) ** steps_of(key_list[2], (DOMAIN_PARTS, NP), ((0, 8),), -0.2, 0.2)), 0.5, 4.0),
        "stiffness": normal_values(key_list[3], (24, 24), 24 ** -0.5, 1.25, (), jnp.float32),
        "elem_nodes": plant(jax.random.randint(key_list[4], (DOMAIN_PARTS, 8, NE), 0, NP), jax.random.fold_in(key_list[4], 1), 0, NP - 1).astype(jnp.int32),
        "modulus": jnp.clip(jnp.exp(math.log(3.0) - 2.3025851 * jax.random.uniform(key_list[5], (DOMAIN_PARTS, NE), jnp.float32) ** steps_of(key_list[5], (DOMAIN_PARTS, NE), ((0, 8), (1, 4)), -0.2, 0.2)), 0.3, 3.0),
        "surf_nodes": plant(jax.random.randint(key_list[6], (DOMAIN_PARTS, SB, BLOCK), 0, NP), jax.random.fold_in(key_list[6], 1), 0, NP - 1).astype(jnp.int32),
        "block_region": draw_block_region(jax.random.fold_in(key_list[15], 71), 0),
        "face_pos": normal_values(key_list[8], (DOMAIN_PARTS, FB, 3, BLOCK), 1.0, 6.0, ((0, 8),), jnp.float32),
        "face_normal": normal_values(key_list[9], (DOMAIN_PARTS, FB, 3, BLOCK), 1.0, 6.0, ((0, 8),), jnp.float32),
        "tile_slot": draw_tile_slot(jax.random.fold_in(key_list[15], 71), 0),
        "tile_face": plant(jax.random.randint(key_list[11], (DOMAIN_PARTS, TILES), 0, FB), jax.random.fold_in(key_list[11], 1), 0, FB - 1).astype(jnp.int32),
        "tile_weight": normal_values(key_list[12], (DOMAIN_PARTS, TILES, BLOCK, BLOCK), BLOCK ** -0.5, 0.5, ((0, 8), (1, 4))),
        "shared_lo": plant(jax.random.randint(key_list[13], (DOMAIN_PARTS, SH), 0, NP), jax.random.fold_in(key_list[13], 1), 0, NP - 1).astype(jnp.int32),
        "shared_hi": plant(jax.random.randint(key_list[14], (DOMAIN_PARTS, SH), 0, NP), jax.random.fold_in(key_list[14], 1), 0, NP - 1).astype(jnp.int32),
    }


penalty = 4.0


def box_forces(args):
    received, slot, face, weights, fpos, fnorm = args
    xs = received[slot].astype(jnp.float32)
    pf = fpos[face]
    nf = fnorm[face]
    interp = jnp.einsum('tck,tik->tci', xs, weights.astype(jnp.float32))
    gap = jnp.sum(nf * (interp - pf), axis=1)
    pressure = penalty * jnp.maximum(-gap, 0.0)
    push = (pressure[:, None, :] * nf).astype(jnp.bfloat16)
    tile_force = jnp.einsum('tci,tik->tck', push.astype(jnp.float32), weights.astype(jnp.float32))
    start = jnp.zeros((DOMAIN_PARTS * CAP, 3, BLOCK), jnp.float32)
    return start.at[slot].add(tile_force)


def reference(coords, disp, mass, stiffness, elem_nodes, modulus, surf_nodes, block_region, face_pos, face_normal, tile_slot, tile_face, tile_weight, shared_lo, shared_hi):
    positions = coords + disp
    blocks = jax.vmap(lambda p, s: jnp.take(p, s, axis=1))(positions, surf_nodes)
    blocks = jnp.moveaxis(blocks, 1, 2).astype(jnp.bfloat16)
    order = jnp.arange(SB, dtype=jnp.int32)
    same = block_region[:, None, :] == block_region[:, :, None]
    rank = jnp.sum(same & (order[None, None, :] < order[None, :, None]), axis=2).astype(jnp.int32)
    source = jnp.arange(DOMAIN_PARTS, dtype=jnp.int32)[:, None]
    flat = (block_region * (DOMAIN_PARTS * CAP) + source * CAP + rank).reshape(-1)
    buffer = jnp.zeros((DOMAIN_PARTS * DOMAIN_PARTS * CAP, 3, BLOCK), jnp.bfloat16)
    buffer = buffer.at[flat].set(blocks.reshape(-1, 3, BLOCK)).reshape(DOMAIN_PARTS, DOMAIN_PARTS * CAP, 3, BLOCK)
    contact_force = lax.map(box_forces, (buffer, tile_slot, tile_face, tile_weight, face_pos, face_normal))
    back = contact_force[block_region, source * CAP + rank]

    def partition_force(args):
        moved, corner_points, scale, surf, block_force = args
        f_contact = jnp.zeros((3, NP), jnp.float32).at[:, surf].add(jnp.moveaxis(block_force, 0, 1))
        local = moved[:, corner_points].reshape(24, -1)
        elem_force = jnp.dot(stiffness, local, precision=lax.Precision.HIGHEST) * scale[None, :]
        f_int = jnp.zeros((3, NP), jnp.float32).at[:, corner_points].add(elem_force.reshape(3, 8, -1))
        return f_contact - f_int

    own = lax.map(partition_force, (disp, elem_nodes, modulus, surf_nodes, back))
    full = jnp.concatenate([own, mass[:, None, :]], axis=1)
    pack_lo = jax.vmap(lambda f, i: f[:, i])(full, shared_lo)
    pack_hi = jax.vmap(lambda f, i: f[:, i])(full, shared_hi)
    zero = jnp.zeros_like(pack_lo[:1])
    from_upper = jnp.concatenate([pack_lo[1:], zero], axis=0)
    from_lower = jnp.concatenate([zero, pack_hi[:-1]], axis=0)
    total = jax.vmap(lambda f, h, u, l, w: f.at[:, h].add(u).at[:, l].add(w))(full, shared_hi, from_upper, shared_lo, from_lower)
    return total[:, :3] / total[:, 3:]
```

```python
import functools

import jax
import jax.numpy as jnp
from jax import lax
from jax.experimental import pallas as pl
from jax.experimental.pallas import tpu as pltpu
from jax.sharding import PartitionSpec as P

penalty = 4.0
lanes = 128
wide = 256
rowwise = lax.GatherDimensionNumbers(
    offset_dims=(),
    collapsed_slice_dims=(1,),
    start_index_map=(1,),
    operand_batching_dims=(0,),
    start_indices_batching_dims=(0,),
)
vmem = pl.BlockSpec(memory_space=pltpu.VMEM)
smem = pl.BlockSpec(memory_space=pltpu.SMEM)


def call(body, out_shape, in_specs, out_specs, scratch, flops):
    return pl.pallas_call(
        body,
        out_shape=out_shape,
        in_specs=in_specs,
        out_specs=out_specs,
        scratch_shapes=scratch,
        compiler_params=pltpu.CompilerParams(vmem_limit_bytes=32 * 1024 * 1024),
        cost_estimate=pl.CostEstimate(flops=flops, bytes_accessed=1 << 20, transcendentals=0),
    )


def lookup(rows_of, table_rows, wanted, comps, unroll=8):
    low = [(nodes & (lanes - 1))[..., None] for nodes in wanted]
    high = [nodes >> 7 for nodes in wanted]

    def step(r, held):
        rows = [jnp.broadcast_to(row, wanted[0].shape) for row in rows_of(r)]
        new = []
        for v in range(len(wanted)):
            here = high[v] == r
            for c in range(comps):
                found = lax.gather(
                    rows[c], low[v], rowwise, (1, 1), mode=lax.GatherScatterMode.PROMISE_IN_BOUNDS
                )
                new.append(jnp.where(here, found, held[v * comps + c]))
        return tuple(new)

    start = tuple(jnp.zeros(wanted[0].shape, jnp.float32) for _ in range(len(wanted) * comps))
    flat = lax.fori_loop(0, table_rows, step, start, unroll=unroll)
    return [flat[v * comps : (v + 1) * comps] for v in range(len(wanted))]


def add_at_nodes(total_ref, nodes, values, tops):
    count = nodes.shape[0]
    comps = len(values)
    top_row = lax.broadcasted_iota(jnp.int32, (tops, lanes), 0)
    low_row = lax.broadcasted_iota(jnp.int32, (wide, lanes), 0)
    top = nodes >> 8
    low = nodes & (wide - 1)
    coarse = [v.astype(jnp.bfloat16).astype(jnp.float32) for v in values]
    fine = [v - w for v, w in zip(values, coarse)]
    left, right = [], []
    for i in range(count):
        match = top_row == top[i : i + 1]
        pieces = [
            jnp.where(match, v[i : i + 1], 0.0).astype(jnp.bfloat16) for v in coarse + fine
        ]
        left.append(jnp.concatenate(pieces, axis=0))
        right.append(jnp.where(low_row == low[i : i + 1], 1.0, 0.0).astype(jnp.bfloat16))
    both = lax.dot_general(
        jnp.concatenate(left, axis=1),
        jnp.concatenate(right, axis=1),
        (((1,), (1,)), ((), ())),
        preferred_element_type=jnp.float32,
    )
    summed = both[: comps * tops] + both[comps * tops :]
    for c in range(comps):
        for half in range(2):
            at = (c * 2 + half) * tops
            total_ref[at : at + tops] += summed[
                c * tops : (c + 1) * tops, half * lanes : (half + 1) * lanes
            ]


def pack_kernel(cap, region_ref, slot_ref, coords_ref, disp_ref, surf_ref, out_ref, stage):
    parts, rows, _ = out_ref.shape
    nblk = surf_ref.shape[1]
    tiles = slot_ref.shape[1]
    table_rows = coords_ref.shape[2] // lanes

    def rows_of(r):
        at = pl.ds(pl.multiple_of(r * lanes, lanes), lanes)
        here = coords_ref[0, :, at] + disp_ref[0, :, at]
        return [here[c : c + 1] for c in range(3)]

    lane = lax.broadcasted_iota(jnp.int32, (rows - 3 * cap, lanes), 1)
    line = lax.broadcasted_iota(jnp.int32, (rows - 3 * cap, lanes), 0)
    tail = jnp.zeros((rows - 3 * cap, lanes), jnp.float32)
    for t in range(tiles):
        tail = jnp.where((lane == t) & (line == 0), slot_ref[0, t].astype(jnp.float32), tail)
    for q in range(nblk // cap):
        stage[q, 3 * cap :] = tail
    empty = jnp.concatenate([jnp.zeros((3 * cap, lanes), jnp.float32), tail], axis=0)
    for j in range(parts):
        out_ref[j] = empty.astype(jnp.bfloat16)
    group = 4
    for g in range(nblk // (8 * group)):
        first = g * group * 8
        wanted = [surf_ref[0, first + 8 * v : first + 8 * v + 8] for v in range(group)]
        found = lookup(rows_of, table_rows, wanted, 3)
        for v in range(group):
            for part in range(0, 8, min(cap, 8)):
                b = first + 8 * v + part
                size = min(cap, 8)
                for c in range(3):
                    at = c * cap + b % cap
                    stage[b // cap, at : at + size] = found[v][c][part : part + size]
    for q in range(nblk // cap):
        out_ref[region_ref[0, q * cap]] = stage[q].astype(jnp.bfloat16)


def element_kernel(disp_ref, stiff_ref, modulus_ref, nodes_ref, out_ref, local):
    corners, count = nodes_ref.shape[1:]
    nodes_all = disp_ref.shape[2]

    def rows_of(r):
        here = disp_ref[0, :, pl.ds(pl.multiple_of(r * lanes, lanes), lanes)]
        return [here[c : c + 1] for c in range(3)]

    group = 4
    for g in range(count // (lanes * group)):
        cuts = [slice((g * group + v) * lanes, (g * group + v + 1) * lanes) for v in range(group)]
        found = lookup(rows_of, nodes_all // lanes, [nodes_ref[0, :, cut] for cut in cuts], 3)
        for v, cut in enumerate(cuts):
            for c in range(3):
                local[c * corners : (c + 1) * corners, cut] = found[v][c]
    force = jnp.dot(
        stiff_ref[...],
        local[...],
        precision=lax.Precision.HIGHEST,
        preferred_element_type=jnp.float32,
    )
    local[...] = -(force * modulus_ref[...])
    out_ref[...] = jnp.zeros_like(out_ref)

    def spread(g, _):
        cut = pl.ds(pl.multiple_of(g * lanes, lanes), lanes)
        values = [local[c * corners : (c + 1) * corners, cut] for c in range(3)]
        add_at_nodes(out_ref, nodes_ref[0, :, cut], values, nodes_all // wide)
        return 0

    lax.fori_loop(0, count // lanes, spread, 0)


def tile_kernel(cap, slot_ref, face_ref, got_ref, pos_ref, normal_ref, weight_ref, out_ref, slots_ref, flat):
    parts, rows, _ = got_ref.shape
    tiles = slot_ref.shape[1]
    for j in range(parts):
        flat[j * rows : (j + 1) * rows] = got_ref[j].astype(jnp.float32)
    slots_ref[...] = jnp.concatenate(
        [flat[j * rows + 3 * cap : j * rows + 3 * cap + 1] for j in range(parts)], axis=0
    ).astype(jnp.int32)
    forces = []
    for t in range(tiles):
        slot = slot_ref[0, t]
        at = (slot // cap) * rows + slot % cap
        x = jnp.concatenate([flat[pl.ds(at + c * cap, 1)] for c in range(3)], axis=0)
        weight = weight_ref[0, t]
        normal = normal_ref[0, face_ref[0, t]]
        interp = lax.dot_general(
            x.astype(jnp.bfloat16),
            weight,
            (((1,), (1,)), ((), ())),
            preferred_element_type=jnp.float32,
        )
        gap = jnp.sum(normal * (interp - pos_ref[0, face_ref[0, t]]), axis=0, keepdims=True)
        push = (penalty * jnp.maximum(-gap, 0.0) * normal).astype(jnp.bfloat16)
        forces.append(jnp.dot(push, weight, preferred_element_type=jnp.float32))
    all_forces = jnp.concatenate(forces, axis=0)
    for j in range(parts):
        out_ref[j] = all_forces


def contact_kernel(
    cap, tiles, slots_ref, region_ref, back_ref, surf_ref, part_ref, mass_ref, lo_ref, hi_ref,
    out_ref, share_lo_ref, share_hi_ref, run_of, node_rows, force_rows,
):
    parts = back_ref.shape[0]
    nblk = surf_ref.shape[1]
    nodes_all = mass_ref.shape[1]
    tops = nodes_all // wide
    me = lax.axis_index("dom")
    out_ref[...] = part_ref[...]
    node_rows[...] = jnp.full_like(node_rows, -1)

    def clear(j, _):
        run_of[j] = 0
        return 0

    lax.fori_loop(0, parts, clear, 0)
    for q in range(nblk // cap):
        run_of[region_ref[0, q * cap]] = q * cap

    def pick(j, filled):
        for t in range(tiles):
            slot = slots_ref[j, t]
            block = run_of[j] + slot % cap
            node_rows[pl.ds(filled, 1)] = surf_ref[0, pl.ds(block, 1)]
            for c in range(3):
                force_rows[c, pl.ds(filled, 1)] = back_ref[j, t * 3 + c : t * 3 + c + 1]
            filled = filled + jnp.where(slot // cap == me, 1, 0)
        return filled

    filled = lax.fori_loop(0, parts, pick, 0)
    node_rows[pl.ds(filled, 1)] = jnp.full((1, lanes), -1, jnp.int32)

    def spread(g, _):
        at = pl.ds(pl.multiple_of(g * 8, 8), 8)
        add_at_nodes(out_ref, node_rows[at], [force_rows[c, at] for c in range(3)], tops)
        return 0

    lax.fori_loop(0, (filled + 7) // 8, spread, 0)

    def rows_of(r):
        base = (r & 1) * tops + (r >> 1)
        rows = [out_ref[pl.ds(c * 2 * tops + base, 1)] for c in range(3)]
        return rows + [mass_ref[:, pl.ds(pl.multiple_of(r * lanes, lanes), lanes)]]

    shared = lo_ref.shape[1] // lanes
    wanted = jnp.concatenate(
        [ref[:, k * lanes : (k + 1) * lanes] for ref in (lo_ref, hi_ref) for k in range(shared)],
        axis=0,
    )
    found = lookup(rows_of, nodes_all // lanes, [wanted], 4)[0]
    for c in range(4):
        share_lo_ref[c * shared : (c + 1) * shared] = found[c][:shared]
        share_hi_ref[c * shared : (c + 1) * shared] = found[c][shared:]


def share_kernel(part_ref, mass_ref, up_ref, down_ref, lo_ref, hi_ref, out_ref, out_mass_ref, total):
    nodes_all = mass_ref.shape[1]
    tops = nodes_all // wide
    size = 3 * 2 * tops
    total[:size] = part_ref[...]
    for r in range(nodes_all // lanes):
        at = size + (r & 1) * tops + (r >> 1)
        total[at : at + 1] = mass_ref[:, r * lanes : (r + 1) * lanes]
    shared = lo_ref.shape[1] // lanes
    wanted = jnp.concatenate(
        [ref[:, k * lanes : (k + 1) * lanes] for ref in (hi_ref, lo_ref) for k in range(shared)],
        axis=0,
    )
    values = [
        jnp.concatenate(
            [ref[c * shared : (c + 1) * shared] for ref in (up_ref, down_ref)], axis=0
        )
        for c in range(4)
    ]
    add_at_nodes(total, wanted, values, tops)
    out_ref[...] = total[:size]
    out_mass_ref[...] = total[size:]


def accel_kernel(*refs):
    mass_ref, sums, out_ref, quotient = refs[0], refs[1:-2], refs[-2], refs[-1]
    nodes_all = out_ref.shape[2]
    tops = nodes_all // wide
    terms = [ref[...] for ref in sums]
    while len(terms) > 1:
        terms = [a + b for a, b in zip(terms[::2], terms[1::2])]
    mass = mass_ref[...]
    for c in range(3):
        at = slice(c * 2 * tops, (c + 1) * 2 * tops)
        quotient[at] = terms[0][at] / mass
    for r in range(nodes_all // lanes):
        at = (r & 1) * tops + (r >> 1)
        for c in range(3):
            row = c * 2 * tops + at
            out_ref[0, c : c + 1, r * lanes : (r + 1) * lanes] = quotient[row : row + 1]


def shifted(block, axis, distance):
    devices = range(lax.axis_size(axis))
    route = [(i - distance, i) for i in devices if i - distance in devices]
    return lax.ppermute(block, axis, route)


def on_device(
    coords,
    disp,
    mass,
    stiffness,
    elem_nodes,
    modulus,
    surf_nodes,
    block_region,
    face_pos,
    face_normal,
    tile_slot,
    tile_face,
    tile_weight,
    shared_lo,
    shared_hi,
):
    parts = lax.axis_size("dom")
    mates = lax.axis_size("rep")
    nodes_all = disp.shape[2]
    nblk = surf_nodes.shape[1]
    tiles = tile_slot.shape[1]
    cap = max(2, 2 * nblk // parts)
    rows = (3 * cap + 1 + 15) // 16 * 16
    tops = nodes_all // wide
    size = 3 * 2 * tops
    shared = shared_lo.shape[1] // lanes
    f32 = jnp.float32

    outgoing = call(
        functools.partial(pack_kernel, cap),
        jax.ShapeDtypeStruct((parts, rows, lanes), jnp.bfloat16),
        [smem, smem, vmem, vmem, vmem],
        vmem,
        [pltpu.VMEM((nblk // cap, rows, lanes), f32)],
        1 << 30,
    )(block_region, tile_slot, coords, disp, surf_nodes)
    arrived = lax.all_to_all(outgoing, "dom", split_axis=0, concat_axis=0, tiled=True)

    part = call(
        element_kernel,
        jax.ShapeDtypeStruct((size, lanes), f32),
        [vmem] * 4,
        vmem,
        [pltpu.VMEM((24, modulus.shape[1]), f32)],
        1 << 32,
    )(disp, stiffness, modulus, elem_nodes)

    forces, slots = call(
        functools.partial(tile_kernel, cap),
        (
            jax.ShapeDtypeStruct((parts, tiles * 3, lanes), f32),
            jax.ShapeDtypeStruct((parts, lanes), jnp.int32),
        ),
        [smem, smem, vmem, vmem, vmem, vmem],
        (vmem, vmem),
        [pltpu.VMEM((parts * rows, lanes), f32)],
        1 << 28,
    )(tile_slot, tile_face, arrived, face_pos, face_normal, tile_weight)
    back = lax.all_to_all(forces, "dom", split_axis=0, concat_axis=0, tiled=True)

    picked = (parts * tiles + 1 + 7) // 8 * 8
    share = jax.ShapeDtypeStruct((4 * shared, lanes), f32)
    part, share_lo, share_hi = call(
        functools.partial(contact_kernel, cap, tiles),
        (jax.ShapeDtypeStruct((size, lanes), f32), share, share),
        [smem, smem] + [vmem] * 6,
        (vmem, vmem, vmem),
        [
            pltpu.SMEM((parts,), jnp.int32),
            pltpu.VMEM((picked, lanes), jnp.int32),
            pltpu.VMEM((3, picked, lanes), f32),
        ],
        1 << 28,
    )(slots, block_region, back, surf_nodes, part, mass, shared_lo, shared_hi)
    from_upper = shifted(share_lo, "dom", -1)
    from_lower = shifted(share_hi, "dom", 1)

    own, own_mass = call(
        share_kernel,
        (jax.ShapeDtypeStruct((size, lanes), f32), jax.ShapeDtypeStruct((2 * tops, lanes), f32)),
        [vmem] * 6,
        (vmem, vmem),
        [pltpu.VMEM((4 * 2 * tops, lanes), f32)],
        1 << 28,
    )(part, mass, from_upper, from_lower, shared_lo, shared_hi)
    others = [
        lax.ppermute(own, "rep", [(i, i ^ k) for i in range(mates)]) for k in range(1, mates)
    ]
    return call(
        accel_kernel,
        jax.ShapeDtypeStruct((1, 3, nodes_all), f32),
        [vmem] * (2 + len(others)),
        vmem,
        [pltpu.VMEM((size, lanes), f32)],
        1 << 24,
    )(own_mass, own, *others)


def solution(mesh):
    in_specs = (
        P("dom", None, None),
        P("dom", None, None),
        P("dom", None),
        P(),
        P("dom", None, "rep"),
        P("dom", "rep"),
        P("dom", None, None),
        P("dom", None),
        P("dom", None, None, None),
        P("dom", None, None, None),
        P("dom", "rep"),
        P("dom", "rep"),
        P("dom", "rep", None, None),
        P("dom", None),
        P("dom", None),
    )
    out_specs = P("dom", None, None)
    return jax.shard_map(
        on_device, mesh=mesh, in_specs=in_specs, out_specs=out_specs, check_vma=False
    )
```

```python
import functools

import jax
import jax.numpy as jnp
from jax import lax
from jax.experimental import pallas as pl
from jax.experimental.pallas import tpu as pltpu
from jax.sharding import PartitionSpec as P

penalty = 4.0
lanes = 128
wide = 256
vmem = pl.BlockSpec(memory_space=pltpu.VMEM)
smem = pl.BlockSpec(memory_space=pltpu.SMEM)
f32 = jnp.float32
bf16 = jnp.bfloat16


def call(body, out_shape, in_specs, out_specs, scratch, flops):
    return pl.pallas_call(
        body,
        out_shape=out_shape,
        in_specs=in_specs,
        out_specs=out_specs,
        scratch_shapes=scratch,
        compiler_params=pltpu.CompilerParams(vmem_limit_bytes=32 * 1024 * 1024),
        cost_estimate=pl.CostEstimate(flops=flops, bytes_accessed=1 << 20, transcendentals=0),
    )


def one_hot(nodes):
    line = lax.broadcasted_iota(jnp.int32, (wide, lanes), 0)
    return jnp.concatenate(
        [jnp.where(line == (row & (wide - 1)), 1.0, 0.0).astype(bf16) for row in nodes], axis=1
    )


def halves(ref, c, tops):
    at = c * 2 * tops
    return jnp.concatenate(
        [ref[pl.ds(at, tops, stride=2)], ref[pl.ds(at + 1, tops, stride=2)]], axis=1
    )


def two_parts(x):
    coarse = x.astype(bf16)
    return [coarse, (x - coarse.astype(f32)).astype(bf16)]


def lookup(tables, nodes):
    tops = tables[0][0].shape[0]
    stacked = jnp.concatenate([part for table in tables for part in table], axis=0)
    found = jnp.dot(stacked, one_hot(nodes), preferred_element_type=f32)
    line = lax.broadcasted_iota(jnp.int32, (tops, lanes), 0)
    values = [[] for _ in tables]
    for i, row in enumerate(nodes):
        match = line == (row >> 8)
        at = 0
        for c, table in enumerate(tables):
            here = found[at : at + tops, i * lanes : (i + 1) * lanes]
            for p in range(1, len(table)):
                here += found[at + p * tops : at + (p + 1) * tops, i * lanes : (i + 1) * lanes]
            at += len(table) * tops
            values[c].append(jnp.sum(jnp.where(match, here, 0.0), axis=0, keepdims=True))
    return values


def node_sums(nodes, values, tops):
    line = lax.broadcasted_iota(jnp.int32, (tops, lanes), 0)
    comps = len(values)
    left = []
    for i, row in enumerate(nodes):
        match = line == (row >> 8)
        coarse = [v[i].astype(bf16).astype(f32) for v in values]
        fine = [v[i] - w for v, w in zip(values, coarse)]
        left.append(
            jnp.concatenate(
                [jnp.where(match, v, 0.0).astype(bf16) for v in coarse + fine], axis=0
            )
        )
    both = lax.dot_general(
        jnp.concatenate(left, axis=1),
        one_hot(nodes),
        (((1,), (1,)), ((), ())),
        preferred_element_type=f32,
    )
    return both[: comps * tops] + both[comps * tops :]


def add_halves(ref, sums, c, tops, row=None):
    at = (c if row is None else row) * 2 * tops
    for half in range(2):
        ref[pl.ds(at + half, tops, stride=2)] += sums[
            c * tops : (c + 1) * tops, half * lanes : (half + 1) * lanes
        ]


def pack_kernel(cap, slots_ref, region_ref, coords_ref, disp_ref, surf_ref, out_ref, list_ref, stage, run_of):
    parts, rows, _ = out_ref.shape
    nblk = surf_ref.shape[1]
    tiles = slots_ref.shape[2]
    tops = coords_ref.shape[0] // 6
    me = lax.axis_index("dom")
    for q in range(nblk // cap):
        run_of[region_ref[0, q * cap]] = q * cap

    def pick(j, filled):
        for t in range(tiles):
            slot = slots_ref[j, 0, t]
            mine = slot // cap == me
            list_ref[0, filled] = j * tiles + t
            list_ref[1, filled] = jnp.where(mine, run_of[j] + slot % cap, 0)
            filled = filled + jnp.where(mine, 1, 0)
        return filled

    filled = lax.fori_loop(0, parts, pick, 0)
    for i in range(8):
        list_ref[0, filled + i] = 0
        list_ref[1, filled + i] = 0
    list_ref[0, list_ref.shape[1] - 1] = filled
    stage[...] = jnp.zeros_like(stage)
    tables = [[(halves(coords_ref, c, tops) + halves(disp_ref, c, tops)).astype(bf16)] for c in range(3)]

    def gather(g, _):
        index = [list_ref[1, g * 8 + i] for i in range(8)]
        values = lookup(tables, [surf_ref[0, pl.ds(b, 1)] for b in index])
        for i in range(8):
            tile = list_ref[0, g * 8 + i]
            at = (tile // tiles) * rows + (tile % tiles) * 3
            at = jnp.where(g * 8 + i < filled, at, parts * rows)
            for c in range(3):
                stage[pl.ds(at + c, 1)] = values[c][i]
        return 0

    lax.fori_loop(0, (filled + 7) // 8, gather, 0)
    for j in range(parts):
        out_ref[j] = stage[j * rows : (j + 1) * rows].astype(bf16)


def element_kernel(disp_ref, stiff_ref, modulus_ref, nodes_ref, out_ref, local):
    corners, count = nodes_ref.shape[1:]
    tops = disp_ref.shape[0] // 6
    tables = [two_parts(halves(disp_ref, c, tops)) for c in range(3)]
    for g in range(count // lanes):
        cut = slice(g * lanes, (g + 1) * lanes)
        values = lookup(tables, [nodes_ref[0, a : a + 1, cut] for a in range(corners)])
        for c in range(3):
            local[c * corners : (c + 1) * corners, cut] = jnp.concatenate(values[c], axis=0)
    force = jnp.dot(
        stiff_ref[...], local[...], precision=lax.Precision.HIGHEST, preferred_element_type=f32
    )
    out_ref[...] = -(force * modulus_ref[...])


def element_sum_kernel(force_ref, nodes_ref, out_ref, sums):
    corners, count = nodes_ref.shape[1:]
    tops = out_ref.shape[0] // 6
    for g in range(count // lanes):
        cut = slice(g * lanes, (g + 1) * lanes)
        nodes = [nodes_ref[0, a : a + 1, cut] for a in range(corners)]
        values = [
            [force_ref[c * corners + a : c * corners + a + 1, cut] for a in range(corners)]
            for c in range(3)
        ]
        here = node_sums(nodes, values, tops)
        sums[...] = here if g == 0 else sums[...] + here
    out_ref[...] = jnp.zeros_like(out_ref)
    for c in range(3):
        add_halves(out_ref, sums[...], c, tops)


def tile_kernel(cap, slot_ref, face_ref, got_ref, pos_ref, normal_ref, weight_ref, out_ref):
    parts = got_ref.shape[0]
    tiles = slot_ref.shape[1]
    forces = []
    for t in range(tiles):
        x = got_ref[slot_ref[0, t] // cap].astype(f32)[t * 3 : t * 3 + 3].astype(bf16)
        weight = weight_ref[0, t]
        face = face_ref[0, t]
        interp = lax.dot_general(
            x, weight, (((1,), (1,)), ((), ())), preferred_element_type=f32
        )
        normal = jnp.concatenate([normal_ref[0, c, pl.ds(face, 1)] for c in range(3)], axis=0)
        pos = jnp.concatenate([pos_ref[0, c, pl.ds(face, 1)] for c in range(3)], axis=0)
        gap = jnp.sum(normal * (interp - pos), axis=0, keepdims=True)
        push = (penalty * jnp.maximum(-gap, 0.0) * normal).astype(bf16)
        forces.append(jnp.dot(push, weight, preferred_element_type=f32))
    all_forces = jnp.concatenate(forces, axis=0)
    for j in range(parts):
        out_ref[j] = all_forces


def contact_kernel(
    list_ref, back_ref, surf_ref, part_ref, mass_ref, lo_ref, hi_ref, out_ref, share_lo_ref, share_hi_ref
):
    tops = mass_ref.shape[0] // 2
    out_ref[...] = part_ref[...]
    filled = list_ref[0, list_ref.shape[1] - 1]

    def spread(g, _):
        nodes, values = [], [[], [], []]
        for i in range(8):
            row = surf_ref[0, pl.ds(list_ref[1, g * 8 + i], 1)]
            nodes.append(jnp.where(g * 8 + i < filled, row, -1))
            for c in range(3):
                values[c].append(back_ref[pl.ds(list_ref[0, g * 8 + i] * 3 + c, 1)])
        sums = node_sums(nodes, values, tops)
        for c in range(3):
            add_halves(out_ref, sums, c, tops)
        return 0

    lax.fori_loop(0, (filled + 7) // 8, spread, 0)
    shared = lo_ref.shape[0]
    tables = [two_parts(halves(out_ref, c, tops)) for c in range(3)]
    tables.append(two_parts(halves(mass_ref, 0, tops)))
    values = lookup(tables, [ref[k : k + 1] for ref in (lo_ref, hi_ref) for k in range(shared)])
    for c in range(4):
        share_lo_ref[c * shared : (c + 1) * shared] = jnp.concatenate(values[c][:shared], axis=0)
        share_hi_ref[c * shared : (c + 1) * shared] = jnp.concatenate(values[c][shared:], axis=0)


def share_kernel(part_ref, mass_ref, up_ref, down_ref, lo_ref, hi_ref, out_ref, out_mass_ref):
    tops = mass_ref.shape[0] // 2
    out_ref[...] = part_ref[...]
    out_mass_ref[...] = mass_ref[...]
    shared = lo_ref.shape[0]
    nodes = [ref[k : k + 1] for ref in (hi_ref, lo_ref) for k in range(shared)]
    values = [
        [ref[c * shared + k : c * shared + k + 1] for ref in (up_ref, down_ref) for k in range(shared)]
        for c in range(4)
    ]
    sums = node_sums(nodes, values, tops)
    for c in range(3):
        add_halves(out_ref, sums, c, tops)
    add_halves(out_mass_ref, sums, 3, tops, 0)


def accel_kernel(mass_ref, *refs):
    sums, out_ref = refs[:-1], refs[-1]
    terms = [ref[...] for ref in sums]
    while len(terms) > 1:
        terms = [a + b for a, b in zip(terms[::2], terms[1::2])]
    size = mass_ref.shape[0]
    for c in range(3):
        at = slice(c * size, (c + 1) * size)
        out_ref[at] = terms[0][at] / mass_ref[...]


def shifted(block, axis, distance):
    devices = range(lax.axis_size(axis))
    route = [(i - distance, i) for i in devices if i - distance in devices]
    return lax.ppermute(block, axis, route)


def on_device(
    coords,
    disp,
    mass,
    stiffness,
    elem_nodes,
    modulus,
    surf_nodes,
    block_region,
    face_pos,
    face_normal,
    tile_slot,
    tile_face,
    tile_weight,
    shared_lo,
    shared_hi,
):
    parts = lax.axis_size("dom")
    mates = lax.axis_size("rep")
    nodes_all = disp.shape[2]
    nblk = surf_nodes.shape[1]
    tiles = tile_slot.shape[1]
    cap = max(2, 2 * nblk // parts)
    rows = (3 * tiles + 15) // 16 * 16
    picked = parts * tiles + 16
    node_array = jax.ShapeDtypeStruct((3 * nodes_all // lanes, lanes), f32)
    mass_array = jax.ShapeDtypeStruct((nodes_all // lanes, lanes), f32)
    coords = coords.reshape(node_array.shape)
    disp = disp.reshape(node_array.shape)
    mass = mass.reshape(mass_array.shape)
    shared_lo = shared_lo.reshape(-1, lanes)
    shared_hi = shared_hi.reshape(-1, lanes)
    share = jax.ShapeDtypeStruct((4 * shared_lo.shape[0], lanes), f32)

    asked = jnp.broadcast_to(tile_slot[None], (parts, 1, tiles))
    slots = lax.all_to_all(asked, "dom", split_axis=0, concat_axis=0, tiled=True)

    force = call(
        element_kernel,
        jax.ShapeDtypeStruct((24, modulus.shape[1]), f32),
        [vmem] * 4,
        vmem,
        [pltpu.VMEM((24, modulus.shape[1]), f32)],
        1 << 31,
    )(disp, stiffness, modulus, elem_nodes)

    outgoing, picks = call(
        functools.partial(pack_kernel, cap),
        (
            jax.ShapeDtypeStruct((parts, rows, lanes), bf16),
            jax.ShapeDtypeStruct((2, picked), jnp.int32),
        ),
        [smem, smem, vmem, vmem, vmem],
        (vmem, smem),
        [pltpu.VMEM((parts * rows + 8, lanes), f32), pltpu.SMEM((parts,), jnp.int32)],
        1 << 28,
    )(slots, block_region, coords, disp, surf_nodes)
    arrived = lax.all_to_all(outgoing, "dom", split_axis=0, concat_axis=0, tiled=True)

    part = call(
        element_sum_kernel,
        node_array,
        [vmem] * 2,
        vmem,
        [pltpu.VMEM((3 * nodes_all // wide, wide), f32)],
        1 << 30,
    )(force, elem_nodes)

    forces = call(
        functools.partial(tile_kernel, cap),
        jax.ShapeDtypeStruct((parts, tiles * 3, lanes), f32),
        [smem, smem, vmem, vmem, vmem, vmem],
        vmem,
        [],
        1 << 28,
    )(
        tile_slot,
        tile_face,
        arrived,
        jnp.swapaxes(face_pos, 1, 2),
        jnp.swapaxes(face_normal, 1, 2),
        tile_weight,
    )
    back = lax.all_to_all(forces, "dom", split_axis=0, concat_axis=0, tiled=True)

    part, share_lo, share_hi = call(
        contact_kernel,
        (node_array, share, share),
        [smem] + [vmem] * 6,
        (vmem, vmem, vmem),
        [],
        1 << 28,
    )(picks, back.reshape(-1, lanes), surf_nodes, part, mass, shared_lo, shared_hi)
    from_upper = shifted(share_lo, "dom", -1)
    from_lower = shifted(share_hi, "dom", 1)

    own, own_mass = call(
        share_kernel, (node_array, mass_array), [vmem] * 6, (vmem, vmem), [], 1 << 28
    )(part, mass, from_upper, from_lower, shared_lo, shared_hi)
    others = [
        lax.ppermute(own, "rep", [(i, i ^ k) for i in range(mates)]) for k in range(1, mates)
    ]
    accel = call(accel_kernel, node_array, [vmem] * (2 + len(others)), vmem, [], 1 << 24)(
        own_mass, own, *others
    )
    return accel.reshape(1, 3, nodes_all)


def solution(mesh):
    in_specs = (
        P("dom", None, None),
        P("dom", None, None),
        P("dom", None),
        P(),
        P("dom", None, "rep"),
        P("dom", "rep"),
        P("dom", None, None),
        P("dom", None),
        P("dom", None, None, None),
        P("dom", None, None, None),
        P("dom", "rep"),
        P("dom", "rep"),
        P("dom", "rep", None, None),
        P("dom", None),
        P("dom", None),
    )
    out_specs = P("dom", None, None)
    return jax.shard_map(
        on_device, mesh=mesh, in_specs=in_specs, out_specs=out_specs, check_vma=False
    )
```

```python
import functools

import jax
import jax.numpy as jnp
from jax import lax
from jax.experimental import pallas as pl
from jax.experimental.pallas import tpu as pltpu
from jax.sharding import PartitionSpec as P

penalty = 4.0
lanes = 128
wide = 256
vmem = pl.BlockSpec(memory_space=pltpu.VMEM)
smem = pl.BlockSpec(memory_space=pltpu.SMEM)
f32 = jnp.float32
bf16 = jnp.bfloat16


def call(body, out_shape, in_specs, out_specs, scratch, flops):
    return pl.pallas_call(
        body,
        out_shape=out_shape,
        in_specs=in_specs,
        out_specs=out_specs,
        scratch_shapes=scratch,
        compiler_params=pltpu.CompilerParams(vmem_limit_bytes=32 * 1024 * 1024),
        cost_estimate=pl.CostEstimate(flops=flops, bytes_accessed=1 << 20, transcendentals=0),
    )


def one_hot(nodes):
    line = lax.broadcasted_iota(jnp.int32, (wide, lanes), 0)
    return jnp.concatenate(
        [jnp.where(line == (row & (wide - 1)), 1.0, 0.0).astype(bf16) for row in nodes], axis=1
    )


def halves(ref, c, tops):
    at = c * 2 * tops
    return jnp.concatenate(
        [ref[pl.ds(at, tops, stride=2)], ref[pl.ds(at + 1, tops, stride=2)]], axis=1
    )


def two_parts(x):
    coarse = x.astype(bf16)
    return [coarse, (x - coarse.astype(f32)).astype(bf16)]


def lookup(tables, nodes):
    tops = tables[0][0].shape[0]
    stacked = jnp.concatenate([part for table in tables for part in table], axis=0)
    found = jnp.dot(stacked, one_hot(nodes), preferred_element_type=f32)
    line = lax.broadcasted_iota(jnp.int32, (tops, lanes), 0)
    values = [[] for _ in tables]
    for i, row in enumerate(nodes):
        match = line == (row >> 8)
        at = 0
        for c, table in enumerate(tables):
            here = found[at : at + tops, i * lanes : (i + 1) * lanes]
            for p in range(1, len(table)):
                here += found[at + p * tops : at + (p + 1) * tops, i * lanes : (i + 1) * lanes]
            at += len(table) * tops
            values[c].append(jnp.sum(jnp.where(match, here, 0.0), axis=0, keepdims=True))
    return values


def node_sums(nodes, values, tops):
    line = lax.broadcasted_iota(jnp.int32, (tops, lanes), 0)
    comps = len(values)
    left = []
    for i, row in enumerate(nodes):
        match = line == (row >> 8)
        coarse = [v[i].astype(bf16).astype(f32) for v in values]
        fine = [v[i] - w for v, w in zip(values, coarse)]
        left.append(
            jnp.concatenate(
                [jnp.where(match, v, 0.0).astype(bf16) for v in coarse + fine], axis=0
            )
        )
    both = lax.dot_general(
        jnp.concatenate(left, axis=1),
        one_hot(nodes),
        (((1,), (1,)), ((), ())),
        preferred_element_type=f32,
    )
    return both[: comps * tops] + both[comps * tops :]


def add_halves(ref, sums, c, tops, row=None):
    at = (c if row is None else row) * 2 * tops
    for half in range(2):
        ref[pl.ds(at + half, tops, stride=2)] += sums[
            c * tops : (c + 1) * tops, half * lanes : (half + 1) * lanes
        ]


def pack_kernel(cap, region_ref, slot_ref, coords_ref, disp_ref, surf_ref, out_ref, stage):
    parts, rows, _ = out_ref.shape
    nblk = surf_ref.shape[1]
    tiles = slot_ref.shape[1]
    tops = coords_ref.shape[0] // 6
    rest = (rows - 3 * cap, lanes)
    lane = lax.broadcasted_iota(jnp.int32, rest, 1)
    line = lax.broadcasted_iota(jnp.int32, rest, 0)
    tail = jnp.zeros(rest, f32)
    for t in range(tiles):
        tail = jnp.where((lane == t) & (line == 0), slot_ref[0, t].astype(f32), tail)
    for q in range(nblk // cap):
        stage[q, 3 * cap :] = tail
    empty = jnp.concatenate([jnp.zeros((3 * cap, lanes), f32), tail], axis=0).astype(bf16)
    for j in range(parts):
        out_ref[j] = empty
    tables = [
        [(halves(coords_ref, c, tops) + halves(disp_ref, c, tops)).astype(bf16)] for c in range(3)
    ]
    size = min(cap, 8)
    for first in range(0, nblk, 8):
        values = lookup(tables, [surf_ref[0, first + i : first + i + 1] for i in range(8)])
        for b in range(first, first + 8, size):
            for c in range(3):
                at = c * cap + b % cap
                stage[b // cap, at : at + size] = jnp.concatenate(
                    values[c][b - first : b - first + size], axis=0
                )
    for q in range(nblk // cap):
        out_ref[region_ref[0, q * cap]] = stage[q].astype(bf16)


def element_kernel(disp_ref, stiff_ref, modulus_ref, nodes_ref, out_ref, local, sums):
    corners, count = nodes_ref.shape[1:]
    tops = disp_ref.shape[0] // 6
    tables = [two_parts(halves(disp_ref, c, tops)) for c in range(3)]
    cuts = [slice(g * lanes, (g + 1) * lanes) for g in range(count // lanes)]
    nodes = [[nodes_ref[0, a : a + 1, cut] for a in range(corners)] for cut in cuts]
    for cut, here in zip(cuts, nodes):
        values = lookup(tables, here)
        for c in range(3):
            local[c * corners : (c + 1) * corners, cut] = jnp.concatenate(values[c], axis=0)
    force = jnp.dot(
        stiff_ref[...], local[...], precision=lax.Precision.HIGHEST, preferred_element_type=f32
    )
    local[...] = -(force * modulus_ref[...])
    for g, (cut, here) in enumerate(zip(cuts, nodes)):
        values = [
            [local[c * corners + a : c * corners + a + 1, cut] for a in range(corners)]
            for c in range(3)
        ]
        added = node_sums(here, values, tops)
        sums[...] = added if g == 0 else sums[...] + added
    out_ref[...] = jnp.zeros_like(out_ref)
    for c in range(3):
        add_halves(out_ref, sums[...], c, tops)


def tile_kernel(
    cap, slot_ref, face_ref, got_ref, pos_ref, normal_ref, weight_ref, after_ref, out_ref, slots_ref, flat
):
    parts, rows, _ = got_ref.shape
    tiles = slot_ref.shape[1]
    for j in range(parts):
        flat[j * rows : (j + 1) * rows] = got_ref[j].astype(f32)
    slots_ref[...] = jnp.concatenate(
        [flat[j * rows + 3 * cap : j * rows + 3 * cap + 1] for j in range(parts)], axis=0
    ).astype(jnp.int32)
    starts = [(slot_ref[0, t] // cap) * rows + slot_ref[0, t] % cap for t in range(tiles)]
    x = jnp.concatenate(
        [flat[pl.ds(at + c * cap, 1)] for c in range(3) for at in starts], axis=0
    )
    weights = weight_ref[0].reshape(tiles * lanes, lanes)
    crossed = lax.dot_general(
        x.astype(bf16), weights, (((1,), (1,)), ((), ())), preferred_element_type=f32
    )
    line = lax.broadcasted_iota(jnp.int32, (tiles, lanes), 0)
    gap = jnp.zeros((tiles, lanes), f32)
    normals = []
    for c in range(3):
        interp = jnp.zeros((tiles, lanes), f32)
        for t in range(tiles):
            here = crossed[c * tiles : (c + 1) * tiles, t * lanes : (t + 1) * lanes]
            interp = jnp.where(line == t, here, interp)
        faces = [face_ref[0, t] for t in range(tiles)]
        normal = jnp.concatenate([normal_ref[0, c, pl.ds(f, 1)] for f in faces], axis=0)
        pos = jnp.concatenate([pos_ref[0, c, pl.ds(f, 1)] for f in faces], axis=0)
        gap += normal * (interp - pos)
        normals.append(normal)
    pressure = penalty * jnp.maximum(-gap, 0.0)
    push = [pressure * normal for normal in normals]
    spread = jnp.concatenate(
        [
            jnp.concatenate([jnp.where(line == t, p, 0.0) for p in push], axis=0).astype(bf16)
            for t in range(tiles)
        ],
        axis=1,
    )
    forces = jnp.dot(spread, weights, preferred_element_type=f32)
    for j in range(parts):
        out_ref[j] = forces


def list_kernel(cap, tiles, slots_ref, region_ref, list_ref, run_of):
    parts = slots_ref.shape[0]
    nblk = region_ref.shape[1]
    me = lax.axis_index("dom")
    for q in range(nblk // cap):
        run_of[region_ref[0, q * cap]] = q * cap

    def pick(j, filled):
        for t in range(tiles):
            slot = slots_ref[j, t]
            mine = slot // cap == me
            list_ref[0, filled] = j * 3 * tiles + t
            list_ref[1, filled] = jnp.where(mine, run_of[j] + slot % cap, 0)
            filled = filled + jnp.where(mine, 1, 0)
        return filled

    filled = lax.fori_loop(0, parts, pick, 0)
    for i in range(8):
        list_ref[0, filled + i] = 0
        list_ref[1, filled + i] = 0
    list_ref[0, list_ref.shape[1] - 1] = filled


def contact_kernel(
    tiles, list_ref, back_ref, surf_ref, part_ref, mass_ref, lo_ref, hi_ref, out_ref, share_lo_ref, share_hi_ref
):
    tops = mass_ref.shape[0] // 2
    out_ref[...] = part_ref[...]
    filled = list_ref[0, list_ref.shape[1] - 1]

    def spread(g, _):
        nodes, values = [], [[], [], []]
        for i in range(8):
            row = surf_ref[0, pl.ds(list_ref[1, g * 8 + i], 1)]
            nodes.append(jnp.where(g * 8 + i < filled, row, -1))
            for c in range(3):
                values[c].append(back_ref[pl.ds(list_ref[0, g * 8 + i] + c * tiles, 1)])
        sums = node_sums(nodes, values, tops)
        for c in range(3):
            add_halves(out_ref, sums, c, tops)
        return 0

    lax.fori_loop(0, (filled + 7) // 8, spread, 0)
    shared = lo_ref.shape[0]
    tables = [two_parts(halves(out_ref, c, tops)) for c in range(3)]
    tables.append(two_parts(halves(mass_ref, 0, tops)))
    values = lookup(tables, [ref[k : k + 1] for ref in (lo_ref, hi_ref) for k in range(shared)])
    for c in range(4):
        share_lo_ref[c * shared : (c + 1) * shared] = jnp.concatenate(values[c][:shared], axis=0)
        share_hi_ref[c * shared : (c + 1) * shared] = jnp.concatenate(values[c][shared:], axis=0)


def share_kernel(part_ref, mass_ref, up_ref, down_ref, lo_ref, hi_ref, out_ref, out_mass_ref):
    tops = mass_ref.shape[0] // 2
    out_ref[...] = part_ref[...]
    out_mass_ref[...] = mass_ref[...]
    shared = lo_ref.shape[0]
    nodes = [ref[k : k + 1] for ref in (hi_ref, lo_ref) for k in range(shared)]
    values = [
        [ref[c * shared + k : c * shared + k + 1] for ref in (up_ref, down_ref) for k in range(shared)]
        for c in range(4)
    ]
    sums = node_sums(nodes, values, tops)
    for c in range(3):
        add_halves(out_ref, sums, c, tops)
    add_halves(out_mass_ref, sums, 3, tops, 0)


def accel_kernel(mass_ref, *refs):
    sums, out_ref = refs[:-1], refs[-1]
    terms = [ref[...] for ref in sums]
    while len(terms) > 1:
        terms = [a + b for a, b in zip(terms[::2], terms[1::2])]
    size = mass_ref.shape[0]
    for c in range(3):
        at = slice(c * size, (c + 1) * size)
        out_ref[at] = terms[0][at] / mass_ref[...]


def shifted(block, axis, distance):
    devices = range(lax.axis_size(axis))
    route = [(i - distance, i) for i in devices if i - distance in devices]
    return lax.ppermute(block, axis, route)


def on_device(
    coords,
    disp,
    mass,
    stiffness,
    elem_nodes,
    modulus,
    surf_nodes,
    block_region,
    face_pos,
    face_normal,
    tile_slot,
    tile_face,
    tile_weight,
    shared_lo,
    shared_hi,
):
    parts = lax.axis_size("dom")
    mates = lax.axis_size("rep")
    nodes_all = disp.shape[2]
    nblk = surf_nodes.shape[1]
    tiles = tile_slot.shape[1]
    cap = max(2, 2 * nblk // parts)
    rows = (3 * cap + 1 + 15) // 16 * 16
    node_array = jax.ShapeDtypeStruct((3 * nodes_all // lanes, lanes), f32)
    mass_array = jax.ShapeDtypeStruct((nodes_all // lanes, lanes), f32)
    coords = coords.reshape(node_array.shape)
    disp = disp.reshape(node_array.shape)
    mass = mass.reshape(mass_array.shape)
    shared_lo = shared_lo.reshape(-1, lanes)
    shared_hi = shared_hi.reshape(-1, lanes)
    share = jax.ShapeDtypeStruct((4 * shared_lo.shape[0], lanes), f32)

    outgoing = call(
        functools.partial(pack_kernel, cap),
        jax.ShapeDtypeStruct((parts, rows, lanes), bf16),
        [smem, smem, vmem, vmem, vmem],
        vmem,
        [pltpu.VMEM((nblk // cap, rows, lanes), f32)],
        1 << 30,
    )(block_region, tile_slot, coords, disp, surf_nodes)
    arrived = lax.all_to_all(outgoing, "dom", split_axis=0, concat_axis=0, tiled=True)

    part = call(
        element_kernel,
        node_array,
        [vmem] * 4,
        vmem,
        [
            pltpu.VMEM((24, modulus.shape[1]), f32),
            pltpu.VMEM((3 * nodes_all // wide, wide), f32),
        ],
        1 << 32,
    )(disp, stiffness, modulus, elem_nodes)

    forces, slots = call(
        functools.partial(tile_kernel, cap),
        (
            jax.ShapeDtypeStruct((parts, 3 * tiles, lanes), f32),
            jax.ShapeDtypeStruct((parts, lanes), jnp.int32),
        ),
        [smem, smem] + [vmem] * 4 + [pl.BlockSpec(memory_space=pl.ANY)],
        (vmem, vmem),
        [pltpu.VMEM((parts * rows, lanes), f32)],
        1 << 28,
    )(
        tile_slot,
        tile_face,
        arrived,
        jnp.swapaxes(face_pos, 1, 2),
        jnp.swapaxes(face_normal, 1, 2),
        tile_weight,
        part,
    )
    back = lax.all_to_all(forces, "dom", split_axis=0, concat_axis=0, tiled=True)
    picks = call(
        functools.partial(list_kernel, cap, tiles),
        jax.ShapeDtypeStruct((2, parts * tiles + 16), jnp.int32),
        [smem, smem],
        smem,
        [pltpu.SMEM((parts,), jnp.int32)],
        1 << 24,
    )(slots, block_region)

    part, share_lo, share_hi = call(
        functools.partial(contact_kernel, tiles),
        (node_array, share, share),
        [smem] + [vmem] * 6,
        (vmem, vmem, vmem),
        [],
        1 << 28,
    )(picks, back.reshape(-1, lanes), surf_nodes, part, mass, shared_lo, shared_hi)
    from_upper = shifted(share_lo, "dom", -1)
    from_lower = shifted(share_hi, "dom", 1)

    own, own_mass = call(
        share_kernel, (node_array, mass_array), [vmem] * 6, (vmem, vmem), [], 1 << 28
    )(part, mass, from_upper, from_lower, shared_lo, shared_hi)
    others = [
        lax.ppermute(own, "rep", [(i, i ^ k) for i in range(mates)]) for k in range(1, mates)
    ]
    accel = call(accel_kernel, node_array, [vmem] * (2 + len(others)), vmem, [], 1 << 24)(
        own_mass, own, *others
    )
    return accel.reshape(1, 3, nodes_all)


def solution(mesh):
    in_specs = (
        P("dom", None, None),
        P("dom", None, None),
        P("dom", None),
        P(),
        P("dom", None, "rep"),
        P("dom", "rep"),
        P("dom", None, None),
        P("dom", None),
        P("dom", None, None, None),
        P("dom", None, None, None),
        P("dom", "rep"),
        P("dom", "rep"),
        P("dom", "rep", None, None),
        P("dom", None),
        P("dom", None),
    )
    out_specs = P("dom", None, None)
    return jax.shard_map(
        on_device, mesh=mesh, in_specs=in_specs, out_specs=out_specs, check_vma=False
    )
```

```python
import functools

import jax
import jax.numpy as jnp
from jax import lax
from jax.experimental import pallas as pl
from jax.experimental.pallas import tpu as pltpu
from jax.sharding import PartitionSpec as P

penalty = 4.0
lanes = 128
wide = 256
vmem = pl.BlockSpec(memory_space=pltpu.VMEM)
smem = pl.BlockSpec(memory_space=pltpu.SMEM)
hbm = pl.BlockSpec(memory_space=pltpu.HBM)
f32 = jnp.float32
bf16 = jnp.bfloat16


def call(body, out_shape, in_specs, out_specs, scratch, flops, vmem_mib=32):
    return pl.pallas_call(
        body,
        out_shape=out_shape,
        in_specs=in_specs,
        out_specs=out_specs,
        scratch_shapes=scratch,
        compiler_params=pltpu.CompilerParams(vmem_limit_bytes=vmem_mib * 1024 * 1024),
        cost_estimate=pl.CostEstimate(flops=flops, bytes_accessed=1 << 20, transcendentals=0),
    )


def one_hot(nodes):
    line = lax.broadcasted_iota(jnp.int32, (wide, lanes), 0)
    return jnp.concatenate(
        [jnp.where(line == (row & (wide - 1)), 1.0, 0.0).astype(bf16) for row in nodes], axis=1
    )


def halves(ref, c, tops):
    at = c * 2 * tops
    return jnp.concatenate(
        [ref[pl.ds(at, tops, stride=2)], ref[pl.ds(at + 1, tops, stride=2)]], axis=1
    )


def two_parts(x):
    coarse = x.astype(bf16)
    return [coarse, (x - coarse.astype(f32)).astype(bf16)]


def lookup(tables, nodes):
    tops = tables[0][0].shape[0]
    stacked = jnp.concatenate([part for table in tables for part in table], axis=0)
    found = jnp.dot(stacked, one_hot(nodes), preferred_element_type=f32)
    line = lax.broadcasted_iota(jnp.int32, (tops, lanes), 0)
    values = [[] for _ in tables]
    for i, row in enumerate(nodes):
        match = line == (row >> 8)
        at = 0
        for c, table in enumerate(tables):
            here = found[at : at + tops, i * lanes : (i + 1) * lanes]
            for p in range(1, len(table)):
                here += found[at + p * tops : at + (p + 1) * tops, i * lanes : (i + 1) * lanes]
            at += len(table) * tops
            values[c].append(jnp.sum(jnp.where(match, here, 0.0), axis=0, keepdims=True))
    return values


def node_sums(nodes, values, tops):
    line = lax.broadcasted_iota(jnp.int32, (tops, lanes), 0)
    comps = len(values)
    left = []
    for i, row in enumerate(nodes):
        match = line == (row >> 8)
        coarse = [v[i].astype(bf16).astype(f32) for v in values]
        fine = [v[i] - w for v, w in zip(values, coarse)]
        left.append(
            jnp.concatenate(
                [jnp.where(match, v, 0.0).astype(bf16) for v in coarse + fine], axis=0
            )
        )
    both = lax.dot_general(
        jnp.concatenate(left, axis=1),
        one_hot(nodes),
        (((1,), (1,)), ((), ())),
        preferred_element_type=f32,
    )
    return both[: comps * tops] + both[comps * tops :]


def add_halves(ref, sums, c, tops, row=None):
    at = (c if row is None else row) * 2 * tops
    for half in range(2):
        ref[pl.ds(at + half, tops, stride=2)] += sums[
            c * tops : (c + 1) * tops, half * lanes : (half + 1) * lanes
        ]


def pack_kernel(
    cap, region_hbm, slot_hbm, coords_hbm, disp_hbm, surf_hbm, out_ref,
    stage, region_ref, slot_ref, coords_ref, disp_ref, surf_ref, sems,
):
    sources = (coords_hbm, disp_hbm, slot_hbm, surf_hbm, region_hbm)
    places = (coords_ref, disp_ref, slot_ref, surf_ref, region_ref)
    copies = [
        pltpu.make_async_copy(a, b, sems.at[i]) for i, (a, b) in enumerate(zip(sources, places))
    ]
    for copy in copies:
        copy.start()
    parts, rows, _ = out_ref.shape
    nblk = surf_ref.shape[1]
    tiles = slot_ref.shape[1]
    tops = coords_ref.shape[0] // 6
    for copy in copies:
        copy.wait()
    rest = (rows - 3 * cap, lanes)
    lane = lax.broadcasted_iota(jnp.int32, rest, 1)
    line = lax.broadcasted_iota(jnp.int32, rest, 0)
    tail = jnp.zeros(rest, f32)
    for t in range(tiles):
        tail = jnp.where((lane == t) & (line == 0), slot_ref[0, t].astype(f32), tail)
    for q in range(nblk // cap):
        stage[q, 3 * cap :] = tail
    empty = jnp.concatenate([jnp.zeros((3 * cap, lanes), f32), tail], axis=0).astype(bf16)
    for j in range(parts):
        out_ref[j] = empty
    tables = [
        [(halves(coords_ref, c, tops) + halves(disp_ref, c, tops)).astype(bf16)] for c in range(3)
    ]
    size = min(cap, 8)
    for first in range(0, nblk, 8):
        values = lookup(tables, [surf_ref[0, first + i : first + i + 1] for i in range(8)])
        for b in range(first, first + 8, size):
            for c in range(3):
                at = c * cap + b % cap
                stage[b // cap, at : at + size] = jnp.concatenate(
                    values[c][b - first : b - first + size], axis=0
                )
    for q in range(nblk // cap):
        out_ref[region_ref[0, q * cap]] = stage[q].astype(bf16)


def element_kernel(
    cap, rows, slot_ref, face_ref, pos_ref, normal_ref, disp_ref, stiff_ref, modulus_ref, nodes_ref,
    out_ref, faces_ref, starts_ref, local, sums,
):
    tiles = slot_ref.shape[1]
    for t in range(tiles):
        starts_ref[0, t] = (slot_ref[0, t] // cap) * rows + slot_ref[0, t] % cap
        for c in range(3):
            at = c * tiles + t
            faces_ref[0, at : at + 1] = pos_ref[0, c, pl.ds(face_ref[0, t], 1)]
            faces_ref[1, at : at + 1] = normal_ref[0, c, pl.ds(face_ref[0, t], 1)]
    corners, count = nodes_ref.shape[1:]
    tops = disp_ref.shape[0] // 6
    tables = [two_parts(halves(disp_ref, c, tops)) for c in range(3)]
    cuts = [slice(g * lanes, (g + 1) * lanes) for g in range(count // lanes)]
    nodes = [[nodes_ref[0, a : a + 1, cut] for a in range(corners)] for cut in cuts]
    for cut, here in zip(cuts, nodes):
        values = lookup(tables, here)
        for c in range(3):
            local[c * corners : (c + 1) * corners, cut] = jnp.concatenate(values[c], axis=0)
    force = jnp.dot(
        stiff_ref[...], local[...], precision=lax.Precision.HIGHEST, preferred_element_type=f32
    )
    local[...] = -(force * modulus_ref[...])
    for g, (cut, here) in enumerate(zip(cuts, nodes)):
        values = [
            [local[c * corners + a : c * corners + a + 1, cut] for a in range(corners)]
            for c in range(3)
        ]
        added = node_sums(here, values, tops)
        sums[...] = added if g == 0 else sums[...] + added
    out_ref[...] = jnp.zeros_like(out_ref)
    for c in range(3):
        add_halves(out_ref, sums[...], c, tops)


def tile_kernel(cap, starts_ref, got_ref, faces_ref, weight_ref, out_ref, slots_ref, flat):
    parts, rows, _ = got_ref.shape
    tiles = starts_ref.shape[1]
    for j in range(parts):
        flat[j * rows : (j + 1) * rows] = got_ref[j].astype(f32)
    slots_ref[...] = jnp.concatenate(
        [flat[j * rows + 3 * cap : j * rows + 3 * cap + 1] for j in range(parts)], axis=0
    ).astype(jnp.int32)
    x = jnp.concatenate(
        [flat[pl.ds(starts_ref[0, t] + c * cap, 1)] for c in range(3) for t in range(tiles)], axis=0
    )
    weights = weight_ref[0].reshape(tiles * lanes, lanes)
    crossed = lax.dot_general(
        x.astype(bf16), weights, (((1,), (1,)), ((), ())), preferred_element_type=f32
    )
    line = lax.broadcasted_iota(jnp.int32, (tiles, lanes), 0)
    gap = jnp.zeros((tiles, lanes), f32)
    normals = []
    for c in range(3):
        interp = jnp.zeros((tiles, lanes), f32)
        for t in range(tiles):
            here = crossed[c * tiles : (c + 1) * tiles, t * lanes : (t + 1) * lanes]
            interp = jnp.where(line == t, here, interp)
        normal = faces_ref[1, c * tiles : (c + 1) * tiles]
        gap += normal * (interp - faces_ref[0, c * tiles : (c + 1) * tiles])
        normals.append(normal)
    pressure = penalty * jnp.maximum(-gap, 0.0)
    push = [pressure * normal for normal in normals]
    spread = jnp.concatenate(
        [
            jnp.concatenate([jnp.where(line == t, p, 0.0) for p in push], axis=0).astype(bf16)
            for t in range(tiles)
        ],
        axis=1,
    )
    forces = jnp.dot(spread, weights, preferred_element_type=f32)
    for j in range(parts):
        out_ref[j] = forces


def list_kernel(cap, tiles, slots_ref, region_ref, lo_ref, hi_ref, list_ref, both_ref, run_of):
    shared = lo_ref.shape[0]
    both_ref[:shared] = lo_ref[...]
    both_ref[shared:] = hi_ref[...]
    parts = slots_ref.shape[0]
    nblk = region_ref.shape[1]
    me = lax.axis_index("dom")
    for q in range(nblk // cap):
        run_of[region_ref[0, q * cap]] = q * cap

    def pick(j, filled):
        for t in range(tiles):
            slot = slots_ref[j, t]
            mine = slot // cap == me
            list_ref[0, filled] = j * 3 * tiles + t
            list_ref[1, filled] = jnp.where(mine, run_of[j] + slot % cap, 0)
            filled = filled + jnp.where(mine, 1, 0)
        return filled

    filled = lax.fori_loop(0, parts, pick, 0)
    for i in range(8):
        list_ref[0, filled + i] = 0
        list_ref[1, filled + i] = 0
    list_ref[0, list_ref.shape[1] - 1] = filled


def contact_kernel(tiles, list_ref, back_ref, surf_ref, part_ref, out_ref):
    tops = part_ref.shape[0] // 6
    out_ref[...] = part_ref[...]
    filled = list_ref[0, list_ref.shape[1] - 1]

    def spread(g, _):
        nodes, values = [], [[], [], []]
        for i in range(8):
            row = surf_ref[0, pl.ds(list_ref[1, g * 8 + i], 1)]
            nodes.append(jnp.where(g * 8 + i < filled, row, -1))
            for c in range(3):
                values[c].append(back_ref[pl.ds(list_ref[0, g * 8 + i] + c * tiles, 1)])
        sums = node_sums(nodes, values, tops)
        for c in range(3):
            add_halves(out_ref, sums, c, tops)
        return 0

    lax.fori_loop(0, (filled + 7) // 8, spread, 0)


def pair_kernel(part_ref, other_ref, mass_ref, both_ref, out_ref, share_lo_ref, share_hi_ref):
    tops = mass_ref.shape[0] // 2
    out_ref[...] = part_ref[...] + other_ref[...]
    count = both_ref.shape[0]
    shared = count // 2
    tables = [two_parts(halves(out_ref, c, tops)) for c in range(3)]
    tables.append(two_parts(halves(mass_ref, 0, tops)))
    values = lookup(tables, [both_ref[k : k + 1] for k in range(count)])
    for c in range(4):
        share_lo_ref[c * shared : (c + 1) * shared] = jnp.concatenate(values[c][:shared], axis=0)
        share_hi_ref[c * shared : (c + 1) * shared] = jnp.concatenate(values[c][shared:], axis=0)


def share_kernel(part_ref, mass_ref, up_ref, down_ref, both_ref, out_ref, out_mass_ref):
    tops = mass_ref.shape[0] // 2
    out_ref[...] = part_ref[...]
    out_mass_ref[...] = mass_ref[...]
    count = both_ref.shape[0]
    shared = count // 2
    nodes = [both_ref[k : k + 1] for k in range(count)]
    values = [
        [ref[c * shared + k : c * shared + k + 1] for ref in (down_ref, up_ref) for k in range(shared)]
        for c in range(4)
    ]
    sums = node_sums(nodes, values, tops)
    for c in range(3):
        add_halves(out_ref, sums, c, tops)
    add_halves(out_mass_ref, sums, 3, tops, 0)


def accel_kernel(mass_ref, own_ref, other_ref, out_ref):
    total = own_ref[...] + other_ref[...]
    size = mass_ref.shape[0]
    for c in range(3):
        at = slice(c * size, (c + 1) * size)
        out_ref[at] = total[at] / mass_ref[...]


def shifted(block, axis, distance):
    devices = range(lax.axis_size(axis))
    route = [(i - distance, i) for i in devices if i - distance in devices]
    return lax.ppermute(block, axis, route)


def from_mate(block, distance):
    return lax.ppermute(
        block, "rep", [(i, i ^ distance) for i in range(lax.axis_size("rep"))]
    )


def on_device(
    coords,
    disp,
    mass,
    stiffness,
    elem_nodes,
    modulus,
    surf_nodes,
    block_region,
    face_pos,
    face_normal,
    tile_slot,
    tile_face,
    tile_weight,
    shared_lo,
    shared_hi,
):
    parts = lax.axis_size("dom")
    mates = lax.axis_size("rep")
    nodes_all = disp.shape[2]
    nblk = surf_nodes.shape[1]
    tiles = tile_slot.shape[1]
    cap = max(2, 2 * nblk // parts)
    rows = (3 * cap + 1 + 15) // 16 * 16
    node_array = jax.ShapeDtypeStruct((3 * nodes_all // lanes, lanes), f32)
    mass_array = jax.ShapeDtypeStruct((nodes_all // lanes, lanes), f32)
    coords = coords.reshape(node_array.shape)
    disp = disp.reshape(node_array.shape)
    mass = mass.reshape(mass_array.shape)
    shared_lo = shared_lo.reshape(-1, lanes)
    shared_hi = shared_hi.reshape(-1, lanes)
    share = jax.ShapeDtypeStruct((4 * shared_lo.shape[0], lanes), f32)

    outgoing = call(
        functools.partial(pack_kernel, cap),
        jax.ShapeDtypeStruct((parts, rows, lanes), bf16),
        [hbm] * 5,
        vmem,
        [
            pltpu.VMEM((nblk // cap, rows, lanes), f32),
            pltpu.SMEM(block_region.shape, jnp.int32),
            pltpu.SMEM(tile_slot.shape, jnp.int32),
            pltpu.VMEM(coords.shape, f32),
            pltpu.VMEM(disp.shape, f32),
            pltpu.VMEM(surf_nodes.shape, jnp.int32),
            pltpu.SemaphoreType.DMA((5,)),
        ],
        1 << 30,
        60,
    )(block_region, tile_slot, coords, disp, surf_nodes)
    arrived = lax.all_to_all(outgoing, "dom", split_axis=0, concat_axis=0, tiled=True)

    part, faces, starts = call(
        functools.partial(element_kernel, cap, rows),
        (
            node_array,
            jax.ShapeDtypeStruct((2, 3 * tiles, lanes), f32),
            jax.ShapeDtypeStruct((1, tiles), jnp.int32),
        ),
        [smem] * 2 + [vmem] * 6,
        (vmem, vmem, smem),
        [
            pltpu.VMEM((24, modulus.shape[1]), f32),
            pltpu.VMEM((3 * nodes_all // wide, wide), f32),
        ],
        1 << 32,
    )(
        tile_slot,
        tile_face,
        jnp.swapaxes(face_pos, 1, 2),
        jnp.swapaxes(face_normal, 1, 2),
        disp,
        stiffness,
        modulus,
        elem_nodes,
    )

    forces, slots = call(
        functools.partial(tile_kernel, cap),
        (
            jax.ShapeDtypeStruct((parts, 3 * tiles, lanes), f32),
            jax.ShapeDtypeStruct((parts, lanes), jnp.int32),
        ),
        [smem] + [vmem] * 3,
        (vmem, vmem),
        [pltpu.VMEM((parts * rows, lanes), f32)],
        1 << 28,
    )(starts, arrived, faces, tile_weight)
    back = lax.all_to_all(forces, "dom", split_axis=0, concat_axis=0, tiled=True)
    both_array = jax.ShapeDtypeStruct((2 * shared_lo.shape[0], lanes), jnp.int32)
    picks, both = call(
        functools.partial(list_kernel, cap, tiles),
        (jax.ShapeDtypeStruct((2, parts * tiles + 16), jnp.int32), both_array),
        [smem, smem, vmem, vmem],
        (smem, vmem),
        [pltpu.SMEM((parts,), jnp.int32)],
        1 << 24,
    )(slots, block_region, shared_lo, shared_hi)

    part = call(
        functools.partial(contact_kernel, tiles), node_array, [smem] + [vmem] * 3, vmem, [], 1 << 28
    )(picks, back.reshape(-1, lanes), surf_nodes, part)
    pair, share_lo, share_hi = call(
        pair_kernel, (node_array, share, share), [vmem] * 4, (vmem, vmem, vmem), [], 1 << 28
    )(part, from_mate(part, 1), mass, both)
    from_upper = shifted(share_lo, "dom", -1)
    from_lower = shifted(share_hi, "dom", 1)

    own, own_mass = call(
        share_kernel, (node_array, mass_array), [vmem] * 5, (vmem, vmem), [], 1 << 28
    )(pair, mass, from_upper, from_lower, both)
    distance = 2
    while 2 * distance < mates:
        own = own + from_mate(own, distance)
        distance *= 2
    accel = call(accel_kernel, node_array, [vmem] * 3, vmem, [], 1 << 24)(
        own_mass, own, from_mate(own, distance)
    )
    return accel.reshape(1, 3, nodes_all)


def solution(mesh):
    in_specs = (
        P("dom", None, None),
        P("dom", None, None),
        P("dom", None),
        P(),
        P("dom", None, "rep"),
        P("dom", "rep"),
        P("dom", None, None),
        P("dom", None),
        P("dom", None, None, None),
        P("dom", None, None, None),
        P("dom", "rep"),
        P("dom", "rep"),
        P("dom", "rep", None, None),
        P("dom", None),
        P("dom", None),
    )
    out_specs = P("dom", None, None)
    return jax.shard_map(
        on_device, mesh=mesh, in_specs=in_specs, out_specs=out_specs, check_vma=False
    )
```

```python
import functools

import jax
import jax.numpy as jnp
from jax import lax
from jax.experimental import pallas as pl
from jax.experimental.pallas import tpu as pltpu
from jax.sharding import PartitionSpec as P

penalty = 4.0
lanes = 128
wide = 256
vmem = pl.BlockSpec(memory_space=pltpu.VMEM)
smem = pl.BlockSpec(memory_space=pltpu.SMEM)
hbm = pl.BlockSpec(memory_space=pltpu.HBM)
f32 = jnp.float32
bf16 = jnp.bfloat16


def call(body, out_shape, in_specs, out_specs, scratch, flops, vmem_mib=32):
    return pl.pallas_call(
        body,
        out_shape=out_shape,
        in_specs=in_specs,
        out_specs=out_specs,
        scratch_shapes=scratch,
        compiler_params=pltpu.CompilerParams(vmem_limit_bytes=vmem_mib * 1024 * 1024),
        cost_estimate=pl.CostEstimate(flops=flops, bytes_accessed=1 << 20, transcendentals=0),
    )


def one_hot(nodes):
    line = lax.broadcasted_iota(jnp.int32, (wide, lanes), 0).astype(f32).astype(bf16)
    low = [(row & (wide - 1)).astype(f32).astype(bf16) for row in nodes]
    one, zero = jnp.ones((), bf16), jnp.zeros((), bf16)
    return jnp.concatenate([jnp.where(line == row, one, zero) for row in low], axis=1)


def halves(ref, c, tops):
    at = c * 2 * tops
    return jnp.concatenate(
        [ref[pl.ds(at, tops, stride=2)], ref[pl.ds(at + 1, tops, stride=2)]], axis=1
    )


def two_parts(x):
    coarse = x.astype(bf16)
    return [coarse, (x - coarse.astype(f32)).astype(bf16)]


def lookup(tables, nodes):
    tops = tables[0][0].shape[0]
    stacked = jnp.concatenate([part for table in tables for part in table], axis=0)
    found = jnp.dot(stacked, one_hot(nodes), preferred_element_type=f32)
    line = lax.broadcasted_iota(jnp.int32, (tops, lanes), 0)
    values = [[] for _ in tables]
    for i, row in enumerate(nodes):
        match = line == (row >> 8)
        at = 0
        for c, table in enumerate(tables):
            here = found[at : at + tops, i * lanes : (i + 1) * lanes]
            for p in range(1, len(table)):
                here += found[at + p * tops : at + (p + 1) * tops, i * lanes : (i + 1) * lanes]
            at += len(table) * tops
            values[c].append(jnp.sum(jnp.where(match, here, 0.0), axis=0, keepdims=True))
    return values


def node_sums(nodes, values, tops, parts=2):
    line = lax.broadcasted_iota(jnp.int32, (tops, lanes), 0)
    comps = len(values)
    left = []
    for i, row in enumerate(nodes):
        match = line == (row >> 8)
        pieces = [v[i] for v in values]
        if parts == 2:
            coarse = [v.astype(bf16).astype(f32) for v in pieces]
            pieces = coarse + [v - w for v, w in zip(pieces, coarse)]
        left.append(
            jnp.concatenate([jnp.where(match, v, 0.0).astype(bf16) for v in pieces], axis=0)
        )
    both = lax.dot_general(
        jnp.concatenate(left, axis=1),
        one_hot(nodes),
        (((1,), (1,)), ((), ())),
        preferred_element_type=f32,
    )
    return both if parts == 1 else both[: comps * tops] + both[comps * tops :]


def add_halves(ref, sums, c, tops, row=None):
    at = (c if row is None else row) * 2 * tops
    for half in range(2):
        ref[pl.ds(at + half, tops, stride=2)] += sums[
            c * tops : (c + 1) * tops, half * lanes : (half + 1) * lanes
        ]


def pack_kernel(
    cap, region_hbm, slot_hbm, coords_hbm, disp_hbm, surf_hbm, out_ref,
    stage, region_ref, slot_ref, coords_ref, disp_ref, surf_ref, sems,
):
    sources = (coords_hbm, disp_hbm, slot_hbm, surf_hbm, region_hbm)
    places = (coords_ref, disp_ref, slot_ref, surf_ref, region_ref)
    copies = [
        pltpu.make_async_copy(a, b, sems.at[i]) for i, (a, b) in enumerate(zip(sources, places))
    ]
    for copy in copies:
        copy.start()
    parts, rows, _ = out_ref.shape
    nblk = surf_ref.shape[1]
    tiles = slot_ref.shape[1]
    tops = coords_ref.shape[0] // 6
    for copy in copies:
        copy.wait()
    rest = (rows - 3 * cap, lanes)
    lane = lax.broadcasted_iota(jnp.int32, rest, 1)
    line = lax.broadcasted_iota(jnp.int32, rest, 0)
    tail = jnp.zeros(rest, f32)
    for t in range(tiles):
        tail = jnp.where((lane == t) & (line == 0), slot_ref[0, t].astype(f32), tail)
    for q in range(nblk // cap):
        stage[q, 3 * cap :] = tail
    empty = jnp.concatenate([jnp.zeros((3 * cap, lanes), f32), tail], axis=0).astype(bf16)
    for j in range(parts):
        out_ref[j] = empty
    tables = [
        [(halves(coords_ref, c, tops) + halves(disp_ref, c, tops)).astype(bf16)] for c in range(3)
    ]
    size = min(cap, 8)
    for first in range(0, nblk, 8):
        values = lookup(tables, [surf_ref[0, first + i : first + i + 1] for i in range(8)])
        for b in range(first, first + 8, size):
            for c in range(3):
                at = c * cap + b % cap
                stage[b // cap, at : at + size] = jnp.concatenate(
                    values[c][b - first : b - first + size], axis=0
                )
    for q in range(nblk // cap):
        out_ref[region_ref[0, q * cap]] = stage[q].astype(bf16)


def element_kernel(
    cap, rows, slot_ref, face_ref, pos_ref, normal_ref, disp_ref, stiff_ref, modulus_ref, nodes_ref,
    out_ref, faces_ref, starts_ref, local, sums,
):
    tiles = slot_ref.shape[1]
    for t in range(tiles):
        starts_ref[0, t] = (slot_ref[0, t] // cap) * rows + slot_ref[0, t] % cap
        for c in range(3):
            at = c * tiles + t
            faces_ref[0, at : at + 1] = pos_ref[0, c, pl.ds(face_ref[0, t], 1)]
            faces_ref[1, at : at + 1] = normal_ref[0, c, pl.ds(face_ref[0, t], 1)]
    corners, count = nodes_ref.shape[1:]
    tops = disp_ref.shape[0] // 6
    tables = [two_parts(halves(disp_ref, c, tops)) for c in range(3)]
    cuts = [slice(g * lanes, (g + 1) * lanes) for g in range(count // lanes)]
    nodes = [[nodes_ref[0, a : a + 1, cut] for a in range(corners)] for cut in cuts]
    for cut, here in zip(cuts, nodes):
        values = lookup(tables, here)
        for c in range(3):
            local[c * corners : (c + 1) * corners, cut] = jnp.concatenate(values[c], axis=0)
    force = jnp.dot(
        stiff_ref[...], local[...], precision=lax.Precision.HIGHEST, preferred_element_type=f32
    )
    local[...] = -(force * modulus_ref[...])
    for g, (cut, here) in enumerate(zip(cuts, nodes)):
        values = [
            [local[c * corners + a : c * corners + a + 1, cut] for a in range(corners)]
            for c in range(3)
        ]
        added = node_sums(here, values, tops)
        sums[...] = added if g == 0 else sums[...] + added
    out_ref[...] = jnp.zeros_like(out_ref)
    for c in range(3):
        add_halves(out_ref, sums[...], c, tops)


def tile_kernel(cap, starts_ref, got_ref, faces_ref, weight_ref, out_ref, slots_ref, flat):
    parts, rows, _ = got_ref.shape
    tiles = starts_ref.shape[1]
    for j in range(parts):
        flat[j * rows : (j + 1) * rows] = got_ref[j].astype(f32)
    slots_ref[...] = jnp.concatenate(
        [flat[j * rows + 3 * cap : j * rows + 3 * cap + 1] for j in range(parts)], axis=0
    ).astype(jnp.int32)
    x = jnp.concatenate(
        [flat[pl.ds(starts_ref[0, t] + c * cap, 1)] for c in range(3) for t in range(tiles)], axis=0
    )
    weights = weight_ref[0].reshape(tiles * lanes, lanes)
    crossed = lax.dot_general(
        x.astype(bf16), weights, (((1,), (1,)), ((), ())), preferred_element_type=f32
    )
    line = lax.broadcasted_iota(jnp.int32, (tiles, lanes), 0)
    gap = jnp.zeros((tiles, lanes), f32)
    normals = []
    for c in range(3):
        interp = jnp.zeros((tiles, lanes), f32)
        for t in range(tiles):
            here = crossed[c * tiles : (c + 1) * tiles, t * lanes : (t + 1) * lanes]
            interp = jnp.where(line == t, here, interp)
        normal = faces_ref[1, c * tiles : (c + 1) * tiles]
        gap += normal * (interp - faces_ref[0, c * tiles : (c + 1) * tiles])
        normals.append(normal)
    pressure = penalty * jnp.maximum(-gap, 0.0)
    push = [pressure * normal for normal in normals]
    spread = jnp.concatenate(
        [
            jnp.concatenate([jnp.where(line == t, p, 0.0) for p in push], axis=0).astype(bf16)
            for t in range(tiles)
        ],
        axis=1,
    )
    forces = jnp.dot(spread, weights, preferred_element_type=f32).astype(bf16)
    pad = out_ref.shape[1] - forces.shape[0]
    if pad:
        forces = jnp.concatenate([forces, jnp.zeros((pad, lanes), bf16)], axis=0)
    for j in range(parts):
        out_ref[j] = forces


def list_kernel(cap, tiles, force_rows, slots_ref, region_ref, lo_ref, hi_ref, list_ref, both_ref, run_of):
    shared = lo_ref.shape[0]
    both_ref[:shared] = lo_ref[...]
    both_ref[shared:] = hi_ref[...]
    parts = slots_ref.shape[0]
    nblk = region_ref.shape[1]
    me = lax.axis_index("dom")
    for q in range(nblk // cap):
        run_of[region_ref[0, q * cap]] = q * cap

    def pick(j, filled):
        run = run_of[j]
        slots = [slots_ref[j, t] for t in range(tiles)]
        mine = [slot // cap == me for slot in slots]
        blocks = [jnp.where(own, run + slot % cap, 0) for own, slot in zip(mine, slots)]
        places = []
        for own in mine:
            places.append(filled)
            filled = filled + jnp.where(own, 1, 0)
        for t in range(tiles):
            list_ref[0, places[t]] = j * force_rows + t
            list_ref[1, places[t]] = blocks[t]
        return filled

    filled = lax.fori_loop(0, parts, pick, 0)
    for i in range(8):
        list_ref[0, filled + i] = 0
        list_ref[1, filled + i] = 0
    list_ref[0, list_ref.shape[1] - 1] = filled


def contact_kernel(tiles, list_ref, back_ref, surf_ref, part_ref, out_ref, back):
    parts, rows, _ = back_ref.shape
    tops = part_ref.shape[0] // 6
    out_ref[...] = part_ref[...]
    for j in range(parts):
        back[j * rows : (j + 1) * rows] = back_ref[j].astype(f32)
    filled = list_ref[0, list_ref.shape[1] - 1]

    def spread(g, _):
        nodes, values = [], [[], [], []]
        for i in range(8):
            row = surf_ref[0, pl.ds(list_ref[1, g * 8 + i], 1)]
            nodes.append(jnp.where(g * 8 + i < filled, row, -1))
            for c in range(3):
                values[c].append(back[pl.ds(list_ref[0, g * 8 + i] + c * tiles, 1)])
        sums = node_sums(nodes, values, tops, 1)
        for c in range(3):
            add_halves(out_ref, sums, c, tops)
        return 0

    lax.fori_loop(0, (filled + 7) // 8, spread, 0)


def pair_kernel(part_ref, other_ref, mass_ref, both_ref, out_ref, share_lo_ref, share_hi_ref):
    tops = mass_ref.shape[0] // 2
    out_ref[...] = part_ref[...] + other_ref[...]
    count = both_ref.shape[0]
    shared = count // 2
    tables = [two_parts(halves(out_ref, c, tops)) for c in range(3)]
    tables.append(two_parts(halves(mass_ref, 0, tops)))
    values = lookup(tables, [both_ref[k : k + 1] for k in range(count)])
    for c in range(4):
        share_lo_ref[c * shared : (c + 1) * shared] = jnp.concatenate(values[c][:shared], axis=0)
        share_hi_ref[c * shared : (c + 1) * shared] = jnp.concatenate(values[c][shared:], axis=0)


def summed(terms):
    while len(terms) > 1:
        terms = [a + b for a, b in zip(terms[::2], terms[1::2])]
    return terms[0]


def accel_kernel(pairs, mass_ref, both_ref, *refs):
    sum_refs, up_refs, down_refs = refs[:pairs], refs[pairs : 2 * pairs], refs[2 * pairs : 3 * pairs]
    out_ref, total, total_mass = refs[3 * pairs :]
    tops = mass_ref.shape[0] // 2
    total[...] = summed([ref[...] for ref in sum_refs])
    total_mass[...] = mass_ref[...]
    count = both_ref.shape[0]
    shared = count // 2
    nodes = [both_ref[k : k + 1] for k in range(count)]
    values = [[] for _ in range(4)]
    for terms in (down_refs, up_refs):
        force = summed([ref[: 3 * shared] for ref in terms])
        for k in range(shared):
            for c in range(3):
                values[c].append(force[c * shared + k : c * shared + k + 1])
            values[3].append(terms[0][3 * shared + k : 3 * shared + k + 1])
    sums = node_sums(nodes, values, tops)
    for c in range(3):
        add_halves(total, sums, c, tops)
    add_halves(total_mass, sums, 3, tops, 0)
    size = 2 * tops
    for c in range(3):
        at = slice(c * size, (c + 1) * size)
        out_ref[at] = total[at] / total_mass[...]


def shifted(block, distance, mate):
    parts, mates = lax.axis_size("dom"), lax.axis_size("rep")
    route = [
        ((s - distance) * mates + (r ^ mate), s * mates + r)
        for s in range(parts)
        if 0 <= s - distance < parts
        for r in range(mates)
    ]
    return lax.ppermute(block, ("dom", "rep"), route)


def from_mate(block, distance):
    return lax.ppermute(
        block, "rep", [(i, i ^ distance) for i in range(lax.axis_size("rep"))]
    )


def on_device(
    coords,
    disp,
    mass,
    stiffness,
    elem_nodes,
    modulus,
    surf_nodes,
    block_region,
    face_pos,
    face_normal,
    tile_slot,
    tile_face,
    tile_weight,
    shared_lo,
    shared_hi,
):
    parts = lax.axis_size("dom")
    mates = lax.axis_size("rep")
    nodes_all = disp.shape[2]
    nblk = surf_nodes.shape[1]
    tiles = tile_slot.shape[1]
    cap = max(2, 2 * nblk // parts)
    rows = (3 * cap + 1 + 15) // 16 * 16
    force_rows = (3 * tiles + 15) // 16 * 16
    node_array = jax.ShapeDtypeStruct((3 * nodes_all // lanes, lanes), f32)
    mass_array = jax.ShapeDtypeStruct((nodes_all // lanes, lanes), f32)
    coords = coords.reshape(node_array.shape)
    disp = disp.reshape(node_array.shape)
    mass = mass.reshape(mass_array.shape)
    shared_lo = shared_lo.reshape(-1, lanes)
    shared_hi = shared_hi.reshape(-1, lanes)
    share = jax.ShapeDtypeStruct((4 * shared_lo.shape[0], lanes), f32)

    outgoing = call(
        functools.partial(pack_kernel, cap),
        jax.ShapeDtypeStruct((parts, rows, lanes), bf16),
        [hbm] * 5,
        vmem,
        [
            pltpu.VMEM((nblk // cap, rows, lanes), f32),
            pltpu.SMEM(block_region.shape, jnp.int32),
            pltpu.SMEM(tile_slot.shape, jnp.int32),
            pltpu.VMEM(coords.shape, f32),
            pltpu.VMEM(disp.shape, f32),
            pltpu.VMEM(surf_nodes.shape, jnp.int32),
            pltpu.SemaphoreType.DMA((5,)),
        ],
        1 << 30,
        60,
    )(block_region, tile_slot, coords, disp, surf_nodes)
    arrived = lax.all_to_all(outgoing, "dom", split_axis=0, concat_axis=0, tiled=True)

    part, faces, starts = call(
        functools.partial(element_kernel, cap, rows),
        (
            node_array,
            jax.ShapeDtypeStruct((2, 3 * tiles, lanes), f32),
            jax.ShapeDtypeStruct((1, tiles), jnp.int32),
        ),
        [smem] * 2 + [vmem] * 6,
        (vmem, vmem, smem),
        [
            pltpu.VMEM((24, modulus.shape[1]), f32),
            pltpu.VMEM((3 * nodes_all // wide, wide), f32),
        ],
        1 << 32,
    )(
        tile_slot,
        tile_face,
        jnp.swapaxes(face_pos, 1, 2),
        jnp.swapaxes(face_normal, 1, 2),
        disp,
        stiffness,
        modulus,
        elem_nodes,
    )

    forces, slots = call(
        functools.partial(tile_kernel, cap),
        (
            jax.ShapeDtypeStruct((parts, force_rows, lanes), bf16),
            jax.ShapeDtypeStruct((parts, lanes), jnp.int32),
        ),
        [smem] + [vmem] * 3,
        (vmem, vmem),
        [pltpu.VMEM((parts * rows, lanes), f32)],
        1 << 28,
    )(starts, arrived, faces, tile_weight)
    back = lax.all_to_all(forces, "dom", split_axis=0, concat_axis=0, tiled=True)
    both_array = jax.ShapeDtypeStruct((2 * shared_lo.shape[0], lanes), jnp.int32)
    picks, both = call(
        functools.partial(list_kernel, cap, tiles, force_rows),
        (jax.ShapeDtypeStruct((2, parts * tiles + 16), jnp.int32), both_array),
        [smem, smem, vmem, vmem],
        (smem, vmem),
        [pltpu.SMEM((parts,), jnp.int32)],
        1 << 24,
    )(slots, block_region, shared_lo, shared_hi)

    part = call(
        functools.partial(contact_kernel, tiles),
        node_array,
        [smem] + [vmem] * 3,
        vmem,
        [pltpu.VMEM((parts * force_rows, lanes), f32)],
        1 << 28,
    )(picks, back, surf_nodes, part)
    pair, share_lo, share_hi = call(
        pair_kernel, (node_array, share, share), [vmem] * 4, (vmem, vmem, vmem), [], 1 << 28
    )(part, from_mate(part, 1), mass, both)
    steps = range(0, mates, 2)
    sums = [pair] + [from_mate(pair, k) for k in steps[1:]]
    from_upper = [shifted(share_lo, -1, k) for k in steps]
    from_lower = [shifted(share_hi, 1, k) for k in steps]
    accel = call(
        functools.partial(accel_kernel, len(steps)),
        node_array,
        [vmem] * (2 + 3 * len(steps)),
        vmem,
        [pltpu.VMEM(node_array.shape, f32), pltpu.VMEM(mass_array.shape, f32)],
        1 << 24,
    )(mass, both, *sums, *from_upper, *from_lower)
    return accel.reshape(1, 3, nodes_all)


def solution(mesh):
    in_specs = (
        P("dom", None, None),
        P("dom", None, None),
        P("dom", None),
        P(),
        P("dom", None, "rep"),
        P("dom", "rep"),
        P("dom", None, None),
        P("dom", None),
        P("dom", None, None, None),
        P("dom", None, None, None),
        P("dom", "rep"),
        P("dom", "rep"),
        P("dom", "rep", None, None),
        P("dom", None),
        P("dom", None),
    )
    out_specs = P("dom", None, None)
    return jax.shard_map(
        on_device, mesh=mesh, in_specs=in_specs, out_specs=out_specs, check_vma=False
    )
```

```python
import functools

import jax
import jax.numpy as jnp
from jax import lax
from jax.experimental import pallas as pl
from jax.experimental.pallas import tpu as pltpu
from jax.sharding import PartitionSpec as P

penalty = 4.0
lanes = 128
wide = 256
vmem = pl.BlockSpec(memory_space=pltpu.VMEM)
smem = pl.BlockSpec(memory_space=pltpu.SMEM)
hbm = pl.BlockSpec(memory_space=pltpu.HBM)
f32 = jnp.float32
bf16 = jnp.bfloat16


def call(body, out_shape, in_specs, out_specs, scratch, flops, vmem_mib=32):
    return pl.pallas_call(
        body,
        out_shape=out_shape,
        in_specs=in_specs,
        out_specs=out_specs,
        scratch_shapes=scratch,
        compiler_params=pltpu.CompilerParams(vmem_limit_bytes=vmem_mib * 1024 * 1024),
        cost_estimate=pl.CostEstimate(flops=flops, bytes_accessed=1 << 20, transcendentals=0),
    )


def one_hot(nodes):
    line = lax.broadcasted_iota(jnp.int32, (wide, lanes), 0).astype(f32).astype(bf16)
    low = [(row & (wide - 1)).astype(f32).astype(bf16) for row in nodes]
    one, zero = jnp.ones((), bf16), jnp.zeros((), bf16)
    return jnp.concatenate([jnp.where(line == row, one, zero) for row in low], axis=1)


def halves(ref, c, tops):
    at = c * 2 * tops
    return jnp.concatenate(
        [ref[pl.ds(at, tops, stride=2)], ref[pl.ds(at + 1, tops, stride=2)]], axis=1
    )


def two_parts(x):
    coarse = x.astype(bf16)
    return [coarse, (x - coarse.astype(f32)).astype(bf16)]


def lookup(tables, nodes):
    tops = tables[0][0].shape[0]
    stacked = jnp.concatenate([part for table in tables for part in table], axis=0)
    found = jnp.dot(stacked, one_hot(nodes), preferred_element_type=f32)
    line = lax.broadcasted_iota(jnp.int32, (tops, lanes), 0)
    values = [[] for _ in tables]
    for i, row in enumerate(nodes):
        match = line == (row >> 8)
        at = 0
        for c, table in enumerate(tables):
            here = found[at : at + tops, i * lanes : (i + 1) * lanes]
            for p in range(1, len(table)):
                here += found[at + p * tops : at + (p + 1) * tops, i * lanes : (i + 1) * lanes]
            at += len(table) * tops
            values[c].append(jnp.sum(jnp.where(match, here, 0.0), axis=0, keepdims=True))
    return values


def node_sums(nodes, values, tops, parts=2):
    line = lax.broadcasted_iota(jnp.int32, (tops, lanes), 0)
    comps = len(values)
    left = []
    for i, row in enumerate(nodes):
        match = line == (row >> 8)
        pieces = [v[i] for v in values]
        if parts == 2:
            coarse = [v.astype(bf16).astype(f32) for v in pieces]
            pieces = coarse + [v - w for v, w in zip(pieces, coarse)]
        left.append(
            jnp.concatenate([jnp.where(match, v, 0.0).astype(bf16) for v in pieces], axis=0)
        )
    both = lax.dot_general(
        jnp.concatenate(left, axis=1),
        one_hot(nodes),
        (((1,), (1,)), ((), ())),
        preferred_element_type=f32,
    )
    return both if parts == 1 else both[: comps * tops] + both[comps * tops :]


def add_halves(ref, sums, c, tops, row=None):
    at = (c if row is None else row) * 2 * tops
    for half in range(2):
        ref[pl.ds(at + half, tops, stride=2)] += sums[
            c * tops : (c + 1) * tops, half * lanes : (half + 1) * lanes
        ]


def pack_kernel(
    cap, region_hbm, slot_hbm, coords_hbm, disp_hbm, surf_hbm, out_ref,
    stage, region_ref, slot_ref, coords_ref, disp_ref, surf_ref, sems,
):
    sources = (coords_hbm, disp_hbm, slot_hbm, surf_hbm, region_hbm)
    places = (coords_ref, disp_ref, slot_ref, surf_ref, region_ref)
    copies = [
        pltpu.make_async_copy(a, b, sems.at[i]) for i, (a, b) in enumerate(zip(sources, places))
    ]
    for copy in copies:
        copy.start()
    parts, rows, _ = out_ref.shape
    nblk = surf_ref.shape[1]
    tiles = slot_ref.shape[1]
    tops = coords_ref.shape[0] // 6
    for copy in copies:
        copy.wait()
    rest = (rows - 3 * cap, lanes)
    lane = lax.broadcasted_iota(jnp.int32, rest, 1)
    line = lax.broadcasted_iota(jnp.int32, rest, 0)
    tail = jnp.zeros(rest, f32)
    for t in range(tiles):
        tail = jnp.where((lane == t) & (line == 0), slot_ref[0, t].astype(f32), tail)
    for q in range(nblk // cap):
        stage[q, 3 * cap :] = tail
    empty = jnp.concatenate([jnp.zeros((3 * cap, lanes), f32), tail], axis=0).astype(bf16)
    for j in range(parts):
        out_ref[j] = empty
    tables = [
        [(halves(coords_ref, c, tops) + halves(disp_ref, c, tops)).astype(bf16)] for c in range(3)
    ]
    size = min(cap, 8)
    for first in range(0, nblk, 8):
        values = lookup(tables, [surf_ref[0, first + i : first + i + 1] for i in range(8)])
        for b in range(first, first + 8, size):
            for c in range(3):
                at = c * cap + b % cap
                stage[b // cap, at : at + size] = jnp.concatenate(
                    values[c][b - first : b - first + size], axis=0
                )
    for q in range(nblk // cap):
        out_ref[region_ref[0, q * cap]] = stage[q].astype(bf16)


def element_kernel(
    cap, rows, slot_ref, face_ref, pos_ref, normal_ref, disp_ref, stiff_ref, modulus_ref, nodes_ref,
    out_ref, faces_ref, starts_ref, local, sums,
):
    tiles = slot_ref.shape[1]
    for t in range(tiles):
        starts_ref[0, t] = (slot_ref[0, t] // cap) * rows + slot_ref[0, t] % cap
        for c in range(3):
            at = c * tiles + t
            faces_ref[0, at : at + 1] = pos_ref[0, c, pl.ds(face_ref[0, t], 1)]
            faces_ref[1, at : at + 1] = normal_ref[0, c, pl.ds(face_ref[0, t], 1)]
    corners, count = nodes_ref.shape[1:]
    tops = disp_ref.shape[0] // 6
    tables = [two_parts(halves(disp_ref, c, tops)) for c in range(3)]
    cuts = [slice(g * lanes, (g + 1) * lanes) for g in range(count // lanes)]
    nodes = [[nodes_ref[0, a : a + 1, cut] for a in range(corners)] for cut in cuts]
    for cut, here in zip(cuts, nodes):
        values = lookup(tables, here)
        for c in range(3):
            local[c * corners : (c + 1) * corners, cut] = jnp.concatenate(values[c], axis=0)
    force = jnp.dot(
        stiff_ref[...], local[...], precision=lax.Precision.HIGHEST, preferred_element_type=f32
    )
    local[...] = -(force * modulus_ref[...])
    for g, (cut, here) in enumerate(zip(cuts, nodes)):
        values = [
            [local[c * corners + a : c * corners + a + 1, cut] for a in range(corners)]
            for c in range(3)
        ]
        added = node_sums(here, values, tops)
        sums[...] = added if g == 0 else sums[...] + added
    out_ref[...] = jnp.zeros_like(out_ref)
    for c in range(3):
        add_halves(out_ref, sums[...], c, tops)


def tile_kernel(cap, starts_ref, got_ref, faces_ref, weight_ref, out_ref, slots_ref, flat):
    parts, rows, _ = got_ref.shape
    tiles = starts_ref.shape[1]
    for j in range(parts):
        flat[j * rows : (j + 1) * rows] = got_ref[j].astype(f32)
    slots_ref[...] = jnp.concatenate(
        [flat[j * rows + 3 * cap : j * rows + 3 * cap + 1] for j in range(parts)], axis=0
    ).astype(jnp.int32)
    x = jnp.concatenate(
        [flat[pl.ds(starts_ref[0, t] + c * cap, 1)] for c in range(3) for t in range(tiles)], axis=0
    )
    weights = weight_ref[0].reshape(tiles * lanes, lanes)
    crossed = lax.dot_general(
        x.astype(bf16), weights, (((1,), (1,)), ((), ())), preferred_element_type=f32
    )
    line = lax.broadcasted_iota(jnp.int32, (tiles, lanes), 0)
    gap = jnp.zeros((tiles, lanes), f32)
    normals = []
    for c in range(3):
        interp = jnp.zeros((tiles, lanes), f32)
        for t in range(tiles):
            here = crossed[c * tiles : (c + 1) * tiles, t * lanes : (t + 1) * lanes]
            interp = jnp.where(line == t, here, interp)
        normal = faces_ref[1, c * tiles : (c + 1) * tiles]
        gap += normal * (interp - faces_ref[0, c * tiles : (c + 1) * tiles])
        normals.append(normal)
    pressure = penalty * jnp.maximum(-gap, 0.0)
    push = [pressure * normal for normal in normals]
    spread = jnp.concatenate(
        [
            jnp.concatenate([jnp.where(line == t, p, 0.0) for p in push], axis=0).astype(bf16)
            for t in range(tiles)
        ],
        axis=1,
    )
    forces = jnp.dot(spread, weights, preferred_element_type=f32).astype(bf16)
    pad = out_ref.shape[1] - forces.shape[0]
    if pad:
        forces = jnp.concatenate([forces, jnp.zeros((pad, lanes), bf16)], axis=0)
    for j in range(parts):
        out_ref[j] = forces


def list_kernel(cap, tiles, force_rows, slots_ref, region_ref, lo_ref, hi_ref, list_ref, both_ref, run_of):
    shared = lo_ref.shape[0]
    both_ref[:shared] = lo_ref[...]
    both_ref[shared:] = hi_ref[...]
    parts = slots_ref.shape[0]
    nblk = region_ref.shape[1]
    me = lax.axis_index("dom")
    for q in range(nblk // cap):
        run_of[region_ref[0, q * cap]] = q * cap

    def pick(j, filled):
        run = run_of[j]
        slots = [slots_ref[j, t] for t in range(tiles)]
        mine = [slot // cap == me for slot in slots]
        blocks = [jnp.where(own, run + slot % cap, 0) for own, slot in zip(mine, slots)]
        places = []
        for own in mine:
            places.append(filled)
            filled = filled + jnp.where(own, 1, 0)
        for t in range(tiles):
            list_ref[0, places[t]] = j * force_rows + t
            list_ref[1, places[t]] = blocks[t]
        return filled

    filled = lax.fori_loop(0, parts, pick, 0)
    for i in range(8):
        list_ref[0, filled + i] = 0
        list_ref[1, filled + i] = 0
    list_ref[0, list_ref.shape[1] - 1] = filled


def contact_kernel(tiles, list_ref, back_ref, surf_ref, part_ref, out_ref, back):
    parts, rows, _ = back_ref.shape
    tops = part_ref.shape[0] // 6
    out_ref[...] = part_ref[...]
    for j in range(parts):
        back[j * rows : (j + 1) * rows] = back_ref[j].astype(f32)
    filled = list_ref[0, list_ref.shape[1] - 1]

    def spread(g, _):
        nodes, values = [], [[], [], []]
        for i in range(8):
            row = surf_ref[0, pl.ds(list_ref[1, g * 8 + i], 1)]
            nodes.append(jnp.where(g * 8 + i < filled, row, -1))
            for c in range(3):
                values[c].append(back[pl.ds(list_ref[0, g * 8 + i] + c * tiles, 1)])
        sums = node_sums(nodes, values, tops, 1)
        for c in range(3):
            add_halves(out_ref, sums, c, tops)
        return 0

    lax.fori_loop(0, (filled + 7) // 8, spread, 0)


def pair_kernel(part_ref, other_ref, mass_ref, both_ref, out_ref, first_ref, second_ref):
    even = lax.axis_index("dom") % 2 == 0
    tops = mass_ref.shape[0] // 2
    out_ref[...] = part_ref[...] + other_ref[...]
    count = both_ref.shape[0]
    shared = count // 2
    tables = [two_parts(halves(out_ref, c, tops)) for c in range(3)]
    tables.append(two_parts(halves(mass_ref, 0, tops)))
    values = lookup(tables, [both_ref[k : k + 1] for k in range(count)])
    for c in range(4):
        lower = jnp.concatenate(values[c][:shared], axis=0)
        upper = jnp.concatenate(values[c][shared:], axis=0)
        first_ref[c * shared : (c + 1) * shared] = jnp.where(even, upper, lower)
        second_ref[c * shared : (c + 1) * shared] = jnp.where(even, lower, upper)


def share_kernel(part_ref, mass_ref, first_ref, second_ref, both_ref, out_ref, out_mass_ref):
    even = lax.axis_index("dom") % 2 == 0
    tops = mass_ref.shape[0] // 2
    out_ref[...] = part_ref[...]
    out_mass_ref[...] = mass_ref[...]
    first, second = first_ref[...], second_ref[...]
    lower = jnp.where(even, second, first)
    upper = jnp.where(even, first, second)
    count = both_ref.shape[0]
    shared = count // 2
    nodes = [both_ref[k : k + 1] for k in range(count)]
    values = [
        [pack[c * shared + k : c * shared + k + 1] for pack in (lower, upper) for k in range(shared)]
        for c in range(4)
    ]
    sums = node_sums(nodes, values, tops)
    for c in range(3):
        add_halves(out_ref, sums, c, tops)
    add_halves(out_mass_ref, sums, 3, tops, 0)


def accel_kernel(mass_ref, own_ref, other_ref, out_ref):
    total = own_ref[...] + other_ref[...]
    size = mass_ref.shape[0]
    for c in range(3):
        at = slice(c * size, (c + 1) * size)
        out_ref[at] = total[at] / mass_ref[...]


def swapped(block, start):
    lows = range(start, lax.axis_size("dom") - 1, 2)
    return lax.ppermute(block, "dom", [(s, s + 1) for s in lows] + [(s + 1, s) for s in lows])


def from_mate(block, distance):
    return lax.ppermute(
        block, "rep", [(i, i ^ distance) for i in range(lax.axis_size("rep"))]
    )


def on_device(
    coords,
    disp,
    mass,
    stiffness,
    elem_nodes,
    modulus,
    surf_nodes,
    block_region,
    face_pos,
    face_normal,
    tile_slot,
    tile_face,
    tile_weight,
    shared_lo,
    shared_hi,
):
    parts = lax.axis_size("dom")
    mates = lax.axis_size("rep")
    nodes_all = disp.shape[2]
    nblk = surf_nodes.shape[1]
    tiles = tile_slot.shape[1]
    cap = max(2, 2 * nblk // parts)
    rows = (3 * cap + 1 + 15) // 16 * 16
    force_rows = (3 * tiles + 15) // 16 * 16
    node_array = jax.ShapeDtypeStruct((3 * nodes_all // lanes, lanes), f32)
    mass_array = jax.ShapeDtypeStruct((nodes_all // lanes, lanes), f32)
    coords = coords.reshape(node_array.shape)
    disp = disp.reshape(node_array.shape)
    mass = mass.reshape(mass_array.shape)
    shared_lo = shared_lo.reshape(-1, lanes)
    shared_hi = shared_hi.reshape(-1, lanes)
    share = jax.ShapeDtypeStruct((4 * shared_lo.shape[0], lanes), f32)

    outgoing = call(
        functools.partial(pack_kernel, cap),
        jax.ShapeDtypeStruct((parts, rows, lanes), bf16),
        [hbm] * 5,
        vmem,
        [
            pltpu.VMEM((nblk // cap, rows, lanes), f32),
            pltpu.SMEM(block_region.shape, jnp.int32),
            pltpu.SMEM(tile_slot.shape, jnp.int32),
            pltpu.VMEM(coords.shape, f32),
            pltpu.VMEM(disp.shape, f32),
            pltpu.VMEM(surf_nodes.shape, jnp.int32),
            pltpu.SemaphoreType.DMA((5,)),
        ],
        1 << 30,
        60,
    )(block_region, tile_slot, coords, disp, surf_nodes)
    arrived = lax.all_to_all(outgoing, "dom", split_axis=0, concat_axis=0, tiled=True)

    part, faces, starts = call(
        functools.partial(element_kernel, cap, rows),
        (
            node_array,
            jax.ShapeDtypeStruct((2, 3 * tiles, lanes), f32),
            jax.ShapeDtypeStruct((1, tiles), jnp.int32),
        ),
        [smem] * 2 + [vmem] * 6,
        (vmem, vmem, smem),
        [
            pltpu.VMEM((24, modulus.shape[1]), f32),
            pltpu.VMEM((3 * nodes_all // wide, wide), f32),
        ],
        1 << 32,
    )(
        tile_slot,
        tile_face,
        jnp.swapaxes(face_pos, 1, 2),
        jnp.swapaxes(face_normal, 1, 2),
        disp,
        stiffness,
        modulus,
        elem_nodes,
    )

    forces, slots = call(
        functools.partial(tile_kernel, cap),
        (
            jax.ShapeDtypeStruct((parts, force_rows, lanes), bf16),
            jax.ShapeDtypeStruct((parts, lanes), jnp.int32),
        ),
        [smem] + [vmem] * 3,
        (vmem, vmem),
        [pltpu.VMEM((parts * rows, lanes), f32)],
        1 << 28,
    )(starts, arrived, faces, tile_weight)
    back = lax.all_to_all(forces, "dom", split_axis=0, concat_axis=0, tiled=True)
    both_array = jax.ShapeDtypeStruct((2 * shared_lo.shape[0], lanes), jnp.int32)
    picks, both = call(
        functools.partial(list_kernel, cap, tiles, force_rows),
        (jax.ShapeDtypeStruct((2, parts * tiles + 16), jnp.int32), both_array),
        [smem, smem, vmem, vmem],
        (smem, vmem),
        [pltpu.SMEM((parts,), jnp.int32)],
        1 << 24,
    )(slots, block_region, shared_lo, shared_hi)

    part = call(
        functools.partial(contact_kernel, tiles),
        node_array,
        [smem] + [vmem] * 3,
        vmem,
        [pltpu.VMEM((parts * force_rows, lanes), f32)],
        1 << 28,
    )(picks, back, surf_nodes, part)
    pair, first, second = call(
        pair_kernel, (node_array, share, share), [vmem] * 4, (vmem, vmem, vmem), [], 1 << 28
    )(part, from_mate(part, 1), mass, both)
    own, own_mass = call(
        share_kernel, (node_array, mass_array), [vmem] * 5, (vmem, vmem), [], 1 << 28
    )(pair, mass, swapped(first, 0), swapped(second, 1), both)
    distance = 2
    while 2 * distance < mates:
        own = own + from_mate(own, distance)
        distance *= 2
    accel = call(accel_kernel, node_array, [vmem] * 3, vmem, [], 1 << 24)(
        own_mass, own, from_mate(own, distance)
    )
    return accel.reshape(1, 3, nodes_all)


def solution(mesh):
    in_specs = (
        P("dom", None, None),
        P("dom", None, None),
        P("dom", None),
        P(),
        P("dom", None, "rep"),
        P("dom", "rep"),
        P("dom", None, None),
        P("dom", None),
        P("dom", None, None, None),
        P("dom", None, None, None),
        P("dom", "rep"),
        P("dom", "rep"),
        P("dom", "rep", None, None),
        P("dom", None),
        P("dom", None),
    )
    out_specs = P("dom", None, None)
    return jax.shard_map(
        on_device, mesh=mesh, in_specs=in_specs, out_specs=out_specs, check_vma=False
    )
```

```python
import functools

import jax
import jax.numpy as jnp
from jax import lax
from jax.experimental import pallas as pl
from jax.experimental.pallas import tpu as pltpu
from jax.sharding import PartitionSpec as P

penalty = 4.0
lanes = 128
wide = 256
vmem = pl.BlockSpec(memory_space=pltpu.VMEM)
smem = pl.BlockSpec(memory_space=pltpu.SMEM)
hbm = pl.BlockSpec(memory_space=pltpu.HBM)
f32 = jnp.float32
bf16 = jnp.bfloat16


def call(body, out_shape, in_specs, out_specs, scratch, flops, vmem_mib=32):
    return pl.pallas_call(
        body,
        out_shape=out_shape,
        in_specs=in_specs,
        out_specs=out_specs,
        scratch_shapes=scratch,
        compiler_params=pltpu.CompilerParams(vmem_limit_bytes=vmem_mib * 1024 * 1024),
        cost_estimate=pl.CostEstimate(flops=flops, bytes_accessed=1 << 20, transcendentals=0),
    )


def one_hot(nodes):
    line = lax.broadcasted_iota(jnp.int32, (wide, lanes), 0).astype(f32).astype(bf16)
    low = [(row & (wide - 1)).astype(f32).astype(bf16) for row in nodes]
    one, zero = jnp.ones((), bf16), jnp.zeros((), bf16)
    return jnp.concatenate([jnp.where(line == row, one, zero) for row in low], axis=1)


def halves(ref, c, tops):
    at = c * 2 * tops
    return jnp.concatenate(
        [ref[pl.ds(at, tops, stride=2)], ref[pl.ds(at + 1, tops, stride=2)]], axis=1
    )


def two_parts(x):
    coarse = x.astype(bf16)
    return [coarse, (x - coarse.astype(f32)).astype(bf16)]


def lookup(tables, nodes):
    tops = tables[0][0].shape[0]
    stacked = jnp.concatenate([part for table in tables for part in table], axis=0)
    found = jnp.dot(stacked, one_hot(nodes), preferred_element_type=f32)
    line = lax.broadcasted_iota(jnp.int32, (tops, lanes), 0)
    values = [[] for _ in tables]
    for i, row in enumerate(nodes):
        match = line == (row >> 8)
        at = 0
        for c, table in enumerate(tables):
            here = found[at : at + tops, i * lanes : (i + 1) * lanes]
            for p in range(1, len(table)):
                here += found[at + p * tops : at + (p + 1) * tops, i * lanes : (i + 1) * lanes]
            at += len(table) * tops
            values[c].append(jnp.sum(jnp.where(match, here, 0.0), axis=0, keepdims=True))
    return values


def node_sums(nodes, values, tops, parts=2):
    line = lax.broadcasted_iota(jnp.int32, (tops, lanes), 0)
    comps = len(values)
    left = []
    for i, row in enumerate(nodes):
        match = line == (row >> 8)
        pieces = [v[i] for v in values]
        if parts == 2:
            coarse = [v.astype(bf16).astype(f32) for v in pieces]
            pieces = coarse + [v - w for v, w in zip(pieces, coarse)]
        left.append(
            jnp.concatenate([jnp.where(match, v, 0.0).astype(bf16) for v in pieces], axis=0)
        )
    both = lax.dot_general(
        jnp.concatenate(left, axis=1),
        one_hot(nodes),
        (((1,), (1,)), ((), ())),
        preferred_element_type=f32,
    )
    return both if parts == 1 else both[: comps * tops] + both[comps * tops :]


def add_halves(ref, sums, c, tops, row=None):
    at = (c if row is None else row) * 2 * tops
    for half in range(2):
        ref[pl.ds(at + half, tops, stride=2)] += sums[
            c * tops : (c + 1) * tops, half * lanes : (half + 1) * lanes
        ]


def pack_kernel(
    cap, region_hbm, slot_hbm, coords_hbm, disp_hbm, surf_hbm, out_ref,
    stage, region_ref, slot_ref, coords_ref, disp_ref, surf_ref, sems,
):
    sources = (coords_hbm, disp_hbm, slot_hbm, surf_hbm, region_hbm)
    places = (coords_ref, disp_ref, slot_ref, surf_ref, region_ref)
    copies = [
        pltpu.make_async_copy(a, b, sems.at[i]) for i, (a, b) in enumerate(zip(sources, places))
    ]
    for copy in copies:
        copy.start()
    parts, rows, _ = out_ref.shape
    nblk = surf_ref.shape[1]
    runs = nblk // cap
    half = cap // 2
    offset = lax.rem(lax.axis_index("rep"), 2) * half
    tiles = slot_ref.shape[1]
    tops = coords_ref.shape[0] // 6
    for copy in copies:
        copy.wait()
    rest = (rows - 3 * half, lanes)
    lane = lax.broadcasted_iota(jnp.int32, rest, 1)
    line = lax.broadcasted_iota(jnp.int32, rest, 0)
    tail = jnp.zeros(rest, f32)
    for t in range(tiles):
        tail = jnp.where((lane == t) & (line == 0), slot_ref[0, t].astype(f32), tail)
    for q in range(runs):
        stage[q, 3 * half :] = tail
    empty = jnp.concatenate([jnp.zeros((3 * half, lanes), f32), tail], axis=0).astype(bf16)
    for j in range(parts):
        out_ref[j] = empty
    tables = [
        [(halves(coords_ref, c, tops) + halves(disp_ref, c, tops)).astype(bf16)] for c in range(3)
    ]
    size = min(half, 8)
    for first in range(0, runs * half, 8):
        picks = range(first, first + 8)
        values = lookup(
            tables, [surf_ref[0, pl.ds(offset + (n // half) * cap + n % half, 1)] for n in picks]
        )
        for n in range(first, first + 8, size):
            for c in range(3):
                at = c * half + n % half
                stage[n // half, at : at + size] = jnp.concatenate(
                    values[c][n - first : n - first + size], axis=0
                )
    for q in range(runs):
        out_ref[region_ref[0, q * cap]] = stage[q].astype(bf16)


def element_kernel(
    cap, rows, parts, slot_ref, face_ref, pos_ref, normal_ref, disp_ref, stiff_ref, modulus_ref, nodes_ref,
    out_ref, faces_ref, starts_ref, local, sums,
):
    tiles = slot_ref.shape[1]
    for t in range(tiles):
        source, k = slot_ref[0, t] // cap, slot_ref[0, t] % cap
        starts_ref[0, t] = ((k // (cap // 2)) * parts + source) * rows + k % (cap // 2)
        for c in range(3):
            at = c * tiles + t
            faces_ref[0, at : at + 1] = pos_ref[0, c, pl.ds(face_ref[0, t], 1)]
            faces_ref[1, at : at + 1] = normal_ref[0, c, pl.ds(face_ref[0, t], 1)]
    corners, count = nodes_ref.shape[1:]
    tops = disp_ref.shape[0] // 6
    tables = [two_parts(halves(disp_ref, c, tops)) for c in range(3)]
    cuts = [slice(g * lanes, (g + 1) * lanes) for g in range(count // lanes)]
    nodes = [[nodes_ref[0, a : a + 1, cut] for a in range(corners)] for cut in cuts]
    for cut, here in zip(cuts, nodes):
        values = lookup(tables, here)
        for c in range(3):
            local[c * corners : (c + 1) * corners, cut] = jnp.concatenate(values[c], axis=0)
    force = jnp.dot(
        stiff_ref[...], local[...], precision=lax.Precision.HIGHEST, preferred_element_type=f32
    )
    local[...] = -(force * modulus_ref[...])
    for g, (cut, here) in enumerate(zip(cuts, nodes)):
        values = [
            [local[c * corners + a : c * corners + a + 1, cut] for a in range(corners)]
            for c in range(3)
        ]
        added = node_sums(here, values, tops)
        sums[...] = added if g == 0 else sums[...] + added
    out_ref[...] = jnp.zeros_like(out_ref)
    for c in range(3):
        add_halves(out_ref, sums[...], c, tops)


def tile_kernel(cap, starts_ref, got_ref, other_ref, faces_ref, weight_ref, out_ref, slots_ref, flat):
    parts, rows, _ = got_ref.shape
    half = cap // 2
    tiles = starts_ref.shape[1]
    core = lax.rem(lax.axis_index("rep"), 2)
    for ref, which in ((got_ref, core), (other_ref, 1 - core)):
        for j in range(parts):
            at = pl.multiple_of((which * parts + j) * rows, 8)
            flat[pl.ds(at, rows)] = ref[j].astype(f32)
    slots_ref[...] = jnp.concatenate(
        [flat[pl.ds((core * parts + j) * rows + 3 * half, 1)] for j in range(parts)], axis=0
    ).astype(jnp.int32)
    x = jnp.concatenate(
        [flat[pl.ds(starts_ref[0, t] + c * half, 1)] for c in range(3) for t in range(tiles)], axis=0
    )
    weights = weight_ref[0].reshape(tiles * lanes, lanes)
    crossed = lax.dot_general(
        x.astype(bf16), weights, (((1,), (1,)), ((), ())), preferred_element_type=f32
    )
    line = lax.broadcasted_iota(jnp.int32, (tiles, lanes), 0)
    gap = jnp.zeros((tiles, lanes), f32)
    normals = []
    for c in range(3):
        interp = jnp.zeros((tiles, lanes), f32)
        for t in range(tiles):
            here = crossed[c * tiles : (c + 1) * tiles, t * lanes : (t + 1) * lanes]
            interp = jnp.where(line == t, here, interp)
        normal = faces_ref[1, c * tiles : (c + 1) * tiles]
        gap += normal * (interp - faces_ref[0, c * tiles : (c + 1) * tiles])
        normals.append(normal)
    pressure = penalty * jnp.maximum(-gap, 0.0)
    push = [pressure * normal for normal in normals]
    spread = jnp.concatenate(
        [
            jnp.concatenate([jnp.where(line == t, p, 0.0) for p in push], axis=0).astype(bf16)
            for t in range(tiles)
        ],
        axis=1,
    )
    forces = jnp.dot(spread, weights, preferred_element_type=f32).astype(bf16)
    pad = out_ref.shape[0] - forces.shape[0]
    if pad:
        forces = jnp.concatenate([forces, jnp.zeros((pad, lanes), bf16)], axis=0)
    out_ref[...] = forces


def list_kernel(cap, tiles, force_rows, slots_ref, region_ref, lo_ref, hi_ref, list_ref, both_ref, run_of):
    shared = lo_ref.shape[0]
    both_ref[:shared] = lo_ref[...]
    both_ref[shared:] = hi_ref[...]
    parts = slots_ref.shape[0]
    nblk = region_ref.shape[1]
    me = lax.axis_index("dom")
    for q in range(nblk // cap):
        run_of[region_ref[0, q * cap]] = q * cap

    bits = (parts - 1).bit_length()

    def pick(place, filled):
        j = me
        for bit in range(bits):
            j = j ^ (((place >> bit) & 1) << (bits - 1 - bit))
        run = run_of[j]
        slots = [slots_ref[j, t] for t in range(tiles)]
        mine = [slot // cap == me for slot in slots]
        blocks = [jnp.where(own, run + slot % cap, 0) for own, slot in zip(mine, slots)]
        places = []
        for own in mine:
            places.append(filled)
            filled = filled + jnp.where(own, 1, 0)
        for t in range(tiles):
            list_ref[0, places[t]] = place * force_rows + t
            list_ref[1, places[t]] = blocks[t]
        return filled

    filled = lax.fori_loop(0, parts, pick, 0)
    for i in range(8):
        list_ref[0, filled + i] = 0
        list_ref[1, filled + i] = 0
    list_ref[0, list_ref.shape[1] - 1] = filled


def contact_kernel(tiles, list_ref, held_ref, got_ref, surf_ref, part_ref, out_ref, back):
    size = held_ref.shape[0]
    tops = part_ref.shape[0] // 6
    out_ref[...] = part_ref[...]
    back[:size] = held_ref[...].astype(f32)
    back[size:] = got_ref[...].astype(f32)
    filled = list_ref[0, list_ref.shape[1] - 1]

    def spread(g, _):
        nodes, values = [], [[], [], []]
        for i in range(8):
            row = surf_ref[0, pl.ds(list_ref[1, g * 8 + i], 1)]
            nodes.append(jnp.where(g * 8 + i < filled, row, -1))
            for c in range(3):
                values[c].append(back[pl.ds(list_ref[0, g * 8 + i] + c * tiles, 1)])
        sums = node_sums(nodes, values, tops, 1)
        for c in range(3):
            add_halves(out_ref, sums, c, tops)
        return 0

    lax.fori_loop(0, (filled + 7) // 8, spread, 0)


def pair_kernel(part_ref, other_ref, mass_ref, both_ref, out_ref, first_ref, second_ref):
    even = lax.axis_index("dom") % 2 == 0
    tops = mass_ref.shape[0] // 2
    out_ref[...] = part_ref[...] + other_ref[...]
    count = both_ref.shape[0]
    shared = count // 2
    tables = [two_parts(halves(out_ref, c, tops)) for c in range(3)]
    tables.append(two_parts(halves(mass_ref, 0, tops)))
    values = lookup(tables, [both_ref[k : k + 1] for k in range(count)])
    for c in range(4):
        lower = jnp.concatenate(values[c][:shared], axis=0)
        upper = jnp.concatenate(values[c][shared:], axis=0)
        first_ref[c * shared : (c + 1) * shared] = jnp.where(even, upper, lower)
        second_ref[c * shared : (c + 1) * shared] = jnp.where(even, lower, upper)


def share_kernel(part_ref, mass_ref, first_ref, second_ref, both_ref, out_ref, out_mass_ref):
    even = lax.axis_index("dom") % 2 == 0
    tops = mass_ref.shape[0] // 2
    out_ref[...] = part_ref[...]
    out_mass_ref[...] = mass_ref[...]
    first, second = first_ref[...], second_ref[...]
    lower = jnp.where(even, second, first)
    upper = jnp.where(even, first, second)
    count = both_ref.shape[0]
    shared = count // 2
    nodes = [both_ref[k : k + 1] for k in range(count)]
    values = [
        [pack[c * shared + k : c * shared + k + 1] for pack in (lower, upper) for k in range(shared)]
        for c in range(4)
    ]
    sums = node_sums(nodes, values, tops)
    for c in range(3):
        add_halves(out_ref, sums, c, tops)
    add_halves(out_mass_ref, sums, 3, tops, 0)


def accel_kernel(mass_ref, own_ref, other_ref, out_ref):
    total = own_ref[...] + other_ref[...]
    size = mass_ref.shape[0]
    for c in range(3):
        at = slice(c * size, (c + 1) * size)
        out_ref[at] = total[at] / mass_ref[...]


def swapped(block, start):
    lows = range(start, lax.axis_size("dom") - 1, 2)
    return lax.ppermute(block, "dom", [(s, s + 1) for s in lows] + [(s + 1, s) for s in lows])


def from_mate(block, distance):
    return lax.ppermute(
        block, "rep", [(i, i ^ distance) for i in range(lax.axis_size("rep"))]
    )


def across(block, distance):
    return lax.ppermute(
        block, "dom", [(s, s ^ distance) for s in range(lax.axis_size("dom"))]
    )


def on_device(
    coords,
    disp,
    mass,
    stiffness,
    elem_nodes,
    modulus,
    surf_nodes,
    block_region,
    face_pos,
    face_normal,
    tile_slot,
    tile_face,
    tile_weight,
    shared_lo,
    shared_hi,
):
    parts = lax.axis_size("dom")
    mates = lax.axis_size("rep")
    nodes_all = disp.shape[2]
    nblk = surf_nodes.shape[1]
    tiles = tile_slot.shape[1]
    cap = max(2, 2 * nblk // parts)
    rows = (3 * (cap // 2) + 1 + 15) // 16 * 16
    force_rows = (3 * tiles + 15) // 16 * 16
    node_array = jax.ShapeDtypeStruct((3 * nodes_all // lanes, lanes), f32)
    mass_array = jax.ShapeDtypeStruct((nodes_all // lanes, lanes), f32)
    coords = coords.reshape(node_array.shape)
    disp = disp.reshape(node_array.shape)
    mass = mass.reshape(mass_array.shape)
    shared_lo = shared_lo.reshape(-1, lanes)
    shared_hi = shared_hi.reshape(-1, lanes)
    share = jax.ShapeDtypeStruct((4 * shared_lo.shape[0], lanes), f32)

    outgoing = call(
        functools.partial(pack_kernel, cap),
        jax.ShapeDtypeStruct((parts, rows, lanes), bf16),
        [hbm] * 5,
        vmem,
        [
            pltpu.VMEM((nblk // cap, rows, lanes), f32),
            pltpu.SMEM(block_region.shape, jnp.int32),
            pltpu.SMEM(tile_slot.shape, jnp.int32),
            pltpu.VMEM(coords.shape, f32),
            pltpu.VMEM(disp.shape, f32),
            pltpu.VMEM(surf_nodes.shape, jnp.int32),
            pltpu.SemaphoreType.DMA((5,)),
        ],
        1 << 30,
        60,
    )(block_region, tile_slot, coords, disp, surf_nodes)
    arrived = lax.all_to_all(outgoing, "dom", split_axis=0, concat_axis=0, tiled=True)

    part, faces, starts = call(
        functools.partial(element_kernel, cap, rows, parts),
        (
            node_array,
            jax.ShapeDtypeStruct((2, 3 * tiles, lanes), f32),
            jax.ShapeDtypeStruct((1, tiles), jnp.int32),
        ),
        [smem] * 2 + [vmem] * 6,
        (vmem, vmem, smem),
        [
            pltpu.VMEM((24, modulus.shape[1]), f32),
            pltpu.VMEM((3 * nodes_all // wide, wide), f32),
        ],
        1 << 32,
    )(
        tile_slot,
        tile_face,
        jnp.swapaxes(face_pos, 1, 2),
        jnp.swapaxes(face_normal, 1, 2),
        disp,
        stiffness,
        modulus,
        elem_nodes,
    )

    forces, slots = call(
        functools.partial(tile_kernel, cap),
        (
            jax.ShapeDtypeStruct((force_rows, lanes), bf16),
            jax.ShapeDtypeStruct((parts, lanes), jnp.int32),
        ),
        [smem] + [vmem] * 4,
        (vmem, vmem),
        [pltpu.VMEM((2 * parts * rows, lanes), f32)],
        1 << 28,
    )(starts, arrived, from_mate(arrived, 1), faces, tile_weight)
    held, distance = forces, parts // 2
    while distance > 1:
        held = jnp.concatenate([held, across(held, distance)], axis=0)
        distance //= 2
    got = across(held, 1)
    both_array = jax.ShapeDtypeStruct((2 * shared_lo.shape[0], lanes), jnp.int32)
    picks, both = call(
        functools.partial(list_kernel, cap, tiles, force_rows),
        (jax.ShapeDtypeStruct((2, parts * tiles + 16), jnp.int32), both_array),
        [smem, smem, vmem, vmem],
        (smem, vmem),
        [pltpu.SMEM((parts,), jnp.int32)],
        1 << 24,
    )(slots, block_region, shared_lo, shared_hi)

    part = call(
        functools.partial(contact_kernel, tiles),
        node_array,
        [smem] + [vmem] * 4,
        vmem,
        [pltpu.VMEM((parts * force_rows, lanes), f32)],
        1 << 28,
    )(picks, held, got, surf_nodes, part)
    pair, first, second = call(
        pair_kernel, (node_array, share, share), [vmem] * 4, (vmem, vmem, vmem), [], 1 << 28
    )(part, from_mate(part, 1), mass, both)
    own, own_mass = call(
        share_kernel, (node_array, mass_array), [vmem] * 5, (vmem, vmem), [], 1 << 28
    )(pair, mass, swapped(first, 0), swapped(second, 1), both)
    distance = 2
    while 2 * distance < mates:
        own = own + from_mate(own, distance)
        distance *= 2
    accel = call(accel_kernel, node_array, [vmem] * 3, vmem, [], 1 << 24)(
        own_mass, own, from_mate(own, distance)
    )
    return accel.reshape(1, 3, nodes_all)


def solution(mesh):
    in_specs = (
        P("dom", None, None),
        P("dom", None, None),
        P("dom", None),
        P(),
        P("dom", None, "rep"),
        P("dom", "rep"),
        P("dom", None, None),
        P("dom", None),
        P("dom", None, None, None),
        P("dom", None, None, None),
        P("dom", "rep"),
        P("dom", "rep"),
        P("dom", "rep", None, None),
        P("dom", None),
        P("dom", None),
    )
    out_specs = P("dom", None, None)
    return jax.shard_map(
        on_device, mesh=mesh, in_specs=in_specs, out_specs=out_specs, check_vma=False
    )
```

```python
import functools

import jax
import jax.numpy as jnp
from jax import lax
from jax.experimental import pallas as pl
from jax.experimental.pallas import tpu as pltpu
from jax.sharding import PartitionSpec as P

penalty = 4.0
lanes = 128
wide = 256
vmem = pl.BlockSpec(memory_space=pltpu.VMEM)
smem = pl.BlockSpec(memory_space=pltpu.SMEM)
hbm = pl.BlockSpec(memory_space=pltpu.HBM)
f32 = jnp.float32
bf16 = jnp.bfloat16


def call(body, out_shape, in_specs, out_specs, scratch, flops, vmem_mib=32):
    return pl.pallas_call(
        body,
        out_shape=out_shape,
        in_specs=in_specs,
        out_specs=out_specs,
        scratch_shapes=scratch,
        compiler_params=pltpu.CompilerParams(vmem_limit_bytes=vmem_mib * 1024 * 1024),
        cost_estimate=pl.CostEstimate(flops=flops, bytes_accessed=1 << 20, transcendentals=0),
    )


def one_hot(nodes):
    line = lax.broadcasted_iota(jnp.int32, (wide, lanes), 0).astype(f32).astype(bf16)
    low = [(row & (wide - 1)).astype(f32).astype(bf16) for row in nodes]
    one, zero = jnp.ones((), bf16), jnp.zeros((), bf16)
    return jnp.concatenate([jnp.where(line == row, one, zero) for row in low], axis=1)


def halves(ref, c, tops):
    at = c * 2 * tops
    return jnp.concatenate(
        [ref[pl.ds(at, tops, stride=2)], ref[pl.ds(at + 1, tops, stride=2)]], axis=1
    )


def two_parts(x):
    coarse = x.astype(bf16)
    return [coarse, (x - coarse.astype(f32)).astype(bf16)]


def lookup(tables, nodes):
    tops = tables[0][0].shape[0]
    stacked = jnp.concatenate([part for table in tables for part in table], axis=0)
    found = jnp.dot(stacked, one_hot(nodes), preferred_element_type=f32)
    line = lax.broadcasted_iota(jnp.int32, (tops, lanes), 0)
    values = [[] for _ in tables]
    for i, row in enumerate(nodes):
        match = line == (row >> 8)
        at = 0
        for c, table in enumerate(tables):
            here = found[at : at + tops, i * lanes : (i + 1) * lanes]
            for p in range(1, len(table)):
                here += found[at + p * tops : at + (p + 1) * tops, i * lanes : (i + 1) * lanes]
            at += len(table) * tops
            values[c].append(jnp.sum(jnp.where(match, here, 0.0), axis=0, keepdims=True))
    return values


def node_sums(nodes, values, tops, parts=2):
    line = lax.broadcasted_iota(jnp.int32, (tops, lanes), 0)
    comps = len(values)
    left = []
    for i, row in enumerate(nodes):
        match = line == (row >> 8)
        pieces = [v[i] for v in values]
        if parts == 2:
            coarse = [v.astype(bf16).astype(f32) for v in pieces]
            pieces = coarse + [v - w for v, w in zip(pieces, coarse)]
        left.append(
            jnp.concatenate([jnp.where(match, v, 0.0).astype(bf16) for v in pieces], axis=0)
        )
    both = lax.dot_general(
        jnp.concatenate(left, axis=1),
        one_hot(nodes),
        (((1,), (1,)), ((), ())),
        preferred_element_type=f32,
    )
    return both if parts == 1 else both[: comps * tops] + both[comps * tops :]


def add_halves(ref, sums, c, tops, row=None):
    at = (c if row is None else row) * 2 * tops
    for half in range(2):
        ref[pl.ds(at + half, tops, stride=2)] += sums[
            c * tops : (c + 1) * tops, half * lanes : (half + 1) * lanes
        ]


def pack_kernel(
    cap, region_hbm, slot_hbm, coords_hbm, disp_hbm, surf_hbm, out_ref,
    stage, region_ref, slot_ref, coords_ref, disp_ref, surf_ref, sems,
):
    sources = (coords_hbm, disp_hbm, slot_hbm, surf_hbm, region_hbm)
    places = (coords_ref, disp_ref, slot_ref, surf_ref, region_ref)
    copies = [
        pltpu.make_async_copy(a, b, sems.at[i]) for i, (a, b) in enumerate(zip(sources, places))
    ]
    for copy in copies:
        copy.start()
    parts, rows, _ = out_ref.shape
    nblk = surf_ref.shape[1]
    tiles = slot_ref.shape[1]
    tops = coords_ref.shape[0] // 6
    for copy in copies:
        copy.wait()
    rest = (rows - 3 * cap, lanes)
    lane = lax.broadcasted_iota(jnp.int32, rest, 1)
    line = lax.broadcasted_iota(jnp.int32, rest, 0)
    tail = jnp.zeros(rest, f32)
    for t in range(tiles):
        tail = jnp.where((lane == t) & (line == 0), slot_ref[0, t].astype(f32), tail)
    for q in range(nblk // cap):
        stage[q, 3 * cap :] = tail
    empty = jnp.concatenate([jnp.zeros((3 * cap, lanes), f32), tail], axis=0).astype(bf16)
    for j in range(parts):
        out_ref[j] = empty
    tables = [
        [(halves(coords_ref, c, tops) + halves(disp_ref, c, tops)).astype(bf16)] for c in range(3)
    ]
    size = min(cap, 8)
    for first in range(0, nblk, 8):
        values = lookup(tables, [surf_ref[0, first + i : first + i + 1] for i in range(8)])
        for b in range(first, first + 8, size):
            for c in range(3):
                at = c * cap + b % cap
                stage[b // cap, at : at + size] = jnp.concatenate(
                    values[c][b - first : b - first + size], axis=0
                )
    for q in range(nblk // cap):
        out_ref[region_ref[0, q * cap]] = stage[q].astype(bf16)


def element_kernel(
    cap, rows, slot_ref, face_ref, pos_ref, normal_ref, disp_ref, stiff_ref, modulus_ref, nodes_ref,
    out_ref, faces_ref, starts_ref, local, sums,
):
    tiles = slot_ref.shape[1]
    for t in range(tiles):
        starts_ref[0, t] = (slot_ref[0, t] // cap) * rows + slot_ref[0, t] % cap
        for c in range(3):
            at = c * tiles + t
            faces_ref[0, at : at + 1] = pos_ref[0, c, pl.ds(face_ref[0, t], 1)]
            faces_ref[1, at : at + 1] = normal_ref[0, c, pl.ds(face_ref[0, t], 1)]
    corners, count = nodes_ref.shape[1:]
    tops = disp_ref.shape[0] // 6
    tables = [two_parts(halves(disp_ref, c, tops)) for c in range(3)]
    cuts = [slice(g * lanes, (g + 1) * lanes) for g in range(count // lanes)]
    nodes = [[nodes_ref[0, a : a + 1, cut] for a in range(corners)] for cut in cuts]
    for cut, here in zip(cuts, nodes):
        values = lookup(tables, here)
        for c in range(3):
            local[c * corners : (c + 1) * corners, cut] = jnp.concatenate(values[c], axis=0)
    force = jnp.dot(
        stiff_ref[...], local[...], precision=lax.Precision.HIGHEST, preferred_element_type=f32
    )
    local[...] = -(force * modulus_ref[...])
    for g, (cut, here) in enumerate(zip(cuts, nodes)):
        values = [
            [local[c * corners + a : c * corners + a + 1, cut] for a in range(corners)]
            for c in range(3)
        ]
        added = node_sums(here, values, tops)
        sums[...] = added if g == 0 else sums[...] + added
    out_ref[...] = jnp.zeros_like(out_ref)
    for c in range(3):
        add_halves(out_ref, sums[...], c, tops)


def tile_kernel(cap, starts_ref, got_ref, faces_ref, weight_ref, out_ref, slots_ref, flat):
    parts, rows, _ = got_ref.shape
    tiles = starts_ref.shape[1]
    for j in range(parts):
        flat[j * rows : (j + 1) * rows] = got_ref[j].astype(f32)
    slots_ref[...] = jnp.concatenate(
        [flat[j * rows + 3 * cap : j * rows + 3 * cap + 1] for j in range(parts)], axis=0
    ).astype(jnp.int32)
    x = jnp.concatenate(
        [flat[pl.ds(starts_ref[0, t] + c * cap, 1)] for c in range(3) for t in range(tiles)], axis=0
    )
    weights = weight_ref[0].reshape(tiles * lanes, lanes)
    crossed = lax.dot_general(
        x.astype(bf16), weights, (((1,), (1,)), ((), ())), preferred_element_type=f32
    )
    line = lax.broadcasted_iota(jnp.int32, (tiles, lanes), 0)
    gap = jnp.zeros((tiles, lanes), f32)
    normals = []
    for c in range(3):
        interp = jnp.zeros((tiles, lanes), f32)
        for t in range(tiles):
            here = crossed[c * tiles : (c + 1) * tiles, t * lanes : (t + 1) * lanes]
            interp = jnp.where(line == t, here, interp)
        normal = faces_ref[1, c * tiles : (c + 1) * tiles]
        gap += normal * (interp - faces_ref[0, c * tiles : (c + 1) * tiles])
        normals.append(normal)
    pressure = penalty * jnp.maximum(-gap, 0.0)
    push = [pressure * normal for normal in normals]
    spread = jnp.concatenate(
        [
            jnp.concatenate([jnp.where(line == t, p, 0.0) for p in push], axis=0).astype(bf16)
            for t in range(tiles)
        ],
        axis=1,
    )
    forces = jnp.dot(spread, weights, preferred_element_type=f32).astype(bf16)
    pad = out_ref.shape[0] - forces.shape[0]
    if pad:
        forces = jnp.concatenate([forces, jnp.zeros((pad, lanes), bf16)], axis=0)
    out_ref[...] = forces


def list_kernel(cap, tiles, force_rows, slots_ref, region_ref, lo_ref, hi_ref, list_ref, both_ref, run_of):
    shared = lo_ref.shape[0]
    both_ref[:shared] = lo_ref[...]
    both_ref[shared:] = hi_ref[...]
    parts = slots_ref.shape[0]
    nblk = region_ref.shape[1]
    me = lax.axis_index("dom")
    for q in range(nblk // cap):
        run_of[region_ref[0, q * cap]] = q * cap

    def pick(place, filled):
        j = me ^ place
        run = run_of[j]
        slots = [slots_ref[j, t] for t in range(tiles)]
        mine = [slot // cap == me for slot in slots]
        blocks = [jnp.where(own, run + slot % cap, 0) for own, slot in zip(mine, slots)]
        places = []
        for own in mine:
            places.append(filled)
            filled = filled + jnp.where(own, 1, 0)
        for t in range(tiles):
            list_ref[0, places[t]] = place * force_rows + t
            list_ref[1, places[t]] = blocks[t]
        return filled

    filled = lax.fori_loop(0, parts, pick, 0)
    for i in range(8):
        list_ref[0, filled + i] = 0
        list_ref[1, filled + i] = 0
    list_ref[0, list_ref.shape[1] - 1] = filled


def contact_kernel(tiles, list_ref, surf_ref, part_ref, *refs):
    back_refs, out_ref, back = refs[:-2], refs[-2], refs[-1]
    size = back_refs[0].shape[0]
    tops = part_ref.shape[0] // 6
    out_ref[...] = part_ref[...]
    for i, ref in enumerate(back_refs):
        back[i * size : (i + 1) * size] = ref[...].astype(f32)
    filled = list_ref[0, list_ref.shape[1] - 1]

    def spread(g, _):
        nodes, values = [], [[], [], []]
        for i in range(8):
            row = surf_ref[0, pl.ds(list_ref[1, g * 8 + i], 1)]
            nodes.append(jnp.where(g * 8 + i < filled, row, -1))
            for c in range(3):
                values[c].append(back[pl.ds(list_ref[0, g * 8 + i] + c * tiles, 1)])
        sums = node_sums(nodes, values, tops, 1)
        for c in range(3):
            add_halves(out_ref, sums, c, tops)
        return 0

    lax.fori_loop(0, (filled + 7) // 8, spread, 0)


def pair_kernel(part_ref, other_ref, mass_ref, both_ref, out_ref, first_ref, second_ref):
    even = lax.axis_index("dom") % 2 == 0
    tops = mass_ref.shape[0] // 2
    out_ref[...] = part_ref[...] + other_ref[...]
    count = both_ref.shape[0]
    shared = count // 2
    tables = [two_parts(halves(out_ref, c, tops)) for c in range(3)]
    tables.append(two_parts(halves(mass_ref, 0, tops)))
    values = lookup(tables, [both_ref[k : k + 1] for k in range(count)])
    for c in range(4):
        lower = jnp.concatenate(values[c][:shared], axis=0)
        upper = jnp.concatenate(values[c][shared:], axis=0)
        first_ref[c * shared : (c + 1) * shared] = jnp.where(even, upper, lower)
        second_ref[c * shared : (c + 1) * shared] = jnp.where(even, lower, upper)


def share_kernel(part_ref, mass_ref, first_ref, second_ref, both_ref, out_ref, out_mass_ref, total):
    even = lax.axis_index("dom") % 2 == 0
    tops = mass_ref.shape[0] // 2
    total[...] = part_ref[...]
    out_mass_ref[...] = mass_ref[...]
    first, second = first_ref[...], second_ref[...]
    lower = jnp.where(even, second, first)
    upper = jnp.where(even, first, second)
    count = both_ref.shape[0]
    shared = count // 2
    nodes = [both_ref[k : k + 1] for k in range(count)]
    values = [
        [pack[c * shared + k : c * shared + k + 1] for pack in (lower, upper) for k in range(shared)]
        for c in range(4)
    ]
    sums = node_sums(nodes, values, tops)
    for c in range(3):
        add_halves(total, sums, c, tops)
    add_halves(out_mass_ref, sums, 3, tops, 0)
    out_ref[...] = total[...].astype(bf16)


def accel_kernel(mass_ref, own_ref, other_ref, out_ref):
    total = own_ref[...].astype(f32) + other_ref[...].astype(f32)
    size = mass_ref.shape[0]
    for c in range(3):
        at = slice(c * size, (c + 1) * size)
        out_ref[at] = total[at] / mass_ref[...]


def swapped(block, start):
    lows = range(start, lax.axis_size("dom") - 1, 2)
    return lax.ppermute(block, "dom", [(s, s + 1) for s in lows] + [(s + 1, s) for s in lows])


def from_mate(block, distance):
    return lax.ppermute(
        block, "rep", [(i, i ^ distance) for i in range(lax.axis_size("rep"))]
    )


def across(block, distance):
    return lax.ppermute(
        block, "dom", [(s, s ^ distance) for s in range(lax.axis_size("dom"))]
    )


def on_device(
    coords,
    disp,
    mass,
    stiffness,
    elem_nodes,
    modulus,
    surf_nodes,
    block_region,
    face_pos,
    face_normal,
    tile_slot,
    tile_face,
    tile_weight,
    shared_lo,
    shared_hi,
):
    parts = lax.axis_size("dom")
    assert lax.axis_size("rep") == 4
    nodes_all = disp.shape[2]
    nblk = surf_nodes.shape[1]
    tiles = tile_slot.shape[1]
    cap = max(2, 2 * nblk // parts)
    rows = (3 * cap + 1 + 15) // 16 * 16
    force_rows = (3 * tiles + 15) // 16 * 16
    node_array = jax.ShapeDtypeStruct((3 * nodes_all // lanes, lanes), f32)
    mass_array = jax.ShapeDtypeStruct((nodes_all // lanes, lanes), f32)
    coords = coords.reshape(node_array.shape)
    disp = disp.reshape(node_array.shape)
    mass = mass.reshape(mass_array.shape)
    shared_lo = shared_lo.reshape(-1, lanes)
    shared_hi = shared_hi.reshape(-1, lanes)
    share = jax.ShapeDtypeStruct((4 * shared_lo.shape[0], lanes), f32)

    outgoing = call(
        functools.partial(pack_kernel, cap),
        jax.ShapeDtypeStruct((parts, rows, lanes), bf16),
        [hbm] * 5,
        vmem,
        [
            pltpu.VMEM((nblk // cap, rows, lanes), f32),
            pltpu.SMEM(block_region.shape, jnp.int32),
            pltpu.SMEM(tile_slot.shape, jnp.int32),
            pltpu.VMEM(coords.shape, f32),
            pltpu.VMEM(disp.shape, f32),
            pltpu.VMEM(surf_nodes.shape, jnp.int32),
            pltpu.SemaphoreType.DMA((5,)),
        ],
        1 << 30,
        60,
    )(block_region, tile_slot, coords, disp, surf_nodes)
    arrived = lax.all_to_all(outgoing, "dom", split_axis=0, concat_axis=0, tiled=True)

    part, faces, starts = call(
        functools.partial(element_kernel, cap, rows),
        (
            node_array,
            jax.ShapeDtypeStruct((2, 3 * tiles, lanes), f32),
            jax.ShapeDtypeStruct((1, tiles), jnp.int32),
        ),
        [smem] * 2 + [vmem] * 6,
        (vmem, vmem, smem),
        [
            pltpu.VMEM((24, modulus.shape[1]), f32),
            pltpu.VMEM((3 * nodes_all // wide, wide), f32),
        ],
        1 << 32,
    )(
        tile_slot,
        tile_face,
        jnp.swapaxes(face_pos, 1, 2),
        jnp.swapaxes(face_normal, 1, 2),
        disp,
        stiffness,
        modulus,
        elem_nodes,
    )

    forces, slots = call(
        functools.partial(tile_kernel, cap),
        (
            jax.ShapeDtypeStruct((force_rows, lanes), bf16),
            jax.ShapeDtypeStruct((parts, lanes), jnp.int32),
        ),
        [smem] + [vmem] * 3,
        (vmem, vmem),
        [pltpu.VMEM((parts * rows, lanes), f32)],
        1 << 28,
    )(starts, arrived, faces, tile_weight)
    held, distance = forces, 1
    while 4 * distance < parts:
        held = jnp.concatenate([held, across(held, distance)], axis=0)
        distance *= 2
    back = [held] + [across(held, d) for d in range(distance, parts, distance)]
    both_array = jax.ShapeDtypeStruct((2 * shared_lo.shape[0], lanes), jnp.int32)
    picks, both = call(
        functools.partial(list_kernel, cap, tiles, force_rows),
        (jax.ShapeDtypeStruct((2, parts * tiles + 16), jnp.int32), both_array),
        [smem, smem, vmem, vmem],
        (smem, vmem),
        [pltpu.SMEM((parts,), jnp.int32)],
        1 << 24,
    )(slots, block_region, shared_lo, shared_hi)

    part = call(
        functools.partial(contact_kernel, tiles),
        node_array,
        [smem] + [vmem] * (2 + len(back)),
        vmem,
        [pltpu.VMEM((parts * force_rows, lanes), f32)],
        1 << 28,
    )(picks, surf_nodes, part, *back)
    pair, first, second = call(
        pair_kernel, (node_array, share, share), [vmem] * 4, (vmem, vmem, vmem), [], 1 << 28
    )(part, from_mate(part, 1), mass, both)
    second = swapped(second, 1)
    first = swapped(first, 0)
    own, own_mass = call(
        share_kernel,
        (jax.ShapeDtypeStruct(node_array.shape, bf16), mass_array),
        [vmem] * 5,
        (vmem, vmem),
        [pltpu.VMEM(node_array.shape, f32)],
        1 << 28,
    )(pair, mass, first, second, both)
    accel = call(accel_kernel, node_array, [vmem] * 3, vmem, [], 1 << 24)(
        own_mass, own, from_mate(own, 2)
    )
    return accel.reshape(1, 3, nodes_all)


def solution(mesh):
    in_specs = (
        P("dom", None, None),
        P("dom", None, None),
        P("dom", None),
        P(),
        P("dom", None, "rep"),
        P("dom", "rep"),
        P("dom", None, None),
        P("dom", None),
        P("dom", None, None, None),
        P("dom", None, None, None),
        P("dom", "rep"),
        P("dom", "rep"),
        P("dom", "rep", None, None),
        P("dom", None),
        P("dom", None),
    )
    out_specs = P("dom", None, None)
    return jax.shard_map(
        on_device, mesh=mesh, in_specs=in_specs, out_specs=out_specs, check_vma=False
    )
```

```python
import functools

import jax
import jax.numpy as jnp
from jax import lax
from jax.experimental import pallas as pl
from jax.experimental.pallas import tpu as pltpu
from jax.sharding import PartitionSpec as P

penalty = 4.0
lanes = 128
wide = 256
code_bits = 12
code = 1 << code_bits
vmem = pl.BlockSpec(memory_space=pltpu.VMEM)
smem = pl.BlockSpec(memory_space=pltpu.SMEM)
hbm = pl.BlockSpec(memory_space=pltpu.HBM)
f32 = jnp.float32
bf16 = jnp.bfloat16


def call(body, out_shape, in_specs, out_specs, scratch, flops, vmem_mib=32):
    return pl.pallas_call(
        body,
        out_shape=out_shape,
        in_specs=in_specs,
        out_specs=out_specs,
        scratch_shapes=scratch,
        compiler_params=pltpu.CompilerParams(vmem_limit_bytes=vmem_mib * 1024 * 1024),
        cost_estimate=pl.CostEstimate(flops=flops, bytes_accessed=1 << 20, transcendentals=0),
    )


def one_hot(nodes):
    line = lax.broadcasted_iota(jnp.int32, (wide, lanes), 0).astype(f32).astype(bf16)
    low = [(row & (wide - 1)).astype(f32).astype(bf16) for row in nodes]
    one, zero = jnp.ones((), bf16), jnp.zeros((), bf16)
    return jnp.concatenate([jnp.where(line == row, one, zero) for row in low], axis=1)


def halves(ref, c, tops):
    at = c * 2 * tops
    return jnp.concatenate(
        [ref[pl.ds(at, tops, stride=2)], ref[pl.ds(at + 1, tops, stride=2)]], axis=1
    )


def two_parts(x):
    coarse = x.astype(bf16)
    return [coarse, (x - coarse.astype(f32)).astype(bf16)]


def lookup(tables, nodes):
    tops = tables[0][0].shape[0]
    stacked = jnp.concatenate([part for table in tables for part in table], axis=0)
    found = jnp.dot(stacked, one_hot(nodes), preferred_element_type=f32)
    line = lax.broadcasted_iota(jnp.int32, (tops, lanes), 0)
    values = [[] for _ in tables]
    for i, row in enumerate(nodes):
        match = line == (row >> 8)
        at = 0
        for c, table in enumerate(tables):
            here = found[at : at + tops, i * lanes : (i + 1) * lanes]
            for p in range(1, len(table)):
                here += found[at + p * tops : at + (p + 1) * tops, i * lanes : (i + 1) * lanes]
            at += len(table) * tops
            values[c].append(jnp.sum(jnp.where(match, here, 0.0), axis=0, keepdims=True))
    return values


def node_sums(nodes, values, tops, parts=2):
    line = lax.broadcasted_iota(jnp.int32, (tops, lanes), 0)
    comps = len(values)
    left = []
    for i, row in enumerate(nodes):
        match = line == (row >> 8)
        pieces = [v[i] for v in values]
        if parts == 2:
            coarse = [v.astype(bf16).astype(f32) for v in pieces]
            pieces = coarse + [v - w for v, w in zip(pieces, coarse)]
        left.append(
            jnp.concatenate([jnp.where(match, v, 0.0).astype(bf16) for v in pieces], axis=0)
        )
    both = lax.dot_general(
        jnp.concatenate(left, axis=1),
        one_hot(nodes),
        (((1,), (1,)), ((), ())),
        preferred_element_type=f32,
    )
    return both if parts == 1 else both[: comps * tops] + both[comps * tops :]


def add_halves(ref, sums, c, tops, row=None):
    at = (c if row is None else row) * 2 * tops
    for half in range(2):
        ref[pl.ds(at + half, tops, stride=2)] += sums[
            c * tops : (c + 1) * tops, half * lanes : (half + 1) * lanes
        ]


def pack_kernel(
    cap, region_hbm, slot_hbm, coords_hbm, disp_hbm, surf_hbm, out_ref,
    stage, region_ref, slot_ref, coords_ref, disp_ref, surf_ref, sems,
):
    sources = (coords_hbm, disp_hbm, slot_hbm, surf_hbm, region_hbm)
    places = (coords_ref, disp_ref, slot_ref, surf_ref, region_ref)
    copies = [
        pltpu.make_async_copy(a, b, sems.at[i]) for i, (a, b) in enumerate(zip(sources, places))
    ]
    for copy in copies:
        copy.start()
    parts, rows, _ = out_ref.shape
    nblk = surf_ref.shape[1]
    tiles = slot_ref.shape[1]
    tops = coords_ref.shape[0] // 6
    for copy in copies:
        copy.wait()
    rest = (rows - 3 * cap, lanes)
    lane = lax.broadcasted_iota(jnp.int32, rest, 1)
    line = lax.broadcasted_iota(jnp.int32, rest, 0)
    tail = jnp.zeros(rest, f32)
    for t in range(tiles):
        tail = jnp.where((lane == t) & (line == 0), slot_ref[0, t].astype(f32), tail)
    for q in range(nblk // cap):
        stage[q, 3 * cap :] = tail
    empty = jnp.concatenate([jnp.zeros((3 * cap, lanes), f32), tail], axis=0).astype(bf16)
    for j in range(parts):
        out_ref[j] = empty
    tables = [
        [(halves(coords_ref, c, tops) + halves(disp_ref, c, tops)).astype(bf16)] for c in range(3)
    ]
    size = min(cap, 8)
    for first in range(0, nblk, 8):
        values = lookup(tables, [surf_ref[0, first + i : first + i + 1] for i in range(8)])
        for b in range(first, first + 8, size):
            for c in range(3):
                at = c * cap + b % cap
                stage[b // cap, at : at + size] = jnp.concatenate(
                    values[c][b - first : b - first + size], axis=0
                )
    for q in range(nblk // cap):
        out_ref[region_ref[0, q * cap]] = stage[q].astype(bf16)


def element_kernel(
    cap, rows, slot_ref, face_ref, pos_ref, normal_ref, disp_ref, stiff_ref, modulus_ref, nodes_ref,
    mass_ref, lo_ref, hi_ref, surf_ref, region_ref,
    out_ref, faces_ref, starts_ref, first_ref, second_ref, local, sums,
):
    tiles = slot_ref.shape[1]
    for t in range(tiles):
        starts_ref[0, t] = (slot_ref[0, t] // cap) * rows + slot_ref[0, t] % cap
        for c in range(3):
            at = c * tiles + t
            faces_ref[0, at : at + 1] = pos_ref[0, c, pl.ds(face_ref[0, t], 1)]
            faces_ref[1, at : at + 1] = normal_ref[0, c, pl.ds(face_ref[0, t], 1)]
    corners, count = nodes_ref.shape[1:]
    tops = disp_ref.shape[0] // 6
    tables = [two_parts(halves(disp_ref, c, tops)) for c in range(3)]
    cuts = [slice(g * lanes, (g + 1) * lanes) for g in range(count // lanes)]
    nodes = [[nodes_ref[0, a : a + 1, cut] for a in range(corners)] for cut in cuts]
    for cut, here in zip(cuts, nodes):
        values = lookup(tables, here)
        for c in range(3):
            local[c * corners : (c + 1) * corners, cut] = jnp.concatenate(values[c], axis=0)
    force = jnp.dot(
        stiff_ref[...], local[...], precision=lax.Precision.HIGHEST, preferred_element_type=f32
    )
    local[...] = -(force * modulus_ref[...])
    for g, (cut, here) in enumerate(zip(cuts, nodes)):
        values = [
            [local[c * corners + a : c * corners + a + 1, cut] for a in range(corners)]
            for c in range(3)
        ]
        added = node_sums(here, values, tops)
        sums[...] = added if g == 0 else sums[...] + added
    out_ref[...] = jnp.zeros_like(out_ref)
    for c in range(3):
        add_halves(out_ref, sums[...], c, tops)
    even = lax.axis_index("dom") % 2 == 0
    nblk = surf_ref.shape[1]
    shared = lo_ref.shape[0]
    head = first_ref.shape[0] - 4 * shared
    tables = [two_parts(sums[c * tops : (c + 1) * tops]) for c in range(3)]
    tables.append(two_parts(halves(mass_ref, 0, tops)))
    values = lookup(tables, [ref[k : k + 1] for ref in (lo_ref, hi_ref) for k in range(shared)])
    lower_list, upper_list = lo_ref[...].astype(f32), hi_ref[...].astype(f32)
    for ref, up in ((first_ref, even), (second_ref, jnp.logical_not(even))):
        ref[:nblk] = surf_ref[0].astype(f32)
        ref[nblk : nblk + shared] = jnp.where(up, upper_list, lower_list)
        ref[nblk + shared : nblk + shared + 1] = region_ref[...].astype(f32)
        ref[nblk + shared + 1 : head] = jnp.zeros((head - nblk - shared - 1, lanes), f32)
        for c in range(4):
            lower = jnp.concatenate(values[c][:shared], axis=0)
            upper = jnp.concatenate(values[c][shared:], axis=0)
            ref[head + c * shared : head + (c + 1) * shared] = jnp.where(up, upper, lower)


def neighbour_kernel(
    part_ref, mass_ref, lo_ref, hi_ref, region_ref, first_ref, second_ref,
    out_ref, out_mass_ref, surf_ref, nodes_ref, regions_ref,
):
    even = lax.axis_index("dom") % 2 == 0
    tops = mass_ref.shape[0] // 2
    nblk = surf_ref.shape[1]
    shared = lo_ref.shape[0]
    head = first_ref.shape[0] - 4 * shared
    out_ref[...] = part_ref[...]
    out_mass_ref[...] = mass_ref[...]
    first, second = first_ref[...], second_ref[...]
    packs = [jnp.where(even, second, first), jnp.where(even, first, second)]
    for i, pack in enumerate(packs):
        surf_ref[i] = pack[:nblk].astype(jnp.int32)
        nodes_ref[(2 + i) * shared : (3 + i) * shared] = pack[nblk : nblk + shared].astype(jnp.int32)
        regions_ref[2 * i : 2 * i + 1] = pack[nblk + shared : nblk + shared + 1].astype(jnp.int32)
    regions_ref[1:2] = region_ref[...]
    nodes_ref[:shared] = lo_ref[...]
    nodes_ref[shared : 2 * shared] = hi_ref[...]
    nodes = [ref[k : k + 1] for ref in (lo_ref, hi_ref) for k in range(shared)]
    values = [
        [pack[head + c * shared + k : head + c * shared + k + 1] for pack in packs for k in range(shared)]
        for c in range(4)
    ]
    sums = node_sums(nodes, values, tops)
    for c in range(3):
        add_halves(out_ref, sums, c, tops)
    add_halves(out_mass_ref, sums, 3, tops, 0)


def tile_kernel(cap, starts_ref, got_ref, faces_ref, weight_ref, out_ref, slots_ref, flat):
    parts, rows, _ = got_ref.shape
    tiles = starts_ref.shape[1]
    for j in range(parts):
        flat[j * rows : (j + 1) * rows] = got_ref[j].astype(f32)
    slots_ref[...] = jnp.concatenate(
        [flat[j * rows + 3 * cap : j * rows + 3 * cap + 1] for j in range(parts)], axis=0
    ).astype(jnp.int32)
    x = jnp.concatenate(
        [flat[pl.ds(starts_ref[0, t] + c * cap, 1)] for c in range(3) for t in range(tiles)], axis=0
    )
    weights = weight_ref[0].reshape(tiles * lanes, lanes)
    crossed = lax.dot_general(
        x.astype(bf16), weights, (((1,), (1,)), ((), ())), preferred_element_type=f32
    )
    line = lax.broadcasted_iota(jnp.int32, (tiles, lanes), 0)
    gap = jnp.zeros((tiles, lanes), f32)
    normals = []
    for c in range(3):
        interp = jnp.zeros((tiles, lanes), f32)
        for t in range(tiles):
            here = crossed[c * tiles : (c + 1) * tiles, t * lanes : (t + 1) * lanes]
            interp = jnp.where(line == t, here, interp)
        normal = faces_ref[1, c * tiles : (c + 1) * tiles]
        gap += normal * (interp - faces_ref[0, c * tiles : (c + 1) * tiles])
        normals.append(normal)
    pressure = penalty * jnp.maximum(-gap, 0.0)
    push = [pressure * normal for normal in normals]
    spread = jnp.concatenate(
        [
            jnp.concatenate([jnp.where(line == t, p, 0.0) for p in push], axis=0).astype(bf16)
            for t in range(tiles)
        ],
        axis=1,
    )
    forces = jnp.dot(spread, weights, preferred_element_type=f32).astype(bf16)
    pad = out_ref.shape[0] - forces.shape[0]
    if pad:
        forces = jnp.concatenate([forces, jnp.zeros((pad, lanes), bf16)], axis=0)
    out_ref[...] = forces


def list_kernel(cap, tiles, force_rows, slots_ref, regions_ref, list_ref, run_of):
    parts = slots_ref.shape[0]
    nblk = regions_ref.shape[1]
    shift = cap.bit_length() - 1
    me = lax.axis_index("dom")
    for p in range(3):
        for q in range(nblk // cap):
            run_of[p, regions_ref[p, q * cap]] = q * cap

    def pick(place, filled):
        j = me ^ place
        runs = [run_of[p, j] for p in range(3)]
        slots = [slots_ref[j, t] for t in range(tiles)]
        filled = list(filled)
        stores = []
        for t, slot in enumerate(slots):
            source = (slot >> shift) - me + 1
            entry = (place * force_rows + t) * code + (slot & (cap - 1))
            for p in range(3):
                stores.append((p, filled[p], entry + runs[p]))
                filled[p] = filled[p] + jnp.where(source == p, 1, 0)
        for p, at, entry in stores:
            list_ref[p, at] = entry
        return tuple(filled)

    zero = jnp.int32(0)
    filled = lax.fori_loop(0, parts, pick, (zero, zero, zero))
    for p in range(3):
        for i in range(8):
            list_ref[p, filled[p] + i] = 0
        list_ref[3, p] = filled[p]


def contact_kernel(tiles, list_ref, surf_ref, next_ref, nodes_ref, part_ref, *refs):
    back_refs, out_ref, back, sums, total = refs[:-4], refs[-4], refs[-3], refs[-2], refs[-1]
    size = back_refs[0].shape[0]
    tops = part_ref.shape[0] // 6
    shared = nodes_ref.shape[0] // 4
    total[...] = part_ref[...]
    for i, ref in enumerate(back_refs):
        back[i * size : (i + 1) * size] = ref[...].astype(f32)
    found = {}
    for p, blocks in ((1, surf_ref.at[0]), (0, next_ref.at[0]), (2, next_ref.at[1])):
        filled = list_ref[3, p]
        sums[...] = jnp.zeros_like(sums)

        def spread(g, _):
            nodes, values = [], [[], [], []]
            for i in range(8):
                entry = list_ref[p, g * 8 + i]
                row = blocks[pl.ds(entry & (code - 1), 1)]
                nodes.append(jnp.where(g * 8 + i < filled, row, -1))
                for c in range(3):
                    values[c].append(back[pl.ds((entry >> code_bits) + c * tiles, 1)])
            sums[...] += node_sums(nodes, values, tops, 1)
            return 0

        lax.fori_loop(0, (filled + 7) // 8, spread, 0)
        if p == 1:
            for c in range(3):
                add_halves(total, sums[...], c, tops)
        else:
            at = (2 + p // 2) * shared
            found[p] = lookup(
                [two_parts(sums[c * tops : (c + 1) * tops]) for c in range(3)],
                [nodes_ref[at + k : at + k + 1] for k in range(shared)],
            )
    added = node_sums(
        [nodes_ref[k : k + 1] for k in range(2 * shared)],
        [found[0][c] + found[2][c] for c in range(3)],
        tops,
    )
    for c in range(3):
        add_halves(total, added, c, tops)
    out_ref[...] = total[...].astype(bf16)


def accel_kernel(mass_ref, *refs):
    out_ref = refs[-1]
    terms = [ref[...].astype(f32) for ref in refs[:-1]]
    while len(terms) > 1:
        terms = [a + b for a, b in zip(terms[::2], terms[1::2])]
    size = mass_ref.shape[0]
    for c in range(3):
        at = slice(c * size, (c + 1) * size)
        out_ref[at] = terms[0][at] / mass_ref[...]


def swapped(block, start):
    lows = range(start, lax.axis_size("dom") - 1, 2)
    return lax.ppermute(block, "dom", [(s, s + 1) for s in lows] + [(s + 1, s) for s in lows])


def from_mate(block, distance):
    return lax.ppermute(
        block, "rep", [(i, i ^ distance) for i in range(lax.axis_size("rep"))]
    )


def across(block, distance):
    return lax.ppermute(
        block, "dom", [(s, s ^ distance) for s in range(lax.axis_size("dom"))]
    )


def on_device(
    coords,
    disp,
    mass,
    stiffness,
    elem_nodes,
    modulus,
    surf_nodes,
    block_region,
    face_pos,
    face_normal,
    tile_slot,
    tile_face,
    tile_weight,
    shared_lo,
    shared_hi,
):
    parts = lax.axis_size("dom")
    assert lax.axis_size("rep") == 4
    nodes_all = disp.shape[2]
    nblk = surf_nodes.shape[1]
    tiles = tile_slot.shape[1]
    cap = max(2, 2 * nblk // parts)
    rows = (3 * cap + 1 + 15) // 16 * 16
    force_rows = (3 * tiles + 15) // 16 * 16
    node_array = jax.ShapeDtypeStruct((3 * nodes_all // lanes, lanes), f32)
    mass_array = jax.ShapeDtypeStruct((nodes_all // lanes, lanes), f32)
    coords = coords.reshape(node_array.shape)
    disp = disp.reshape(node_array.shape)
    mass = mass.reshape(mass_array.shape)
    shared_lo = shared_lo.reshape(-1, lanes)
    shared_hi = shared_hi.reshape(-1, lanes)
    shared = shared_lo.shape[0]
    payload = jax.ShapeDtypeStruct((nblk + (shared + 8) // 8 * 8 + 4 * shared, lanes), f32)

    outgoing = call(
        functools.partial(pack_kernel, cap),
        jax.ShapeDtypeStruct((parts, rows, lanes), bf16),
        [hbm] * 5,
        vmem,
        [
            pltpu.VMEM((nblk // cap, rows, lanes), f32),
            pltpu.SMEM(block_region.shape, jnp.int32),
            pltpu.SMEM(tile_slot.shape, jnp.int32),
            pltpu.VMEM(coords.shape, f32),
            pltpu.VMEM(disp.shape, f32),
            pltpu.VMEM(surf_nodes.shape, jnp.int32),
            pltpu.SemaphoreType.DMA((5,)),
        ],
        1 << 30,
        60,
    )(block_region, tile_slot, coords, disp, surf_nodes)
    arrived = lax.all_to_all(outgoing, "dom", split_axis=0, concat_axis=0, tiled=True)

    part, faces, starts, first, second = call(
        functools.partial(element_kernel, cap, rows),
        (
            node_array,
            jax.ShapeDtypeStruct((2, 3 * tiles, lanes), f32),
            jax.ShapeDtypeStruct((1, tiles), jnp.int32),
            payload,
            payload,
        ),
        [smem] * 2 + [vmem] * 11,
        (vmem, vmem, smem, vmem, vmem),
        [
            pltpu.VMEM((24, modulus.shape[1]), f32),
            pltpu.VMEM((3 * nodes_all // wide, wide), f32),
        ],
        1 << 32,
    )(
        tile_slot,
        tile_face,
        jnp.swapaxes(face_pos, 1, 2),
        jnp.swapaxes(face_normal, 1, 2),
        disp,
        stiffness,
        modulus,
        elem_nodes,
        mass,
        shared_lo,
        shared_hi,
        surf_nodes,
        block_region,
    )
    first, second = swapped(first, 0), swapped(second, 1)

    forces, slots = call(
        functools.partial(tile_kernel, cap),
        (
            jax.ShapeDtypeStruct((force_rows, lanes), bf16),
            jax.ShapeDtypeStruct((parts, lanes), jnp.int32),
        ),
        [smem] + [vmem] * 3,
        (vmem, vmem),
        [pltpu.VMEM((parts * rows, lanes), f32)],
        1 << 28,
    )(starts, arrived, faces, tile_weight)
    held, distance = forces, 1
    while 4 * distance < parts:
        held = jnp.concatenate([held, across(held, distance)], axis=0)
        distance *= 2
    back = [held] + [across(held, d) for d in range(distance, parts, distance)]
    part, mass, next_surf, nodes, regions = call(
        neighbour_kernel,
        (
            node_array,
            mass_array,
            jax.ShapeDtypeStruct((2, nblk, lanes), jnp.int32),
            jax.ShapeDtypeStruct((4 * shared, lanes), jnp.int32),
            jax.ShapeDtypeStruct((3, nblk), jnp.int32),
        ),
        [vmem] * 7,
        (vmem,) * 5,
        [],
        1 << 26,
    )(part, mass, shared_lo, shared_hi, block_region, first, second)
    picks = call(
        functools.partial(list_kernel, cap, tiles, force_rows),
        jax.ShapeDtypeStruct((4, parts * tiles + 16), jnp.int32),
        [smem, smem],
        smem,
        [pltpu.SMEM((3, parts), jnp.int32)],
        1 << 24,
    )(slots, regions)
    own = call(
        functools.partial(contact_kernel, tiles),
        jax.ShapeDtypeStruct(node_array.shape, bf16),
        [smem] + [vmem] * (4 + len(back)),
        vmem,
        [
            pltpu.VMEM((parts * force_rows, lanes), f32),
            pltpu.VMEM((3 * nodes_all // wide, wide), f32),
            pltpu.VMEM(node_array.shape, f32),
        ],
        1 << 28,
    )(picks, surf_nodes, next_surf, nodes, part, *back)
    accel = call(accel_kernel, node_array, [vmem] * 5, vmem, [], 1 << 24)(
        mass, own, *[from_mate(own, k) for k in (1, 2, 3)]
    )
    return accel.reshape(1, 3, nodes_all)


def solution(mesh):
    in_specs = (
        P("dom", None, None),
        P("dom", None, None),
        P("dom", None),
        P(),
        P("dom", None, "rep"),
        P("dom", "rep"),
        P("dom", None, None),
        P("dom", None),
        P("dom", None, None, None),
        P("dom", None, None, None),
        P("dom", "rep"),
        P("dom", "rep"),
        P("dom", "rep", None, None),
        P("dom", None),
        P("dom", None),
    )
    out_specs = P("dom", None, None)
    return jax.shard_map(
        on_device, mesh=mesh, in_specs=in_specs, out_specs=out_specs, check_vma=False
    )
```

```python
import functools

import jax
import jax.numpy as jnp
from jax import lax
from jax.experimental import pallas as pl
from jax.experimental.pallas import tpu as pltpu
from jax.sharding import PartitionSpec as P

penalty = 4.0
lanes = 128
wide = 256
code_bits = 12
code = 1 << code_bits
vmem = pl.BlockSpec(memory_space=pltpu.VMEM)
smem = pl.BlockSpec(memory_space=pltpu.SMEM)
hbm = pl.BlockSpec(memory_space=pltpu.HBM)
f32 = jnp.float32
bf16 = jnp.bfloat16


def call(body, out_shape, in_specs, out_specs, scratch, flops, vmem_mib=32):
    return pl.pallas_call(
        body,
        out_shape=out_shape,
        in_specs=in_specs,
        out_specs=out_specs,
        scratch_shapes=scratch,
        compiler_params=pltpu.CompilerParams(vmem_limit_bytes=vmem_mib * 1024 * 1024),
        cost_estimate=pl.CostEstimate(flops=flops, bytes_accessed=1 << 20, transcendentals=0),
    )


def one_hot(nodes):
    line = lax.broadcasted_iota(jnp.int32, (wide, lanes), 0).astype(f32).astype(bf16)
    low = [(row & (wide - 1)).astype(f32).astype(bf16) for row in nodes]
    one, zero = jnp.ones((), bf16), jnp.zeros((), bf16)
    return jnp.concatenate([jnp.where(line == row, one, zero) for row in low], axis=1)


def halves(ref, c, tops):
    at = c * 2 * tops
    return jnp.concatenate(
        [ref[pl.ds(at, tops, stride=2)], ref[pl.ds(at + 1, tops, stride=2)]], axis=1
    )


def two_parts(x):
    coarse = x.astype(bf16)
    return [coarse, (x - coarse.astype(f32)).astype(bf16)]


def lookup(tables, nodes):
    tops = tables[0][0].shape[0]
    stacked = jnp.concatenate([part for table in tables for part in table], axis=0)
    found = jnp.dot(stacked, one_hot(nodes), preferred_element_type=f32)
    line = lax.broadcasted_iota(jnp.int32, (tops, lanes), 0)
    values = [[] for _ in tables]
    for i, row in enumerate(nodes):
        match = line == (row >> 8)
        at = 0
        for c, table in enumerate(tables):
            here = found[at : at + tops, i * lanes : (i + 1) * lanes]
            for p in range(1, len(table)):
                here += found[at + p * tops : at + (p + 1) * tops, i * lanes : (i + 1) * lanes]
            at += len(table) * tops
            values[c].append(jnp.sum(jnp.where(match, here, 0.0), axis=0, keepdims=True))
    return values


def node_sums(nodes, values, tops, parts=2):
    line = lax.broadcasted_iota(jnp.int32, (tops, lanes), 0)
    comps = len(values)
    left = []
    for i, row in enumerate(nodes):
        match = line == (row >> 8)
        pieces = [v[i] for v in values]
        if parts == 2:
            coarse = [v.astype(bf16).astype(f32) for v in pieces]
            pieces = coarse + [v - w for v, w in zip(pieces, coarse)]
        left.append(
            jnp.concatenate([jnp.where(match, v, 0.0).astype(bf16) for v in pieces], axis=0)
        )
    both = lax.dot_general(
        jnp.concatenate(left, axis=1),
        one_hot(nodes),
        (((1,), (1,)), ((), ())),
        preferred_element_type=f32,
    )
    return both if parts == 1 else both[: comps * tops] + both[comps * tops :]


def add_halves(ref, sums, c, tops, row=None):
    at = (c if row is None else row) * 2 * tops
    for half in range(2):
        ref[pl.ds(at + half, tops, stride=2)] += sums[
            c * tops : (c + 1) * tops, half * lanes : (half + 1) * lanes
        ]


def pack_kernel(
    cap, region_hbm, slot_hbm, coords_hbm, disp_hbm, surf_hbm, out_ref,
    stage, region_ref, slot_ref, coords_ref, disp_ref, surf_ref, sems,
):
    sources = (coords_hbm, disp_hbm, slot_hbm, surf_hbm, region_hbm)
    places = (coords_ref, disp_ref, slot_ref, surf_ref, region_ref)
    copies = [
        pltpu.make_async_copy(a, b, sems.at[i]) for i, (a, b) in enumerate(zip(sources, places))
    ]
    for copy in copies:
        copy.start()
    parts, rows, _ = out_ref.shape
    nblk = surf_ref.shape[1]
    tiles = slot_ref.shape[1]
    tops = coords_ref.shape[0] // 6
    for copy in copies:
        copy.wait()
    rest = (rows - 3 * cap, lanes)
    lane = lax.broadcasted_iota(jnp.int32, rest, 1)
    line = lax.broadcasted_iota(jnp.int32, rest, 0)
    tail = jnp.zeros(rest, f32)
    for t in range(tiles):
        tail = jnp.where((lane == t) & (line == 0), slot_ref[0, t].astype(f32), tail)
    for q in range(nblk // cap):
        stage[q, 3 * cap :] = tail
    empty = jnp.concatenate([jnp.zeros((3 * cap, lanes), f32), tail], axis=0).astype(bf16)
    for j in range(parts):
        out_ref[j] = empty
    tables = [
        [(halves(coords_ref, c, tops) + halves(disp_ref, c, tops)).astype(bf16)] for c in range(3)
    ]
    size = min(cap, 8)
    for first in range(0, nblk, 8):
        values = lookup(tables, [surf_ref[0, first + i : first + i + 1] for i in range(8)])
        for b in range(first, first + 8, size):
            for c in range(3):
                at = c * cap + b % cap
                stage[b // cap, at : at + size] = jnp.concatenate(
                    values[c][b - first : b - first + size], axis=0
                )
    for q in range(nblk // cap):
        out_ref[region_ref[0, q * cap]] = stage[q].astype(bf16)


def face_kernel(cap, rows, slot_ref, face_ref, pos_ref, normal_ref, faces_ref, starts_ref):
    tiles = slot_ref.shape[1]
    for t in range(tiles):
        starts_ref[0, t] = (slot_ref[0, t] // cap) * rows + slot_ref[0, t] % cap
        for c in range(3):
            at = c * tiles + t
            faces_ref[0, at : at + 1] = pos_ref[0, c, pl.ds(face_ref[0, t], 1)]
            faces_ref[1, at : at + 1] = normal_ref[0, c, pl.ds(face_ref[0, t], 1)]


def element_kernel(
    disp_ref, stiff_ref, modulus_ref, nodes_ref, mass_ref, lo_ref, hi_ref, surf_ref, region_ref,
    out_ref, first_ref, second_ref, local, sums,
):
    corners, count = nodes_ref.shape[1:]
    tops = disp_ref.shape[0] // 6
    tables = [two_parts(halves(disp_ref, c, tops)) for c in range(3)]
    cuts = [slice(g * lanes, (g + 1) * lanes) for g in range(count // lanes)]
    nodes = [[nodes_ref[0, a : a + 1, cut] for a in range(corners)] for cut in cuts]
    for cut, here in zip(cuts, nodes):
        values = lookup(tables, here)
        for c in range(3):
            local[c * corners : (c + 1) * corners, cut] = jnp.concatenate(values[c], axis=0)
    force = jnp.dot(
        stiff_ref[...], local[...], precision=lax.Precision.HIGHEST, preferred_element_type=f32
    )
    local[...] = -(force * modulus_ref[...])
    for g, (cut, here) in enumerate(zip(cuts, nodes)):
        values = [
            [local[c * corners + a : c * corners + a + 1, cut] for a in range(corners)]
            for c in range(3)
        ]
        added = node_sums(here, values, tops)
        sums[...] = added if g == 0 else sums[...] + added
    out_ref[...] = jnp.zeros_like(out_ref)
    for c in range(3):
        add_halves(out_ref, sums[...], c, tops)
    even = lax.axis_index("dom") % 2 == 0
    nblk = surf_ref.shape[1]
    shared = lo_ref.shape[0]
    head = first_ref.shape[0] - 4 * shared
    tables = [two_parts(sums[c * tops : (c + 1) * tops]) for c in range(3)]
    tables.append(two_parts(halves(mass_ref, 0, tops)))
    values = lookup(tables, [ref[k : k + 1] for ref in (lo_ref, hi_ref) for k in range(shared)])
    lower_list, upper_list = lo_ref[...].astype(f32), hi_ref[...].astype(f32)
    for ref, up in ((first_ref, even), (second_ref, jnp.logical_not(even))):
        ref[:nblk] = surf_ref[0].astype(f32)
        ref[nblk : nblk + shared] = jnp.where(up, upper_list, lower_list)
        ref[nblk + shared : nblk + shared + 1] = region_ref[...].astype(f32)
        ref[nblk + shared + 1 : head] = jnp.zeros((head - nblk - shared - 1, lanes), f32)
        for c in range(4):
            lower = jnp.concatenate(values[c][:shared], axis=0)
            upper = jnp.concatenate(values[c][shared:], axis=0)
            ref[head + c * shared : head + (c + 1) * shared] = jnp.where(up, upper, lower)


def neighbour_kernel(
    part_ref, mass_ref, lo_ref, hi_ref, own_surf_ref, region_ref, first_ref, second_ref,
    out_ref, out_mass_ref, surf_ref, nodes_ref, regions_ref,
):
    even = lax.axis_index("dom") % 2 == 0
    tops = mass_ref.shape[0] // 2
    nblk = own_surf_ref.shape[1]
    nodes_all = mass_ref.shape[0] * lanes
    shared = lo_ref.shape[0]
    head = first_ref.shape[0] - 4 * shared
    out_ref[...] = part_ref[...]
    out_mass_ref[...] = mass_ref[...]
    first, second = first_ref[...], second_ref[...]
    packs = [jnp.where(even, second, first), jnp.where(even, first, second)]
    for i, pack in enumerate(packs):
        surf_ref[2 * i * nblk : (2 * i + 1) * nblk] = pack[:nblk].astype(jnp.int32) + 2 * i * nodes_all
        nodes_ref[(2 + i) * shared : (3 + i) * shared] = pack[nblk : nblk + shared].astype(jnp.int32)
        regions_ref[2 * i : 2 * i + 1] = pack[nblk + shared : nblk + shared + 1].astype(jnp.int32)
    surf_ref[nblk : 2 * nblk] = own_surf_ref[0] + nodes_all
    regions_ref[1:2] = region_ref[...]
    nodes_ref[:shared] = lo_ref[...]
    nodes_ref[shared : 2 * shared] = hi_ref[...]
    nodes = [ref[k : k + 1] for ref in (lo_ref, hi_ref) for k in range(shared)]
    values = [
        [pack[head + c * shared + k : head + c * shared + k + 1] for pack in packs for k in range(shared)]
        for c in range(4)
    ]
    sums = node_sums(nodes, values, tops)
    for c in range(3):
        add_halves(out_ref, sums, c, tops)
    add_halves(out_mass_ref, sums, 3, tops, 0)


def tile_kernel(cap, starts_ref, got_ref, faces_ref, weight_ref, out_ref, slots_ref, flat):
    parts, rows, _ = got_ref.shape
    tiles = starts_ref.shape[1]
    for j in range(parts):
        flat[j * rows : (j + 1) * rows] = got_ref[j].astype(f32)
    slots_ref[...] = jnp.concatenate(
        [flat[j * rows + 3 * cap : j * rows + 3 * cap + 1] for j in range(parts)], axis=0
    ).astype(jnp.int32)
    x = jnp.concatenate(
        [flat[pl.ds(starts_ref[0, t] + c * cap, 1)] for c in range(3) for t in range(tiles)], axis=0
    )
    weights = weight_ref[0].reshape(tiles * lanes, lanes)
    crossed = lax.dot_general(
        x.astype(bf16), weights, (((1,), (1,)), ((), ())), preferred_element_type=f32
    )
    line = lax.broadcasted_iota(jnp.int32, (tiles, lanes), 0)
    gap = jnp.zeros((tiles, lanes), f32)
    normals = []
    for c in range(3):
        interp = jnp.zeros((tiles, lanes), f32)
        for t in range(tiles):
            here = crossed[c * tiles : (c + 1) * tiles, t * lanes : (t + 1) * lanes]
            interp = jnp.where(line == t, here, interp)
        normal = faces_ref[1, c * tiles : (c + 1) * tiles]
        gap += normal * (interp - faces_ref[0, c * tiles : (c + 1) * tiles])
        normals.append(normal)
    pressure = penalty * jnp.maximum(-gap, 0.0)
    push = [pressure * normal for normal in normals]
    spread = jnp.concatenate(
        [
            jnp.concatenate([jnp.where(line == t, p, 0.0) for p in push], axis=0).astype(bf16)
            for t in range(tiles)
        ],
        axis=1,
    )
    forces = jnp.dot(spread, weights, preferred_element_type=f32).astype(bf16)
    pad = out_ref.shape[0] - forces.shape[0]
    if pad:
        forces = jnp.concatenate([forces, jnp.zeros((pad, lanes), bf16)], axis=0)
    out_ref[...] = forces


def list_kernel(cap, tiles, force_rows, slots_ref, regions_ref, list_ref, run_of):
    parts = slots_ref.shape[0]
    nblk = regions_ref.shape[1]
    shift = cap.bit_length() - 1
    me = lax.axis_index("dom")
    for p in range(3):
        for q in range(nblk // cap):
            run_of[p * parts + regions_ref[p, q * cap]] = p * nblk + q * cap

    def pick(place, filled):
        j = me ^ place
        slots = [slots_ref[j, t] for t in range(tiles)]
        which = [(slot >> shift) - me + 1 for slot in slots]
        kept = [(p >= 0) & (p <= 2) for p in which]
        runs = [run_of[jnp.where(own, p, 0) * parts + j] for own, p in zip(kept, which)]
        places = []
        for own in kept:
            places.append(filled)
            filled = filled + jnp.where(own, 1, 0)
        for t in range(tiles):
            entry = (place * force_rows + t) * code + (slots[t] & (cap - 1)) + runs[t]
            list_ref[0, places[t]] = entry
        return filled

    filled = lax.fori_loop(0, parts, pick, jnp.int32(0))
    for i in range(8):
        list_ref[0, filled + i] = 0
    list_ref[0, list_ref.shape[1] - 1] = filled


def contact_kernel(tiles, list_ref, surf_ref, nodes_ref, part_ref, *refs):
    back_refs, out_ref, back, sums, total = refs[:-4], refs[-4], refs[-3], refs[-2], refs[-1]
    size = back_refs[0].shape[0]
    tops = part_ref.shape[0] // 6
    shared = nodes_ref.shape[0] // 4
    total[...] = part_ref[...]
    for i, ref in enumerate(back_refs):
        back[i * size : (i + 1) * size] = ref[...].astype(f32)
    filled = list_ref[0, list_ref.shape[1] - 1]
    sums[...] = jnp.zeros_like(sums)

    def spread(g, _):
        nodes, values = [], [[], [], []]
        for i in range(8):
            entry = list_ref[0, g * 8 + i]
            row = surf_ref[pl.ds(entry & (code - 1), 1)]
            nodes.append(jnp.where(g * 8 + i < filled, row, -1))
            for c in range(3):
                values[c].append(back[pl.ds((entry >> code_bits) + c * tiles, 1)])
        sums[...] += node_sums(nodes, values, 3 * tops, 1)
        return 0

    lax.fori_loop(0, (filled + 7) // 8, spread, 0)
    pieces = [[sums[(c * 3 + p) * tops : (c * 3 + p + 1) * tops] for c in range(3)] for p in range(3)]
    found = []
    for p in (0, 2):
        at = (2 + p // 2) * shared
        found.append(
            lookup(
                [two_parts(piece) for piece in pieces[p]],
                [nodes_ref[at + k : at + k + 1] for k in range(shared)],
            )
        )
    added = node_sums(
        [nodes_ref[k : k + 1] for k in range(2 * shared)],
        [found[0][c] + found[1][c] for c in range(3)],
        tops,
    )
    added += jnp.concatenate(pieces[1], axis=0)
    for c in range(3):
        add_halves(total, added, c, tops)
    out_ref[...] = total[...].astype(bf16)


def accel_kernel(mass_ref, *refs):
    out_ref = refs[-1]
    terms = [ref[...].astype(f32) for ref in refs[:-1]]
    while len(terms) > 1:
        terms = [a + b for a, b in zip(terms[::2], terms[1::2])]
    size = mass_ref.shape[0]
    for c in range(3):
        at = slice(c * size, (c + 1) * size)
        out_ref[at] = terms[0][at] / mass_ref[...]


def swapped(block, start):
    lows = range(start, lax.axis_size("dom") - 1, 2)
    return lax.ppermute(block, "dom", [(s, s + 1) for s in lows] + [(s + 1, s) for s in lows])


def from_mate(block, distance):
    return lax.ppermute(
        block, "rep", [(i, i ^ distance) for i in range(lax.axis_size("rep"))]
    )


def across(block, distance):
    return lax.ppermute(
        block, "dom", [(s, s ^ distance) for s in range(lax.axis_size("dom"))]
    )


def on_device(
    coords,
    disp,
    mass,
    stiffness,
    elem_nodes,
    modulus,
    surf_nodes,
    block_region,
    face_pos,
    face_normal,
    tile_slot,
    tile_face,
    tile_weight,
    shared_lo,
    shared_hi,
):
    parts = lax.axis_size("dom")
    assert lax.axis_size("rep") == 4
    nodes_all = disp.shape[2]
    nblk = surf_nodes.shape[1]
    tiles = tile_slot.shape[1]
    cap = max(2, 2 * nblk // parts)
    rows = (3 * cap + 1 + 15) // 16 * 16
    force_rows = (3 * tiles + 15) // 16 * 16
    node_array = jax.ShapeDtypeStruct((3 * nodes_all // lanes, lanes), f32)
    mass_array = jax.ShapeDtypeStruct((nodes_all // lanes, lanes), f32)
    coords = coords.reshape(node_array.shape)
    disp = disp.reshape(node_array.shape)
    mass = mass.reshape(mass_array.shape)
    shared_lo = shared_lo.reshape(-1, lanes)
    shared_hi = shared_hi.reshape(-1, lanes)
    shared = shared_lo.shape[0]
    payload = jax.ShapeDtypeStruct((nblk + (shared + 8) // 8 * 8 + 4 * shared, lanes), f32)

    outgoing = call(
        functools.partial(pack_kernel, cap),
        jax.ShapeDtypeStruct((parts, rows, lanes), bf16),
        [hbm] * 5,
        vmem,
        [
            pltpu.VMEM((nblk // cap, rows, lanes), f32),
            pltpu.SMEM(block_region.shape, jnp.int32),
            pltpu.SMEM(tile_slot.shape, jnp.int32),
            pltpu.VMEM(coords.shape, f32),
            pltpu.VMEM(disp.shape, f32),
            pltpu.VMEM(surf_nodes.shape, jnp.int32),
            pltpu.SemaphoreType.DMA((5,)),
        ],
        1 << 30,
        60,
    )(block_region, tile_slot, coords, disp, surf_nodes)
    arrived = lax.all_to_all(outgoing, "dom", split_axis=0, concat_axis=0, tiled=True)

    part, first, second = call(
        element_kernel,
        (node_array, payload, payload),
        [vmem] * 9,
        (vmem,) * 3,
        [
            pltpu.VMEM((24, modulus.shape[1]), f32),
            pltpu.VMEM((3 * nodes_all // wide, wide), f32),
        ],
        1 << 32,
    )(
        disp,
        stiffness,
        modulus,
        elem_nodes,
        mass,
        shared_lo,
        shared_hi,
        surf_nodes,
        block_region,
    )
    first, second = swapped(first, 0), swapped(second, 1)
    faces, starts = call(
        functools.partial(face_kernel, cap, rows),
        (
            jax.ShapeDtypeStruct((2, 3 * tiles, lanes), f32),
            jax.ShapeDtypeStruct((1, tiles), jnp.int32),
        ),
        [smem] * 2 + [vmem] * 2,
        (vmem, smem),
        [],
        1 << 20,
    )(tile_slot, tile_face, jnp.swapaxes(face_pos, 1, 2), jnp.swapaxes(face_normal, 1, 2))

    arrived, part = lax.optimization_barrier((arrived, part))
    forces, slots = call(
        functools.partial(tile_kernel, cap),
        (
            jax.ShapeDtypeStruct((force_rows, lanes), bf16),
            jax.ShapeDtypeStruct((parts, lanes), jnp.int32),
        ),
        [smem] + [vmem] * 3,
        (vmem, vmem),
        [pltpu.VMEM((parts * rows, lanes), f32)],
        1 << 28,
    )(starts, arrived, faces, tile_weight)
    part, mass, surf, nodes, regions = call(
        neighbour_kernel,
        (
            node_array,
            mass_array,
            jax.ShapeDtypeStruct((3 * nblk, lanes), jnp.int32),
            jax.ShapeDtypeStruct((4 * shared, lanes), jnp.int32),
            jax.ShapeDtypeStruct((3, nblk), jnp.int32),
        ),
        [vmem] * 8,
        (vmem,) * 5,
        [],
        1 << 26,
    )(part, mass, shared_lo, shared_hi, surf_nodes, block_region, first, second)
    picks = call(
        functools.partial(list_kernel, cap, tiles, force_rows),
        jax.ShapeDtypeStruct((1, parts * tiles + 16), jnp.int32),
        [smem, smem],
        smem,
        [pltpu.SMEM((3 * parts,), jnp.int32)],
        1 << 24,
    )(slots, regions)
    held, distance = forces, 1
    while 4 * distance < parts:
        other, picks = lax.optimization_barrier((across(held, distance), picks))
        held = jnp.concatenate([held, other], axis=0)
        distance *= 2
    back = [held] + [across(held, d) for d in range(distance, parts, distance)]
    own = call(
        functools.partial(contact_kernel, tiles),
        jax.ShapeDtypeStruct(node_array.shape, bf16),
        [smem] + [vmem] * (3 + len(back)),
        vmem,
        [
            pltpu.VMEM((parts * force_rows, lanes), f32),
            pltpu.VMEM((9 * nodes_all // wide, wide), f32),
            pltpu.VMEM(node_array.shape, f32),
        ],
        1 << 28,
    )(picks, surf, nodes, part, *back)
    accel = call(accel_kernel, node_array, [vmem] * 5, vmem, [], 1 << 24)(
        mass, own, *[from_mate(own, k) for k in (1, 2, 3)]
    )
    return accel.reshape(1, 3, nodes_all)


def solution(mesh):
    in_specs = (
        P("dom", None, None),
        P("dom", None, None),
        P("dom", None),
        P(),
        P("dom", None, "rep"),
        P("dom", "rep"),
        P("dom", None, None),
        P("dom", None),
        P("dom", None, None, None),
        P("dom", None, None, None),
        P("dom", "rep"),
        P("dom", "rep"),
        P("dom", "rep", None, None),
        P("dom", None),
        P("dom", None),
    )
    out_specs = P("dom", None, None)
    return jax.shard_map(
        on_device, mesh=mesh, in_specs=in_specs, out_specs=out_specs, check_vma=False
    )
```

```python
import functools

import jax
import jax.numpy as jnp
from jax import lax
from jax.experimental import pallas as pl
from jax.experimental.pallas import tpu as pltpu
from jax.sharding import PartitionSpec as P

penalty = 4.0
lanes = 128
wide = 256
code_bits = 12
code = 1 << code_bits
vmem = pl.BlockSpec(memory_space=pltpu.VMEM)
smem = pl.BlockSpec(memory_space=pltpu.SMEM)
hbm = pl.BlockSpec(memory_space=pltpu.HBM)
f32 = jnp.float32
bf16 = jnp.bfloat16


def call(body, out_shape, in_specs, out_specs, scratch, flops, vmem_mib=32):
    return pl.pallas_call(
        body,
        out_shape=out_shape,
        in_specs=in_specs,
        out_specs=out_specs,
        scratch_shapes=scratch,
        compiler_params=pltpu.CompilerParams(vmem_limit_bytes=vmem_mib * 1024 * 1024),
        cost_estimate=pl.CostEstimate(flops=flops, bytes_accessed=1 << 20, transcendentals=0),
    )


def one_hot(nodes):
    line = lax.broadcasted_iota(jnp.int32, (wide, lanes), 0).astype(f32).astype(bf16)
    low = [(row & (wide - 1)).astype(f32).astype(bf16) for row in nodes]
    one, zero = jnp.ones((), bf16), jnp.zeros((), bf16)
    return jnp.concatenate([jnp.where(line == row, one, zero) for row in low], axis=1)


def halves(ref, c, tops):
    at = c * 2 * tops
    return jnp.concatenate(
        [ref[pl.ds(at, tops, stride=2)], ref[pl.ds(at + 1, tops, stride=2)]], axis=1
    )


def two_parts(x):
    coarse = x.astype(bf16)
    return [coarse, (x - coarse.astype(f32)).astype(bf16)]


def lookup(tables, nodes):
    tops = tables[0][0].shape[0]
    stacked = jnp.concatenate([part for table in tables for part in table], axis=0)
    found = jnp.dot(stacked, one_hot(nodes), preferred_element_type=f32)
    line = lax.broadcasted_iota(jnp.int32, (tops, lanes), 0)
    values = [[] for _ in tables]
    for i, row in enumerate(nodes):
        match = line == (row >> 8)
        at = 0
        for c, table in enumerate(tables):
            here = found[at : at + tops, i * lanes : (i + 1) * lanes]
            for p in range(1, len(table)):
                here += found[at + p * tops : at + (p + 1) * tops, i * lanes : (i + 1) * lanes]
            at += len(table) * tops
            values[c].append(jnp.sum(jnp.where(match, here, 0.0), axis=0, keepdims=True))
    return values


def node_sums(nodes, values, tops, parts=2):
    line = lax.broadcasted_iota(jnp.int32, (tops, lanes), 0)
    comps = len(values)
    left = []
    for i, row in enumerate(nodes):
        match = line == (row >> 8)
        pieces = [v[i] for v in values]
        if parts == 2:
            coarse = [v.astype(bf16).astype(f32) for v in pieces]
            pieces = coarse + [v - w for v, w in zip(pieces, coarse)]
        left.append(
            jnp.concatenate([jnp.where(match, v, 0.0).astype(bf16) for v in pieces], axis=0)
        )
    both = lax.dot_general(
        jnp.concatenate(left, axis=1),
        one_hot(nodes),
        (((1,), (1,)), ((), ())),
        preferred_element_type=f32,
    )
    return both if parts == 1 else both[: comps * tops] + both[comps * tops :]


def add_halves(ref, sums, c, tops, row=None):
    at = (c if row is None else row) * 2 * tops
    for half in range(2):
        ref[pl.ds(at + half, tops, stride=2)] += sums[
            c * tops : (c + 1) * tops, half * lanes : (half + 1) * lanes
        ]


def pack_kernel(
    cap, region_hbm, slot_hbm, coords_hbm, disp_hbm, surf_hbm, out_ref,
    stage, region_ref, slot_ref, coords_ref, disp_ref, surf_ref, sems,
):
    sources = (coords_hbm, disp_hbm, slot_hbm, surf_hbm, region_hbm)
    places = (coords_ref, disp_ref, slot_ref, surf_ref, region_ref)
    copies = [
        pltpu.make_async_copy(a, b, sems.at[i]) for i, (a, b) in enumerate(zip(sources, places))
    ]
    for copy in copies:
        copy.start()
    parts, rows, _ = out_ref.shape
    nblk = surf_ref.shape[1]
    tiles = slot_ref.shape[1]
    tops = coords_ref.shape[0] // 6
    for copy in copies:
        copy.wait()
    rest = (rows - 3 * cap, lanes)
    lane = lax.broadcasted_iota(jnp.int32, rest, 1)
    line = lax.broadcasted_iota(jnp.int32, rest, 0)
    tail = jnp.zeros(rest, f32)
    for t in range(tiles):
        tail = jnp.where((lane == t) & (line == 0), slot_ref[0, t].astype(f32), tail)
    for q in range(nblk // cap):
        stage[q, 3 * cap :] = tail
    empty = jnp.concatenate([jnp.zeros((3 * cap, lanes), f32), tail], axis=0).astype(bf16)
    for j in range(parts):
        out_ref[j] = empty
    tables = [
        [(halves(coords_ref, c, tops) + halves(disp_ref, c, tops)).astype(bf16)] for c in range(3)
    ]
    size = min(cap, 8)
    for first in range(0, nblk, 8):
        values = lookup(tables, [surf_ref[0, first + i : first + i + 1] for i in range(8)])
        for b in range(first, first + 8, size):
            for c in range(3):
                at = c * cap + b % cap
                stage[b // cap, at : at + size] = jnp.concatenate(
                    values[c][b - first : b - first + size], axis=0
                )
    for q in range(nblk // cap):
        out_ref[region_ref[0, q * cap]] = stage[q].astype(bf16)


def element_kernel(disp_ref, stiff_ref, modulus_ref, nodes_ref, out_ref, local, sums):
    corners, count = nodes_ref.shape[1:]
    tops = disp_ref.shape[0] // 6
    tables = [two_parts(halves(disp_ref, c, tops)) for c in range(3)]
    cuts = [slice(g * lanes, (g + 1) * lanes) for g in range(count // lanes)]
    nodes = [[nodes_ref[0, a : a + 1, cut] for a in range(corners)] for cut in cuts]
    for cut, here in zip(cuts, nodes):
        values = lookup(tables, here)
        for c in range(3):
            local[c * corners : (c + 1) * corners, cut] = jnp.concatenate(values[c], axis=0)
    force = jnp.dot(
        stiff_ref[...], local[...], precision=lax.Precision.HIGHEST, preferred_element_type=f32
    )
    local[...] = -(force * modulus_ref[...])
    for g, (cut, here) in enumerate(zip(cuts, nodes)):
        values = [
            [local[c * corners + a : c * corners + a + 1, cut] for a in range(corners)]
            for c in range(3)
        ]
        added = node_sums(here, values, tops)
        sums[...] = added if g == 0 else sums[...] + added
    out_ref[...] = jnp.zeros_like(out_ref)
    for c in range(3):
        add_halves(out_ref, sums[...], c, tops)


def payload_kernel(
    slot_ref, face_ref, part_ref, mass_ref, lo_ref, hi_ref, surf_ref, region_ref,
    first_ref, second_ref, tiles_ref,
):
    for t in range(slot_ref.shape[1]):
        tiles_ref[0, t] = slot_ref[0, t]
        tiles_ref[1, t] = face_ref[0, t]
    even = lax.axis_index("dom") % 2 == 0
    tops = mass_ref.shape[0] // 2
    nblk = surf_ref.shape[1]
    shared = lo_ref.shape[0]
    head = first_ref.shape[0] - 4 * shared
    tables = [two_parts(halves(part_ref, c, tops)) for c in range(3)]
    tables.append(two_parts(halves(mass_ref, 0, tops)))
    values = lookup(tables, [ref[k : k + 1] for ref in (lo_ref, hi_ref) for k in range(shared)])
    lower_list, upper_list = lo_ref[...].astype(f32), hi_ref[...].astype(f32)
    for ref, up in ((first_ref, even), (second_ref, jnp.logical_not(even))):
        ref[:nblk] = surf_ref[0].astype(f32)
        ref[nblk : nblk + shared] = jnp.where(up, upper_list, lower_list)
        ref[nblk + shared : nblk + shared + 1] = region_ref[...].astype(f32)
        ref[nblk + shared + 1 : head] = jnp.zeros((head - nblk - shared - 1, lanes), f32)
        for c in range(4):
            lower = jnp.concatenate(values[c][:shared], axis=0)
            upper = jnp.concatenate(values[c][shared:], axis=0)
            ref[head + c * shared : head + (c + 1) * shared] = jnp.where(up, upper, lower)


def neighbour_kernel(
    part_ref, mass_ref, lo_ref, hi_ref, own_surf_ref, region_ref, first_ref, second_ref,
    out_ref, out_mass_ref, surf_ref, nodes_ref, regions_ref,
):
    even = lax.axis_index("dom") % 2 == 0
    tops = mass_ref.shape[0] // 2
    nblk = own_surf_ref.shape[1]
    nodes_all = mass_ref.shape[0] * lanes
    shared = lo_ref.shape[0]
    head = first_ref.shape[0] - 4 * shared
    out_ref[...] = part_ref[...]
    out_mass_ref[...] = mass_ref[...]
    first, second = first_ref[...], second_ref[...]
    packs = [jnp.where(even, second, first), jnp.where(even, first, second)]
    for i, pack in enumerate(packs):
        surf_ref[2 * i * nblk : (2 * i + 1) * nblk] = pack[:nblk].astype(jnp.int32) + 2 * i * nodes_all
        nodes_ref[(2 + i) * shared : (3 + i) * shared] = pack[nblk : nblk + shared].astype(jnp.int32)
        regions_ref[2 * i : 2 * i + 1] = pack[nblk + shared : nblk + shared + 1].astype(jnp.int32)
    surf_ref[nblk : 2 * nblk] = own_surf_ref[0] + nodes_all
    regions_ref[1:2] = region_ref[...]
    nodes_ref[:shared] = lo_ref[...]
    nodes_ref[shared : 2 * shared] = hi_ref[...]
    nodes = [ref[k : k + 1] for ref in (lo_ref, hi_ref) for k in range(shared)]
    values = [
        [pack[head + c * shared + k : head + c * shared + k + 1] for pack in packs for k in range(shared)]
        for c in range(4)
    ]
    sums = node_sums(nodes, values, tops)
    for c in range(3):
        add_halves(out_ref, sums, c, tops)
    add_halves(out_mass_ref, sums, 3, tops, 0)


def tile_kernel(cap, tiles_ref, got_ref, pos_ref, normal_ref, weight_ref, out_ref, slots_ref, flat):
    parts, rows, _ = got_ref.shape
    tiles = tiles_ref.shape[1]
    shift = cap.bit_length() - 1
    faces = [tiles_ref[1, t] for t in range(tiles)]
    starts = [(tiles_ref[0, t] >> shift) * rows + (tiles_ref[0, t] & (cap - 1)) for t in range(tiles)]
    for j in range(parts):
        flat[j * rows : (j + 1) * rows] = got_ref[j].astype(f32)
    slots_ref[...] = jnp.concatenate(
        [flat[j * rows + 3 * cap : j * rows + 3 * cap + 1] for j in range(parts)], axis=0
    ).astype(jnp.int32)
    x = jnp.concatenate(
        [flat[pl.ds(at + c * cap, 1)] for c in range(3) for at in starts], axis=0
    )
    weights = weight_ref[0].reshape(tiles * lanes, lanes)
    crossed = lax.dot_general(
        x.astype(bf16), weights, (((1,), (1,)), ((), ())), preferred_element_type=f32
    )
    line = lax.broadcasted_iota(jnp.int32, (tiles, lanes), 0)
    gap = jnp.zeros((tiles, lanes), f32)
    normals = []
    for c in range(3):
        interp = jnp.zeros((tiles, lanes), f32)
        for t in range(tiles):
            here = crossed[c * tiles : (c + 1) * tiles, t * lanes : (t + 1) * lanes]
            interp = jnp.where(line == t, here, interp)
        normal = jnp.concatenate([normal_ref[0, c, pl.ds(f, 1)] for f in faces], axis=0)
        pos = jnp.concatenate([pos_ref[0, c, pl.ds(f, 1)] for f in faces], axis=0)
        gap += normal * (interp - pos)
        normals.append(normal)
    pressure = penalty * jnp.maximum(-gap, 0.0)
    push = [pressure * normal for normal in normals]
    spread = jnp.concatenate(
        [
            jnp.concatenate([jnp.where(line == t, p, 0.0) for p in push], axis=0).astype(bf16)
            for t in range(tiles)
        ],
        axis=1,
    )
    forces = jnp.dot(spread, weights, preferred_element_type=f32).astype(bf16)
    pad = out_ref.shape[0] - forces.shape[0]
    if pad:
        forces = jnp.concatenate([forces, jnp.zeros((pad, lanes), bf16)], axis=0)
    out_ref[...] = forces


def list_kernel(cap, tiles, force_rows, slots_ref, regions_ref, list_ref, run_of):
    parts = slots_ref.shape[0]
    nblk = regions_ref.shape[1]
    shift = cap.bit_length() - 1
    me = lax.axis_index("dom")
    for p in range(3):
        for q in range(nblk // cap):
            run_of[p * parts + regions_ref[p, q * cap]] = p * nblk + q * cap

    def pick(place, filled):
        j = me ^ place
        slots = [slots_ref[j, t] for t in range(tiles)]
        which = [(slot >> shift) - me + 1 for slot in slots]
        kept = [(p >= 0) & (p <= 2) for p in which]
        runs = [run_of[jnp.where(own, p, 0) * parts + j] for own, p in zip(kept, which)]
        places = []
        for own in kept:
            places.append(filled)
            filled = filled + jnp.where(own, 1, 0)
        for t in range(tiles):
            entry = (place * force_rows + t) * code + (slots[t] & (cap - 1)) + runs[t]
            list_ref[0, places[t]] = entry
        return filled

    filled = lax.fori_loop(0, parts, pick, jnp.int32(0))
    for i in range(8):
        list_ref[0, filled + i] = 0
    list_ref[0, list_ref.shape[1] - 1] = filled


def contact_kernel(tiles, list_ref, surf_ref, nodes_ref, part_ref, *refs):
    back_refs, out_ref, back, sums, total = refs[:-4], refs[-4], refs[-3], refs[-2], refs[-1]
    size = back_refs[0].shape[0]
    tops = part_ref.shape[0] // 6
    shared = nodes_ref.shape[0] // 4
    total[...] = part_ref[...]
    for i, ref in enumerate(back_refs):
        back[i * size : (i + 1) * size] = ref[...].astype(f32)
    filled = list_ref[0, list_ref.shape[1] - 1]
    sums[...] = jnp.zeros_like(sums)

    def spread(g, _):
        nodes, values = [], [[], [], []]
        for i in range(8):
            entry = list_ref[0, g * 8 + i]
            row = surf_ref[pl.ds(entry & (code - 1), 1)]
            nodes.append(jnp.where(g * 8 + i < filled, row, -1))
            for c in range(3):
                values[c].append(back[pl.ds((entry >> code_bits) + c * tiles, 1)])
        sums[...] += node_sums(nodes, values, 3 * tops, 1)
        return 0

    lax.fori_loop(0, (filled + 7) // 8, spread, 0)
    pieces = [[sums[(c * 3 + p) * tops : (c * 3 + p + 1) * tops] for c in range(3)] for p in range(3)]
    found = []
    for p in (0, 2):
        at = (2 + p // 2) * shared
        found.append(
            lookup(
                [two_parts(piece) for piece in pieces[p]],
                [nodes_ref[at + k : at + k + 1] for k in range(shared)],
            )
        )
    added = node_sums(
        [nodes_ref[k : k + 1] for k in range(2 * shared)],
        [found[0][c] + found[1][c] for c in range(3)],
        tops,
    )
    added += jnp.concatenate(pieces[1], axis=0)
    for c in range(3):
        add_halves(total, added, c, tops)
    out_ref[...] = total[...].astype(bf16)


def accel_kernel(mass_ref, *refs):
    out_ref = refs[-1]
    terms = [ref[...].astype(f32) for ref in refs[:-1]]
    while len(terms) > 1:
        terms = [a + b for a, b in zip(terms[::2], terms[1::2])]
    size = mass_ref.shape[0]
    for c in range(3):
        at = slice(c * size, (c + 1) * size)
        out_ref[at] = terms[0][at] / mass_ref[...]


def swapped(block, start):
    lows = range(start, lax.axis_size("dom") - 1, 2)
    return lax.ppermute(block, "dom", [(s, s + 1) for s in lows] + [(s + 1, s) for s in lows])


def from_mate(block, distance):
    return lax.ppermute(
        block, "rep", [(i, i ^ distance) for i in range(lax.axis_size("rep"))]
    )


def across(block, distance):
    return lax.ppermute(
        block, "dom", [(s, s ^ distance) for s in range(lax.axis_size("dom"))]
    )


def on_device(
    coords,
    disp,
    mass,
    stiffness,
    elem_nodes,
    modulus,
    surf_nodes,
    block_region,
    face_pos,
    face_normal,
    tile_slot,
    tile_face,
    tile_weight,
    shared_lo,
    shared_hi,
):
    parts = lax.axis_size("dom")
    assert lax.axis_size("rep") == 4
    nodes_all = disp.shape[2]
    nblk = surf_nodes.shape[1]
    tiles = tile_slot.shape[1]
    cap = max(2, 2 * nblk // parts)
    rows = (3 * cap + 1 + 15) // 16 * 16
    force_rows = (3 * tiles + 15) // 16 * 16
    node_array = jax.ShapeDtypeStruct((3 * nodes_all // lanes, lanes), f32)
    mass_array = jax.ShapeDtypeStruct((nodes_all // lanes, lanes), f32)
    coords = coords.reshape(node_array.shape)
    disp = disp.reshape(node_array.shape)
    mass = mass.reshape(mass_array.shape)
    shared_lo = shared_lo.reshape(-1, lanes)
    shared_hi = shared_hi.reshape(-1, lanes)
    shared = shared_lo.shape[0]
    payload = jax.ShapeDtypeStruct((nblk + (shared + 8) // 8 * 8 + 4 * shared, lanes), f32)

    outgoing = call(
        functools.partial(pack_kernel, cap),
        jax.ShapeDtypeStruct((parts, rows, lanes), bf16),
        [hbm] * 5,
        vmem,
        [
            pltpu.VMEM((nblk // cap, rows, lanes), f32),
            pltpu.SMEM(block_region.shape, jnp.int32),
            pltpu.SMEM(tile_slot.shape, jnp.int32),
            pltpu.VMEM(coords.shape, f32),
            pltpu.VMEM(disp.shape, f32),
            pltpu.VMEM(surf_nodes.shape, jnp.int32),
            pltpu.SemaphoreType.DMA((5,)),
        ],
        1 << 30,
        60,
    )(block_region, tile_slot, coords, disp, surf_nodes)
    arrived = lax.all_to_all(outgoing, "dom", split_axis=0, concat_axis=0, tiled=True)

    part = call(
        element_kernel,
        node_array,
        [vmem] * 4,
        vmem,
        [
            pltpu.VMEM((24, modulus.shape[1]), f32),
            pltpu.VMEM((3 * nodes_all // wide, wide), f32),
        ],
        1 << 32,
    )(disp, stiffness, modulus, elem_nodes)
    first, second, tile_ids = call(
        payload_kernel,
        (payload, payload, jax.ShapeDtypeStruct((2, tiles), jnp.int32)),
        [smem] * 2 + [vmem] * 6,
        (vmem, vmem, smem),
        [],
        1 << 28,
    )(tile_slot, tile_face, part, mass, shared_lo, shared_hi, surf_nodes, block_region)
    first, second = swapped(first, 0), swapped(second, 1)
    arrived, part = lax.optimization_barrier((arrived, part))
    forces, slots = call(
        functools.partial(tile_kernel, cap),
        (
            jax.ShapeDtypeStruct((force_rows, lanes), bf16),
            jax.ShapeDtypeStruct((parts, lanes), jnp.int32),
        ),
        [smem] + [vmem] * 4,
        (vmem, vmem),
        [pltpu.VMEM((parts * rows, lanes), f32)],
        1 << 28,
    )(
        tile_ids,
        arrived,
        jnp.swapaxes(face_pos, 1, 2),
        jnp.swapaxes(face_normal, 1, 2),
        tile_weight,
    )
    part, mass, surf, nodes, regions = call(
        neighbour_kernel,
        (
            node_array,
            mass_array,
            jax.ShapeDtypeStruct((3 * nblk, lanes), jnp.int32),
            jax.ShapeDtypeStruct((4 * shared, lanes), jnp.int32),
            jax.ShapeDtypeStruct((3, nblk), jnp.int32),
        ),
        [vmem] * 8,
        (vmem,) * 5,
        [],
        1 << 26,
    )(part, mass, shared_lo, shared_hi, surf_nodes, block_region, first, second)
    picks = call(
        functools.partial(list_kernel, cap, tiles, force_rows),
        jax.ShapeDtypeStruct((1, parts * tiles + 16), jnp.int32),
        [smem, smem],
        smem,
        [pltpu.SMEM((3 * parts,), jnp.int32)],
        1 << 24,
    )(slots, regions)
    held, distance = forces, 1
    while 4 * distance < parts:
        other, picks = lax.optimization_barrier((across(held, distance), picks))
        held = jnp.concatenate([held, other], axis=0)
        distance *= 2
    back = [held] + [across(held, d) for d in range(distance, parts, distance)]
    own = call(
        functools.partial(contact_kernel, tiles),
        jax.ShapeDtypeStruct(node_array.shape, bf16),
        [smem] + [vmem] * (3 + len(back)),
        vmem,
        [
            pltpu.VMEM((parts * force_rows, lanes), f32),
            pltpu.VMEM((9 * nodes_all // wide, wide), f32),
            pltpu.VMEM(node_array.shape, f32),
        ],
        1 << 28,
    )(picks, surf, nodes, part, *back)
    accel = call(accel_kernel, node_array, [vmem] * 5, vmem, [], 1 << 24)(
        mass, own, *[from_mate(own, k) for k in (1, 2, 3)]
    )
    return accel.reshape(1, 3, nodes_all)


def solution(mesh):
    in_specs = (
        P("dom", None, None),
        P("dom", None, None),
        P("dom", None),
        P(),
        P("dom", None, "rep"),
        P("dom", "rep"),
        P("dom", None, None),
        P("dom", None),
        P("dom", None, None, None),
        P("dom", None, None, None),
        P("dom", "rep"),
        P("dom", "rep"),
        P("dom", "rep", None, None),
        P("dom", None),
        P("dom", None),
    )
    out_specs = P("dom", None, None)
    return jax.shard_map(
        on_device, mesh=mesh, in_specs=in_specs, out_specs=out_specs, check_vma=False
    )
```

```python
import functools

import jax
import jax.numpy as jnp
from jax import lax
from jax.experimental import pallas as pl
from jax.experimental.pallas import tpu as pltpu
from jax.sharding import PartitionSpec as P

penalty = 4.0
lanes = 128
wide = 256
code_bits = 12
code = 1 << code_bits
vmem = pl.BlockSpec(memory_space=pltpu.VMEM)
smem = pl.BlockSpec(memory_space=pltpu.SMEM)
hbm = pl.BlockSpec(memory_space=pltpu.HBM)
f32 = jnp.float32
bf16 = jnp.bfloat16


def call(body, out_shape, in_specs, out_specs, scratch, flops, vmem_mib=32):
    return pl.pallas_call(
        body,
        out_shape=out_shape,
        in_specs=in_specs,
        out_specs=out_specs,
        scratch_shapes=scratch,
        compiler_params=pltpu.CompilerParams(vmem_limit_bytes=vmem_mib * 1024 * 1024),
        cost_estimate=pl.CostEstimate(flops=flops, bytes_accessed=1 << 20, transcendentals=0),
    )


def one_hot(nodes):
    line = lax.broadcasted_iota(jnp.int32, (wide, lanes), 0).astype(f32).astype(bf16)
    low = [(row & (wide - 1)).astype(f32).astype(bf16) for row in nodes]
    one, zero = jnp.ones((), bf16), jnp.zeros((), bf16)
    return jnp.concatenate([jnp.where(line == row, one, zero) for row in low], axis=1)


def halves(ref, c, tops):
    at = c * 2 * tops
    return jnp.concatenate(
        [ref[pl.ds(at, tops, stride=2)], ref[pl.ds(at + 1, tops, stride=2)]], axis=1
    )


def two_parts(x):
    coarse = x.astype(bf16)
    return [coarse, (x - coarse.astype(f32)).astype(bf16)]


def lookup(tables, nodes):
    tops = tables[0][0].shape[0]
    stacked = jnp.concatenate([part for table in tables for part in table], axis=0)
    found = jnp.dot(stacked, one_hot(nodes), preferred_element_type=f32)
    line = lax.broadcasted_iota(jnp.int32, (tops, lanes), 0)
    values = [[] for _ in tables]
    for i, row in enumerate(nodes):
        match = line == (row >> 8)
        at = 0
        for c, table in enumerate(tables):
            here = found[at : at + tops, i * lanes : (i + 1) * lanes]
            for p in range(1, len(table)):
                here += found[at + p * tops : at + (p + 1) * tops, i * lanes : (i + 1) * lanes]
            at += len(table) * tops
            values[c].append(jnp.sum(jnp.where(match, here, 0.0), axis=0, keepdims=True))
    return values


def node_sums(nodes, values, tops, parts=2):
    line = lax.broadcasted_iota(jnp.int32, (tops, lanes), 0)
    comps = len(values)
    left = []
    for i, row in enumerate(nodes):
        match = line == (row >> 8)
        pieces = [v[i] for v in values]
        if parts == 2:
            coarse = [v.astype(bf16).astype(f32) for v in pieces]
            pieces = coarse + [v - w for v, w in zip(pieces, coarse)]
        left.append(
            jnp.concatenate([jnp.where(match, v, 0.0).astype(bf16) for v in pieces], axis=0)
        )
    both = lax.dot_general(
        jnp.concatenate(left, axis=1),
        one_hot(nodes),
        (((1,), (1,)), ((), ())),
        preferred_element_type=f32,
    )
    return both if parts == 1 else both[: comps * tops] + both[comps * tops :]


def add_halves(ref, sums, c, tops, row=None):
    at = (c if row is None else row) * 2 * tops
    for half in range(2):
        ref[pl.ds(at + half, tops, stride=2)] += sums[
            c * tops : (c + 1) * tops, half * lanes : (half + 1) * lanes
        ]


def pack_kernel(
    cap, region_hbm, slot_hbm, coords_hbm, disp_hbm, surf_hbm, out_ref,
    stage, region_ref, slot_ref, coords_ref, disp_ref, surf_ref, sems,
):
    sources = (coords_hbm, disp_hbm, slot_hbm, surf_hbm, region_hbm)
    places = (coords_ref, disp_ref, slot_ref, surf_ref, region_ref)
    copies = [
        pltpu.make_async_copy(a, b, sems.at[i]) for i, (a, b) in enumerate(zip(sources, places))
    ]
    for copy in copies:
        copy.start()
    parts, rows, _ = out_ref.shape
    nblk = surf_ref.shape[1]
    tiles = slot_ref.shape[1]
    tops = coords_ref.shape[0] // 6
    for copy in copies:
        copy.wait()
    rest = (rows - 3 * cap, lanes)
    lane = lax.broadcasted_iota(jnp.int32, rest, 1)
    line = lax.broadcasted_iota(jnp.int32, rest, 0)
    tail = jnp.zeros(rest, f32)
    for t in range(tiles):
        tail = jnp.where((lane == t) & (line == 0), slot_ref[0, t].astype(f32), tail)
    for q in range(nblk // cap):
        stage[q, 3 * cap :] = tail
    empty = jnp.concatenate([jnp.zeros((3 * cap, lanes), f32), tail], axis=0).astype(bf16)
    for j in range(parts):
        out_ref[j] = empty
    tables = [
        [(halves(coords_ref, c, tops) + halves(disp_ref, c, tops)).astype(bf16)] for c in range(3)
    ]
    size = min(cap, 8)
    for first in range(0, nblk, 8):
        values = lookup(tables, [surf_ref[0, first + i : first + i + 1] for i in range(8)])
        for b in range(first, first + 8, size):
            for c in range(3):
                at = c * cap + b % cap
                stage[b // cap, at : at + size] = jnp.concatenate(
                    values[c][b - first : b - first + size], axis=0
                )
    for q in range(nblk // cap):
        out_ref[region_ref[0, q * cap]] = stage[q].astype(bf16)


def element_kernel(disp_ref, stiff_ref, modulus_ref, nodes_ref, out_ref, local, sums):
    corners, count = nodes_ref.shape[1:]
    tops = disp_ref.shape[0] // 6
    tables = [two_parts(halves(disp_ref, c, tops)) for c in range(3)]
    cuts = [slice(g * lanes, (g + 1) * lanes) for g in range(count // lanes)]
    nodes = [[nodes_ref[0, a : a + 1, cut] for a in range(corners)] for cut in cuts]
    for cut, here in zip(cuts, nodes):
        values = lookup(tables, here)
        for c in range(3):
            local[c * corners : (c + 1) * corners, cut] = jnp.concatenate(values[c], axis=0)
    force = jnp.dot(
        stiff_ref[...], local[...], precision=lax.Precision.HIGHEST, preferred_element_type=f32
    )
    local[...] = -(force * modulus_ref[...])
    for g, (cut, here) in enumerate(zip(cuts, nodes)):
        values = [
            [local[c * corners + a : c * corners + a + 1, cut] for a in range(corners)]
            for c in range(3)
        ]
        added = node_sums(here, values, tops)
        sums[...] = added if g == 0 else sums[...] + added
    out_ref[...] = jnp.zeros_like(out_ref)
    for c in range(3):
        add_halves(out_ref, sums[...], c, tops)


def payload_kernel(
    slot_ref, face_ref, part_ref, mass_ref, lo_ref, hi_ref, surf_ref, region_ref,
    first_ref, second_ref, tiles_ref,
):
    for t in range(slot_ref.shape[1]):
        tiles_ref[0, t] = slot_ref[0, t]
        tiles_ref[1, t] = face_ref[0, t]
    even = lax.axis_index("dom") % 2 == 0
    tops = mass_ref.shape[0] // 2
    nblk = surf_ref.shape[1]
    shared = lo_ref.shape[0]
    head = first_ref.shape[0] - 4 * shared
    tables = [two_parts(halves(part_ref, c, tops)) for c in range(3)]
    tables.append(two_parts(halves(mass_ref, 0, tops)))
    values = lookup(tables, [ref[k : k + 1] for ref in (lo_ref, hi_ref) for k in range(shared)])
    lower_list, upper_list = lo_ref[...].astype(f32), hi_ref[...].astype(f32)
    for ref, up in ((first_ref, even), (second_ref, jnp.logical_not(even))):
        ref[:nblk] = surf_ref[0].astype(f32)
        ref[nblk : nblk + shared] = jnp.where(up, upper_list, lower_list)
        ref[nblk + shared : nblk + shared + 1] = region_ref[...].astype(f32)
        ref[nblk + shared + 1 : head] = jnp.zeros((head - nblk - shared - 1, lanes), f32)
        for c in range(4):
            lower = jnp.concatenate(values[c][:shared], axis=0)
            upper = jnp.concatenate(values[c][shared:], axis=0)
            ref[head + c * shared : head + (c + 1) * shared] = jnp.where(up, upper, lower)


def neighbour_kernel(
    part_ref, mass_ref, lo_ref, hi_ref, own_surf_ref, region_ref, first_ref, second_ref,
    out_ref, out_mass_ref, surf_ref, nodes_ref, regions_ref,
):
    even = lax.axis_index("dom") % 2 == 0
    tops = mass_ref.shape[0] // 2
    nblk = own_surf_ref.shape[1]
    nodes_all = mass_ref.shape[0] * lanes
    shared = lo_ref.shape[0]
    head = first_ref.shape[0] - 4 * shared
    out_ref[...] = part_ref[...]
    out_mass_ref[...] = mass_ref[...]
    first, second = first_ref[...], second_ref[...]
    packs = [jnp.where(even, second, first), jnp.where(even, first, second)]
    for i, pack in enumerate(packs):
        surf_ref[2 * i * nblk : (2 * i + 1) * nblk] = pack[:nblk].astype(jnp.int32) + 2 * i * nodes_all
        nodes_ref[(2 + i) * shared : (3 + i) * shared] = pack[nblk : nblk + shared].astype(jnp.int32)
        regions_ref[2 * i : 2 * i + 1] = pack[nblk + shared : nblk + shared + 1].astype(jnp.int32)
    surf_ref[nblk : 2 * nblk] = own_surf_ref[0] + nodes_all
    regions_ref[1:2] = region_ref[...]
    nodes_ref[:shared] = lo_ref[...]
    nodes_ref[shared : 2 * shared] = hi_ref[...]
    nodes = [ref[k : k + 1] for ref in (lo_ref, hi_ref) for k in range(shared)]
    values = [
        [pack[head + c * shared + k : head + c * shared + k + 1] for pack in packs for k in range(shared)]
        for c in range(4)
    ]
    sums = node_sums(nodes, values, tops)
    for c in range(3):
        add_halves(out_ref, sums, c, tops)
    add_halves(out_mass_ref, sums, 3, tops, 0)


def tile_kernel(cap, tiles_ref, got_ref, pos_ref, normal_ref, weight_ref, out_ref, slots_ref, flat):
    parts, rows, _ = got_ref.shape
    tiles = tiles_ref.shape[1]
    shift = cap.bit_length() - 1
    faces = [tiles_ref[1, t] for t in range(tiles)]
    starts = [(tiles_ref[0, t] >> shift) * rows + (tiles_ref[0, t] & (cap - 1)) for t in range(tiles)]
    for j in range(parts):
        flat[j * rows : (j + 1) * rows] = got_ref[j].astype(f32)
    slots_ref[...] = jnp.concatenate(
        [flat[j * rows + 3 * cap : j * rows + 3 * cap + 1] for j in range(parts)], axis=0
    ).astype(jnp.int32)
    x = jnp.concatenate(
        [flat[pl.ds(at + c * cap, 1)] for c in range(3) for at in starts], axis=0
    )
    weights = weight_ref[0].reshape(tiles * lanes, lanes)
    crossed = lax.dot_general(
        x.astype(bf16), weights, (((1,), (1,)), ((), ())), preferred_element_type=f32
    )
    line = lax.broadcasted_iota(jnp.int32, (tiles, lanes), 0)
    gap = jnp.zeros((tiles, lanes), f32)
    normals = []
    for c in range(3):
        interp = jnp.zeros((tiles, lanes), f32)
        for t in range(tiles):
            here = crossed[c * tiles : (c + 1) * tiles, t * lanes : (t + 1) * lanes]
            interp = jnp.where(line == t, here, interp)
        normal = jnp.concatenate([normal_ref[0, c, pl.ds(f, 1)] for f in faces], axis=0)
        pos = jnp.concatenate([pos_ref[0, c, pl.ds(f, 1)] for f in faces], axis=0)
        gap += normal * (interp - pos)
        normals.append(normal)
    pressure = penalty * jnp.maximum(-gap, 0.0)
    push = [pressure * normal for normal in normals]
    spread = jnp.concatenate(
        [
            jnp.concatenate([jnp.where(line == t, p, 0.0) for p in push], axis=0).astype(bf16)
            for t in range(tiles)
        ],
        axis=1,
    )
    forces = jnp.dot(spread, weights, preferred_element_type=f32).astype(bf16)
    pad = out_ref.shape[0] - forces.shape[0]
    if pad:
        forces = jnp.concatenate([forces, jnp.zeros((pad, lanes), bf16)], axis=0)
    out_ref[...] = forces


def list_kernel(cap, tiles, force_rows, slots_ref, regions_ref, list_ref, run_of):
    parts = slots_ref.shape[0]
    nblk = regions_ref.shape[1]
    shift = cap.bit_length() - 1
    me = lax.axis_index("dom")
    for p in range(3):
        for q in range(nblk // cap):
            run_of[p * parts + regions_ref[p, q * cap]] = p * nblk + q * cap

    def pick(place, filled):
        j = me ^ place
        slots = [slots_ref[j, t] for t in range(tiles)]
        which = [(slot >> shift) - me + 1 for slot in slots]
        kept = [(p >= 0) & (p <= 2) for p in which]
        runs = [run_of[jnp.where(own, p, 0) * parts + j] for own, p in zip(kept, which)]
        places = []
        for own in kept:
            places.append(filled)
            filled = filled + jnp.where(own, 1, 0)
        for t in range(tiles):
            entry = (place * force_rows + t) * code + (slots[t] & (cap - 1)) + runs[t]
            list_ref[0, places[t]] = entry
        return filled

    filled = lax.fori_loop(0, parts, pick, jnp.int32(0))
    for i in range(8):
        list_ref[0, filled + i] = 0
    list_ref[0, list_ref.shape[1] - 1] = filled


def contact_kernel(tiles, list_ref, surf_ref, nodes_ref, part_ref, *refs):
    back_refs, out_ref, back, sums, total = refs[:-4], refs[-4], refs[-3], refs[-2], refs[-1]
    size = back_refs[0].shape[0]
    tops = part_ref.shape[0] // 6
    shared = nodes_ref.shape[0] // 4
    total[...] = part_ref[...]
    for i, ref in enumerate(back_refs):
        back[i * size : (i + 1) * size] = ref[...].astype(f32)
    filled = list_ref[0, list_ref.shape[1] - 1]
    sums[...] = jnp.zeros_like(sums)

    def spread(g, _):
        nodes, values = [], [[], [], []]
        for i in range(8):
            entry = list_ref[0, g * 8 + i]
            row = surf_ref[pl.ds(entry & (code - 1), 1)]
            nodes.append(jnp.where(g * 8 + i < filled, row, -1))
            for c in range(3):
                values[c].append(back[pl.ds((entry >> code_bits) + c * tiles, 1)])
        sums[...] += node_sums(nodes, values, 3 * tops, 1)
        return 0

    lax.fori_loop(0, (filled + 7) // 8, spread, 0)
    pieces = [[sums[(c * 3 + p) * tops : (c * 3 + p + 1) * tops] for c in range(3)] for p in range(3)]
    found = []
    for p in (0, 2):
        at = (2 + p // 2) * shared
        found.append(
            lookup(
                [two_parts(piece) for piece in pieces[p]],
                [nodes_ref[at + k : at + k + 1] for k in range(shared)],
            )
        )
    added = node_sums(
        [nodes_ref[k : k + 1] for k in range(2 * shared)],
        [found[0][c] + found[1][c] for c in range(3)],
        tops,
    )
    added += jnp.concatenate(pieces[1], axis=0)
    for c in range(3):
        add_halves(total, added, c, tops)
    out_ref[...] = total[...].astype(bf16)


def accel_kernel(mass_ref, *refs):
    out_ref = refs[-1]
    terms = [ref[...].astype(f32) for ref in refs[:-1]]
    while len(terms) > 1:
        terms = [a + b for a, b in zip(terms[::2], terms[1::2])]
    size = mass_ref.shape[0]
    for c in range(3):
        at = slice(c * size, (c + 1) * size)
        out_ref[at] = terms[0][at] / mass_ref[...]


def swapped(block, start):
    lows = range(start, lax.axis_size("dom") - 1, 2)
    return lax.ppermute(block, "dom", [(s, s + 1) for s in lows] + [(s + 1, s) for s in lows])


def from_mate(block, distance):
    return lax.ppermute(
        block, "rep", [(i, i ^ distance) for i in range(lax.axis_size("rep"))]
    )


def across(block, distance):
    return lax.ppermute(
        block, "dom", [(s, s ^ distance) for s in range(lax.axis_size("dom"))]
    )


def on_device(
    coords,
    disp,
    mass,
    stiffness,
    elem_nodes,
    modulus,
    surf_nodes,
    block_region,
    face_pos,
    face_normal,
    tile_slot,
    tile_face,
    tile_weight,
    shared_lo,
    shared_hi,
):
    parts = lax.axis_size("dom")
    assert lax.axis_size("rep") == 4
    nodes_all = disp.shape[2]
    nblk = surf_nodes.shape[1]
    tiles = tile_slot.shape[1]
    cap = max(2, 2 * nblk // parts)
    rows = (3 * cap + 1 + 15) // 16 * 16
    force_rows = (3 * tiles + 15) // 16 * 16
    node_array = jax.ShapeDtypeStruct((3 * nodes_all // lanes, lanes), f32)
    mass_array = jax.ShapeDtypeStruct((nodes_all // lanes, lanes), f32)
    coords = coords.reshape(node_array.shape)
    disp = disp.reshape(node_array.shape)
    mass = mass.reshape(mass_array.shape)
    shared_lo = shared_lo.reshape(-1, lanes)
    shared_hi = shared_hi.reshape(-1, lanes)
    shared = shared_lo.shape[0]
    payload = jax.ShapeDtypeStruct((nblk + (shared + 8) // 8 * 8 + 4 * shared, lanes), f32)

    outgoing = call(
        functools.partial(pack_kernel, cap),
        jax.ShapeDtypeStruct((parts, rows, lanes), bf16),
        [hbm] * 5,
        vmem,
        [
            pltpu.VMEM((nblk // cap, rows, lanes), f32),
            pltpu.SMEM(block_region.shape, jnp.int32),
            pltpu.SMEM(tile_slot.shape, jnp.int32),
            pltpu.VMEM(coords.shape, f32),
            pltpu.VMEM(disp.shape, f32),
            pltpu.VMEM(surf_nodes.shape, jnp.int32),
            pltpu.SemaphoreType.DMA((5,)),
        ],
        1 << 30,
        60,
    )(block_region, tile_slot, coords, disp, surf_nodes)
    arrived = lax.all_to_all(outgoing, "dom", split_axis=0, concat_axis=0, tiled=True)

    part = call(
        element_kernel,
        node_array,
        [vmem] * 4,
        vmem,
        [
            pltpu.VMEM((24, modulus.shape[1]), f32),
            pltpu.VMEM((3 * nodes_all // wide, wide), f32),
        ],
        1 << 32,
    )(disp, stiffness, modulus, elem_nodes)
    first, second, tile_ids = call(
        payload_kernel,
        (payload, payload, jax.ShapeDtypeStruct((2, tiles), jnp.int32)),
        [smem] * 2 + [vmem] * 6,
        (vmem, vmem, smem),
        [],
        1 << 28,
    )(tile_slot, tile_face, part, mass, shared_lo, shared_hi, surf_nodes, block_region)
    first = swapped(first, 0)
    arrived, part = lax.optimization_barrier((arrived, part))
    forces, slots = call(
        functools.partial(tile_kernel, cap),
        (
            jax.ShapeDtypeStruct((force_rows, lanes), bf16),
            jax.ShapeDtypeStruct((parts, lanes), jnp.int32),
        ),
        [smem] + [vmem] * 4,
        (vmem, vmem),
        [pltpu.VMEM((parts * rows, lanes), f32)],
        1 << 28,
    )(
        tile_ids,
        arrived,
        jnp.swapaxes(face_pos, 1, 2),
        jnp.swapaxes(face_normal, 1, 2),
        tile_weight,
    )
    forces, second = lax.optimization_barrier((forces, second))
    held, distance = forces, 1
    while 4 * distance < parts:
        held = jnp.concatenate([held, across(held, distance)], axis=0)
        distance *= 2
    back = [held] + [across(held, d) for d in range(distance, parts, distance)]
    second = swapped(second, 1)
    part, mass, surf, nodes, regions = call(
        neighbour_kernel,
        (
            node_array,
            mass_array,
            jax.ShapeDtypeStruct((3 * nblk, lanes), jnp.int32),
            jax.ShapeDtypeStruct((4 * shared, lanes), jnp.int32),
            jax.ShapeDtypeStruct((3, nblk), jnp.int32),
        ),
        [vmem] * 8,
        (vmem,) * 5,
        [],
        1 << 26,
    )(part, mass, shared_lo, shared_hi, surf_nodes, block_region, first, second)
    picks = call(
        functools.partial(list_kernel, cap, tiles, force_rows),
        jax.ShapeDtypeStruct((1, parts * tiles + 16), jnp.int32),
        [smem, smem],
        smem,
        [pltpu.SMEM((3 * parts,), jnp.int32)],
        1 << 24,
    )(slots, regions)
    own = call(
        functools.partial(contact_kernel, tiles),
        jax.ShapeDtypeStruct(node_array.shape, bf16),
        [smem] + [vmem] * (3 + len(back)),
        vmem,
        [
            pltpu.VMEM((parts * force_rows, lanes), f32),
            pltpu.VMEM((9 * nodes_all // wide, wide), f32),
            pltpu.VMEM(node_array.shape, f32),
        ],
        1 << 28,
    )(picks, surf, nodes, part, *back)
    accel = call(accel_kernel, node_array, [vmem] * 5, vmem, [], 1 << 24)(
        mass, own, *[from_mate(own, k) for k in (1, 2, 3)]
    )
    return accel.reshape(1, 3, nodes_all)


def solution(mesh):
    in_specs = (
        P("dom", None, None),
        P("dom", None, None),
        P("dom", None),
        P(),
        P("dom", None, "rep"),
        P("dom", "rep"),
        P("dom", None, None),
        P("dom", None),
        P("dom", None, None, None),
        P("dom", None, None, None),
        P("dom", "rep"),
        P("dom", "rep"),
        P("dom", "rep", None, None),
        P("dom", None),
        P("dom", None),
    )
    out_specs = P("dom", None, None)
    return jax.shard_map(
        on_device, mesh=mesh, in_specs=in_specs, out_specs=out_specs, check_vma=False
    )
```

```python
import functools

import jax
import jax.numpy as jnp
from jax import lax
from jax.experimental import pallas as pl
from jax.experimental.pallas import tpu as pltpu
from jax.sharding import PartitionSpec as P

penalty = 4.0
lanes = 128
wide = 256
code_bits = 12
code = 1 << code_bits
vmem = pl.BlockSpec(memory_space=pltpu.VMEM)
smem = pl.BlockSpec(memory_space=pltpu.SMEM)
hbm = pl.BlockSpec(memory_space=pltpu.HBM)
f32 = jnp.float32
bf16 = jnp.bfloat16


def call(body, out_shape, in_specs, out_specs, scratch, flops, vmem_mib=32):
    return pl.pallas_call(
        body,
        out_shape=out_shape,
        in_specs=in_specs,
        out_specs=out_specs,
        scratch_shapes=scratch,
        compiler_params=pltpu.CompilerParams(vmem_limit_bytes=vmem_mib * 1024 * 1024),
        cost_estimate=pl.CostEstimate(flops=flops, bytes_accessed=1 << 20, transcendentals=0),
    )


def rows_like(count):
    return lax.broadcasted_iota(jnp.int32, (count, lanes), 0).astype(f32).astype(bf16)


def pick(match, values):
    return jnp.where(match, values, jnp.zeros((), bf16))


def one_hot(nodes):
    line = rows_like(wide)
    low = [(row & (wide - 1)).astype(f32).astype(bf16) for row in nodes]
    return jnp.concatenate([pick(line == row, jnp.ones((), bf16)) for row in low], axis=1)


def upper(nodes):
    return [(row >> 8).astype(f32).astype(bf16) for row in nodes]


def halves(ref, c, tops):
    at = c * 2 * tops
    return jnp.concatenate(
        [ref[pl.ds(at, tops, stride=2)], ref[pl.ds(at + 1, tops, stride=2)]], axis=1
    )


def two_parts(x):
    coarse = x.astype(bf16)
    return [coarse, (x - coarse.astype(f32)).astype(bf16)]


def lookup(tables, nodes):
    tops = tables[0][0].shape[0]
    blocks = [part for table in tables for part in table]
    stacked = jnp.concatenate(blocks, axis=0)
    found = jnp.dot(stacked, one_hot(nodes), preferred_element_type=f32).astype(bf16)
    line = rows_like(tops)
    masked = []
    for i, top in enumerate(upper(nodes)):
        match = line == top
        cut = slice(i * lanes, (i + 1) * lanes)
        masked.append(
            jnp.concatenate(
                [pick(match, found[b * tops : (b + 1) * tops, cut]) for b in range(len(blocks))], axis=0
            )
        )
    size = (8, len(blocks) * tops)
    owner = lax.broadcasted_iota(jnp.int32, size, 1) // (len(tables[0]) * tops)
    same = owner == lax.broadcasted_iota(jnp.int32, size, 0)
    chosen = jnp.dot(
        jnp.where(same, 1.0, 0.0).astype(bf16),
        jnp.concatenate(masked, axis=1),
        preferred_element_type=f32,
    )
    return [
        [chosen[c : c + 1, i * lanes : (i + 1) * lanes] for i in range(len(nodes))]
        for c in range(len(tables))
    ]


def node_sums(nodes, values, tops, parts=2):
    line = rows_like(tops)
    comps = len(values)
    left = []
    for i, top in enumerate(upper(nodes)):
        match = line == top
        pieces = [v[i].astype(bf16) for v in values]
        if parts == 2:
            pieces += [(v[i] - w.astype(f32)).astype(bf16) for v, w in zip(values, pieces)]
        left.append(jnp.concatenate([pick(match, piece) for piece in pieces], axis=0))
    both = lax.dot_general(
        jnp.concatenate(left, axis=1),
        one_hot(nodes),
        (((1,), (1,)), ((), ())),
        preferred_element_type=f32,
    )
    return both if parts == 1 else both[: comps * tops] + both[comps * tops :]


def add_halves(ref, sums, c, tops, row=None):
    at = (c if row is None else row) * 2 * tops
    for half in range(2):
        ref[pl.ds(at + half, tops, stride=2)] += sums[
            c * tops : (c + 1) * tops, half * lanes : (half + 1) * lanes
        ]


def pack_kernel(
    cap, region_hbm, slot_hbm, coords_hbm, disp_hbm, surf_hbm, out_ref,
    stage, region_ref, slot_ref, coords_ref, disp_ref, surf_ref, sems,
):
    sources = (coords_hbm, disp_hbm, slot_hbm, surf_hbm, region_hbm)
    places = (coords_ref, disp_ref, slot_ref, surf_ref, region_ref)
    copies = [
        pltpu.make_async_copy(a, b, sems.at[i]) for i, (a, b) in enumerate(zip(sources, places))
    ]
    for copy in copies:
        copy.start()
    parts, rows, _ = out_ref.shape
    nblk = surf_ref.shape[1]
    tiles = slot_ref.shape[1]
    tops = coords_ref.shape[0] // 6
    for copy in copies:
        copy.wait()
    rest = (rows - 3 * cap, lanes)
    lane = lax.broadcasted_iota(jnp.int32, rest, 1)
    line = lax.broadcasted_iota(jnp.int32, rest, 0)
    tail = jnp.zeros(rest, f32)
    for t in range(tiles):
        tail = jnp.where((lane == t) & (line == 0), slot_ref[0, t].astype(f32), tail)
    for q in range(nblk // cap):
        stage[q, 3 * cap :] = tail
    empty = jnp.concatenate([jnp.zeros((3 * cap, lanes), f32), tail], axis=0).astype(bf16)
    for j in range(parts):
        out_ref[j] = empty
    tables = [
        [(halves(coords_ref, c, tops) + halves(disp_ref, c, tops)).astype(bf16)] for c in range(3)
    ]
    size = min(cap, 8)
    for first in range(0, nblk, 8):
        values = lookup(tables, [surf_ref[0, first + i : first + i + 1] for i in range(8)])
        for b in range(first, first + 8, size):
            for c in range(3):
                at = c * cap + b % cap
                stage[b // cap, at : at + size] = jnp.concatenate(
                    values[c][b - first : b - first + size], axis=0
                )
    for q in range(nblk // cap):
        out_ref[region_ref[0, q * cap]] = stage[q].astype(bf16)


def element_kernel(disp_ref, stiff_ref, modulus_ref, nodes_ref, out_ref, local, sums):
    corners, count = nodes_ref.shape[1:]
    tops = disp_ref.shape[0] // 6
    tables = [two_parts(halves(disp_ref, c, tops)) for c in range(3)]
    cuts = [slice(g * lanes, (g + 1) * lanes) for g in range(count // lanes)]
    nodes = [[nodes_ref[0, a : a + 1, cut] for a in range(corners)] for cut in cuts]
    for cut, here in zip(cuts, nodes):
        values = lookup(tables, here)
        for c in range(3):
            local[c * corners : (c + 1) * corners, cut] = jnp.concatenate(values[c], axis=0)
    force = jnp.dot(
        stiff_ref[...], local[...], precision=lax.Precision.HIGHEST, preferred_element_type=f32
    )
    local[...] = -(force * modulus_ref[...])
    for g, (cut, here) in enumerate(zip(cuts, nodes)):
        values = [
            [local[c * corners + a : c * corners + a + 1, cut] for a in range(corners)]
            for c in range(3)
        ]
        added = node_sums(here, values, tops)
        sums[...] = added if g == 0 else sums[...] + added
    out_ref[...] = jnp.zeros_like(out_ref)
    for c in range(3):
        add_halves(out_ref, sums[...], c, tops)


def payload_kernel(
    slot_ref, face_ref, part_ref, mass_ref, lo_ref, hi_ref, surf_ref, region_ref,
    first_ref, second_ref, tiles_ref,
):
    for t in range(slot_ref.shape[1]):
        tiles_ref[0, t] = slot_ref[0, t]
        tiles_ref[1, t] = face_ref[0, t]
    even = lax.axis_index("dom") % 2 == 0
    tops = mass_ref.shape[0] // 2
    nblk = surf_ref.shape[1]
    shared = lo_ref.shape[0]
    head = first_ref.shape[0] - 4 * shared
    tables = [two_parts(halves(part_ref, c, tops)) for c in range(3)]
    tables.append(two_parts(halves(mass_ref, 0, tops)))
    values = lookup(tables, [ref[k : k + 1] for ref in (lo_ref, hi_ref) for k in range(shared)])
    lower_list, upper_list = lo_ref[...].astype(f32), hi_ref[...].astype(f32)
    for ref, up in ((first_ref, even), (second_ref, jnp.logical_not(even))):
        ref[:nblk] = surf_ref[0].astype(f32)
        ref[nblk : nblk + shared] = jnp.where(up, upper_list, lower_list)
        ref[nblk + shared : nblk + shared + 1] = region_ref[...].astype(f32)
        ref[nblk + shared + 1 : head] = jnp.zeros((head - nblk - shared - 1, lanes), f32)
        for c in range(4):
            below = jnp.concatenate(values[c][:shared], axis=0)
            above = jnp.concatenate(values[c][shared:], axis=0)
            ref[head + c * shared : head + (c + 1) * shared] = jnp.where(up, above, below)


def neighbour_kernel(
    part_ref, mass_ref, lo_ref, hi_ref, own_surf_ref, region_ref, first_ref, second_ref,
    out_ref, out_mass_ref, surf_ref, nodes_ref, regions_ref,
):
    even = lax.axis_index("dom") % 2 == 0
    tops = mass_ref.shape[0] // 2
    nblk = own_surf_ref.shape[1]
    nodes_all = mass_ref.shape[0] * lanes
    shared = lo_ref.shape[0]
    head = first_ref.shape[0] - 4 * shared
    out_ref[...] = part_ref[...]
    out_mass_ref[...] = mass_ref[...]
    first, second = first_ref[...], second_ref[...]
    packs = [jnp.where(even, second, first), jnp.where(even, first, second)]
    for i, pack in enumerate(packs):
        surf_ref[2 * i * nblk : (2 * i + 1) * nblk] = pack[:nblk].astype(jnp.int32) + 2 * i * nodes_all
        nodes_ref[(2 + i) * shared : (3 + i) * shared] = pack[nblk : nblk + shared].astype(jnp.int32)
        regions_ref[2 * i : 2 * i + 1] = pack[nblk + shared : nblk + shared + 1].astype(jnp.int32)
    surf_ref[nblk : 2 * nblk] = own_surf_ref[0] + nodes_all
    regions_ref[1:2] = region_ref[...]
    nodes_ref[:shared] = lo_ref[...]
    nodes_ref[shared : 2 * shared] = hi_ref[...]
    nodes = [ref[k : k + 1] for ref in (lo_ref, hi_ref) for k in range(shared)]
    values = [
        [pack[head + c * shared + k : head + c * shared + k + 1] for pack in packs for k in range(shared)]
        for c in range(4)
    ]
    sums = node_sums(nodes, values, tops)
    for c in range(3):
        add_halves(out_ref, sums, c, tops)
    add_halves(out_mass_ref, sums, 3, tops, 0)


def tile_kernel(cap, tiles_ref, got_ref, pos_ref, normal_ref, weight_ref, out_ref, slots_ref, flat):
    parts, rows, _ = got_ref.shape
    tiles = tiles_ref.shape[1]
    shift = cap.bit_length() - 1
    faces = [tiles_ref[1, t] for t in range(tiles)]
    starts = [(tiles_ref[0, t] >> shift) * rows + (tiles_ref[0, t] & (cap - 1)) for t in range(tiles)]
    for j in range(parts):
        flat[j * rows : (j + 1) * rows] = got_ref[j].astype(f32)
    slots_ref[...] = jnp.concatenate(
        [flat[j * rows + 3 * cap : j * rows + 3 * cap + 1] for j in range(parts)], axis=0
    ).astype(jnp.int32)
    x = jnp.concatenate(
        [flat[pl.ds(at + c * cap, 1)] for c in range(3) for at in starts], axis=0
    )
    weights = weight_ref[0].reshape(tiles * lanes, lanes)
    crossed = lax.dot_general(
        x.astype(bf16), weights, (((1,), (1,)), ((), ())), preferred_element_type=f32
    )
    line = lax.broadcasted_iota(jnp.int32, (tiles, lanes), 0)
    gap = jnp.zeros((tiles, lanes), f32)
    normals = []
    for c in range(3):
        interp = jnp.zeros((tiles, lanes), f32)
        for t in range(tiles):
            here = crossed[c * tiles : (c + 1) * tiles, t * lanes : (t + 1) * lanes]
            interp = jnp.where(line == t, here, interp)
        normal = jnp.concatenate([normal_ref[0, c, pl.ds(f, 1)] for f in faces], axis=0)
        pos = jnp.concatenate([pos_ref[0, c, pl.ds(f, 1)] for f in faces], axis=0)
        gap += normal * (interp - pos)
        normals.append(normal)
    pressure = penalty * jnp.maximum(-gap, 0.0)
    push = [pressure * normal for normal in normals]
    spread = jnp.concatenate(
        [
            jnp.concatenate([jnp.where(line == t, p, 0.0) for p in push], axis=0).astype(bf16)
            for t in range(tiles)
        ],
        axis=1,
    )
    forces = jnp.dot(spread, weights, preferred_element_type=f32).astype(bf16)
    pad = out_ref.shape[0] - forces.shape[0]
    if pad:
        forces = jnp.concatenate([forces, jnp.zeros((pad, lanes), bf16)], axis=0)
    out_ref[...] = forces


def list_kernel(cap, tiles, force_rows, slots_ref, regions_ref, list_ref, run_of):
    parts = slots_ref.shape[0]
    nblk = regions_ref.shape[1]
    shift = cap.bit_length() - 1
    me = lax.axis_index("dom")
    for p in range(3):
        for q in range(nblk // cap):
            run_of[p * parts + regions_ref[p, q * cap]] = p * nblk + q * cap

    def take(place, filled):
        j = me ^ place
        slots = [slots_ref[j, t] for t in range(tiles)]
        which = [(slot >> shift) - me + 1 for slot in slots]
        kept = [(p >= 0) & (p <= 2) for p in which]
        runs = [run_of[jnp.where(own, p, 0) * parts + j] for own, p in zip(kept, which)]
        places = []
        for own in kept:
            places.append(filled)
            filled = filled + jnp.where(own, 1, 0)
        for t in range(tiles):
            entry = (place * force_rows + t) * code + (slots[t] & (cap - 1)) + runs[t]
            list_ref[0, places[t]] = entry
        return filled

    filled = lax.fori_loop(0, parts, take, jnp.int32(0))
    for i in range(8):
        list_ref[0, filled + i] = 0
    list_ref[0, list_ref.shape[1] - 1] = filled


def contact_kernel(tiles, list_ref, surf_ref, nodes_ref, part_ref, *refs):
    back_refs, out_ref, back, sums, total = refs[:-4], refs[-4], refs[-3], refs[-2], refs[-1]
    size = back_refs[0].shape[0]
    tops = part_ref.shape[0] // 6
    shared = nodes_ref.shape[0] // 4
    total[...] = part_ref[...]
    for i, ref in enumerate(back_refs):
        back[i * size : (i + 1) * size] = ref[...].astype(f32)
    filled = list_ref[0, list_ref.shape[1] - 1]
    sums[...] = jnp.zeros_like(sums)

    def spread(g, _):
        nodes, values = [], [[], [], []]
        for i in range(8):
            entry = list_ref[0, g * 8 + i]
            row = surf_ref[pl.ds(entry & (code - 1), 1)]
            nodes.append(jnp.where(g * 8 + i < filled, row, -1))
            for c in range(3):
                values[c].append(back[pl.ds((entry >> code_bits) + c * tiles, 1)])
        sums[...] += node_sums(nodes, values, 3 * tops, 1)
        return 0

    lax.fori_loop(0, (filled + 7) // 8, spread, 0)
    pieces = [[sums[(c * 3 + p) * tops : (c * 3 + p + 1) * tops] for c in range(3)] for p in range(3)]
    found = []
    for p in (0, 2):
        at = (2 + p // 2) * shared
        found.append(
            lookup(
                [two_parts(piece) for piece in pieces[p]],
                [nodes_ref[at + k : at + k + 1] for k in range(shared)],
            )
        )
    added = node_sums(
        [nodes_ref[k : k + 1] for k in range(2 * shared)],
        [found[0][c] + found[1][c] for c in range(3)],
        tops,
    )
    added += jnp.concatenate(pieces[1], axis=0)
    for c in range(3):
        add_halves(total, added, c, tops)
    out_ref[...] = total[...].astype(bf16)


def accel_kernel(mass_ref, *refs):
    out_ref = refs[-1]
    terms = [ref[...].astype(f32) for ref in refs[:-1]]
    while len(terms) > 1:
        terms = [a + b for a, b in zip(terms[::2], terms[1::2])]
    size = mass_ref.shape[0]
    for c in range(3):
        at = slice(c * size, (c + 1) * size)
        out_ref[at] = terms[0][at] / mass_ref[...]


def swapped(block, start):
    lows = range(start, lax.axis_size("dom") - 1, 2)
    return lax.ppermute(block, "dom", [(s, s + 1) for s in lows] + [(s + 1, s) for s in lows])


def from_mate(block, distance):
    return lax.ppermute(
        block, "rep", [(i, i ^ distance) for i in range(lax.axis_size("rep"))]
    )


def across(block, distance):
    return lax.ppermute(
        block, "dom", [(s, s ^ distance) for s in range(lax.axis_size("dom"))]
    )


def on_device(
    coords,
    disp,
    mass,
    stiffness,
    elem_nodes,
    modulus,
    surf_nodes,
    block_region,
    face_pos,
    face_normal,
    tile_slot,
    tile_face,
    tile_weight,
    shared_lo,
    shared_hi,
):
    parts = lax.axis_size("dom")
    assert lax.axis_size("rep") == 4
    nodes_all = disp.shape[2]
    nblk = surf_nodes.shape[1]
    tiles = tile_slot.shape[1]
    cap = max(2, 2 * nblk // parts)
    rows = (3 * cap + 1 + 15) // 16 * 16
    force_rows = (3 * tiles + 15) // 16 * 16
    node_array = jax.ShapeDtypeStruct((3 * nodes_all // lanes, lanes), f32)
    mass_array = jax.ShapeDtypeStruct((nodes_all // lanes, lanes), f32)
    coords = coords.reshape(node_array.shape)
    disp = disp.reshape(node_array.shape)
    mass = mass.reshape(mass_array.shape)
    shared_lo = shared_lo.reshape(-1, lanes)
    shared_hi = shared_hi.reshape(-1, lanes)
    shared = shared_lo.shape[0]
    payload = jax.ShapeDtypeStruct((nblk + (shared + 8) // 8 * 8 + 4 * shared, lanes), f32)

    outgoing = call(
        functools.partial(pack_kernel, cap),
        jax.ShapeDtypeStruct((parts, rows, lanes), bf16),
        [hbm] * 5,
        vmem,
        [
            pltpu.VMEM((nblk // cap, rows, lanes), f32),
            pltpu.SMEM(block_region.shape, jnp.int32),
            pltpu.SMEM(tile_slot.shape, jnp.int32),
            pltpu.VMEM(coords.shape, f32),
            pltpu.VMEM(disp.shape, f32),
            pltpu.VMEM(surf_nodes.shape, jnp.int32),
            pltpu.SemaphoreType.DMA((5,)),
        ],
        1 << 30,
        60,
    )(block_region, tile_slot, coords, disp, surf_nodes)
    arrived = lax.all_to_all(outgoing, "dom", split_axis=0, concat_axis=0, tiled=True)

    part = call(
        element_kernel,
        node_array,
        [vmem] * 4,
        vmem,
        [
            pltpu.VMEM((24, modulus.shape[1]), f32),
            pltpu.VMEM((3 * nodes_all // wide, wide), f32),
        ],
        1 << 32,
    )(disp, stiffness, modulus, elem_nodes)
    first, second, tile_ids = call(
        payload_kernel,
        (payload, payload, jax.ShapeDtypeStruct((2, tiles), jnp.int32)),
        [smem] * 2 + [vmem] * 6,
        (vmem, vmem, smem),
        [],
        1 << 28,
    )(tile_slot, tile_face, part, mass, shared_lo, shared_hi, surf_nodes, block_region)
    first = swapped(first, 0)
    arrived, part = lax.optimization_barrier((arrived, part))
    forces, slots = call(
        functools.partial(tile_kernel, cap),
        (
            jax.ShapeDtypeStruct((force_rows, lanes), bf16),
            jax.ShapeDtypeStruct((parts, lanes), jnp.int32),
        ),
        [smem] + [vmem] * 4,
        (vmem, vmem),
        [pltpu.VMEM((parts * rows, lanes), f32)],
        1 << 28,
    )(
        tile_ids,
        arrived,
        jnp.swapaxes(face_pos, 1, 2),
        jnp.swapaxes(face_normal, 1, 2),
        tile_weight,
    )
    forces, second = lax.optimization_barrier((forces, second))
    held, distance = forces, 1
    while 4 * distance < parts:
        held = jnp.concatenate([held, across(held, distance)], axis=0)
        distance *= 2
    back = [held] + [across(held, d) for d in range(distance, parts, distance)]
    second = swapped(second, 1)
    part, mass, surf, nodes, regions = call(
        neighbour_kernel,
        (
            node_array,
            mass_array,
            jax.ShapeDtypeStruct((3 * nblk, lanes), jnp.int32),
            jax.ShapeDtypeStruct((4 * shared, lanes), jnp.int32),
            jax.ShapeDtypeStruct((3, nblk), jnp.int32),
        ),
        [vmem] * 8,
        (vmem,) * 5,
        [],
        1 << 26,
    )(part, mass, shared_lo, shared_hi, surf_nodes, block_region, first, second)
    picks = call(
        functools.partial(list_kernel, cap, tiles, force_rows),
        jax.ShapeDtypeStruct((1, parts * tiles + 16), jnp.int32),
        [smem, smem],
        smem,
        [pltpu.SMEM((3 * parts,), jnp.int32)],
        1 << 24,
    )(slots, regions)
    own = call(
        functools.partial(contact_kernel, tiles),
        jax.ShapeDtypeStruct(node_array.shape, bf16),
        [smem] + [vmem] * (3 + len(back)),
        vmem,
        [
            pltpu.VMEM((parts * force_rows, lanes), f32),
            pltpu.VMEM((9 * nodes_all // wide, wide), f32),
            pltpu.VMEM(node_array.shape, f32),
        ],
        1 << 28,
    )(picks, surf, nodes, part, *back)
    accel = call(accel_kernel, node_array, [vmem] * 5, vmem, [], 1 << 24)(
        mass, own, *[from_mate(own, k) for k in (3, 2, 1)][::-1]
    )
    return accel.reshape(1, 3, nodes_all)


def solution(mesh):
    in_specs = (
        P("dom", None, None),
        P("dom", None, None),
        P("dom", None),
        P(),
        P("dom", None, "rep"),
        P("dom", "rep"),
        P("dom", None, None),
        P("dom", None),
        P("dom", None, None, None),
        P("dom", None, None, None),
        P("dom", "rep"),
        P("dom", "rep"),
        P("dom", "rep", None, None),
        P("dom", None),
        P("dom", None),
    )
    out_specs = P("dom", None, None)
    return jax.shard_map(
        on_device, mesh=mesh, in_specs=in_specs, out_specs=out_specs, check_vma=False
    )
```

```python
import functools

import jax
import jax.numpy as jnp
from jax import lax
from jax.experimental import pallas as pl
from jax.experimental.pallas import tpu as pltpu
from jax.sharding import PartitionSpec as P

penalty = 4.0
lanes = 128
wide = 256
code_bits = 12
code = 1 << code_bits
vmem = pl.BlockSpec(memory_space=pltpu.VMEM)
smem = pl.BlockSpec(memory_space=pltpu.SMEM)
hbm = pl.BlockSpec(memory_space=pltpu.HBM)
f32 = jnp.float32
bf16 = jnp.bfloat16


def call(body, out_shape, in_specs, out_specs, scratch, flops, vmem_mib=32):
    return pl.pallas_call(
        body,
        out_shape=out_shape,
        in_specs=in_specs,
        out_specs=out_specs,
        scratch_shapes=scratch,
        compiler_params=pltpu.CompilerParams(vmem_limit_bytes=vmem_mib * 1024 * 1024),
        cost_estimate=pl.CostEstimate(flops=flops, bytes_accessed=1 << 20, transcendentals=0),
    )


def rows_like(count):
    return lax.broadcasted_iota(jnp.int32, (count, lanes), 0).astype(f32).astype(bf16)


def pick(match, values):
    return jnp.where(match, values, jnp.zeros((), bf16))


def upper(nodes):
    return [(row >> 8).astype(f32).astype(bf16) for row in nodes]


def one_hot(nodes):
    line = lax.broadcasted_iota(jnp.int32, (wide, lanes), 0).astype(f32).astype(bf16)
    low = [(row & (wide - 1)).astype(f32).astype(bf16) for row in nodes]
    one, zero = jnp.ones((), bf16), jnp.zeros((), bf16)
    return jnp.concatenate([jnp.where(line == row, one, zero) for row in low], axis=1)


def halves(ref, c, tops):
    at = c * 2 * tops
    return jnp.concatenate(
        [ref[pl.ds(at, tops, stride=2)], ref[pl.ds(at + 1, tops, stride=2)]], axis=1
    )


def two_parts(x):
    coarse = x.astype(bf16)
    return [coarse, (x - coarse.astype(f32)).astype(bf16)]


def row_sums(rows):
    line = lax.broadcasted_iota(jnp.int32, rows[0].shape, 0)
    for step in (4, 2, 1):
        first = (line & step) == 0
        rows = [
            jnp.where(first, a, b)
            + jnp.where(first, pltpu.roll(a, 8 - step, 0), pltpu.roll(b, step, 0))
            for a, b in zip(rows[:step], rows[step:])
        ]
    return rows[0]


def lookup(tables, nodes):
    tops = tables[0][0].shape[0]
    stacked = jnp.concatenate([part for table in tables for part in table], axis=0)
    found = jnp.dot(stacked, one_hot(nodes), preferred_element_type=f32)
    line = lax.broadcasted_iota(jnp.int32, (tops, lanes), 0)
    rows = [[] for _ in tables]
    for i, row in enumerate(nodes):
        match = line == (row >> 8)
        at = 0
        for c, table in enumerate(tables):
            here = found[at : at + tops, i * lanes : (i + 1) * lanes]
            for p in range(1, len(table)):
                here += found[at + p * tops : at + (p + 1) * tops, i * lanes : (i + 1) * lanes]
            at += len(table) * tops
            here = jnp.where(match, here, 0.0)
            rows[c].append(sum(here[k : k + 8] for k in range(8, tops, 8)) + here[:8])
    if len(nodes) == 8:
        return [row_sums(held) for held in rows]
    return [
        jnp.concatenate([jnp.sum(row, axis=0, keepdims=True) for row in held], axis=0) for held in rows
    ]


def node_sums(nodes, values, tops, parts=2):
    line = rows_like(tops)
    comps = len(values)
    left = []
    for i, top in enumerate(upper(nodes)):
        match = line == top
        pieces = [v[i].astype(bf16) for v in values]
        if parts == 2:
            pieces += [(v[i] - w.astype(f32)).astype(bf16) for v, w in zip(values, pieces)]
        left.append(jnp.concatenate([pick(match, piece) for piece in pieces], axis=0))
    both = lax.dot_general(
        jnp.concatenate(left, axis=1),
        one_hot(nodes),
        (((1,), (1,)), ((), ())),
        preferred_element_type=f32,
    )
    return both if parts == 1 else both[: comps * tops] + both[comps * tops :]


def add_halves(ref, sums, c, tops, row=None):
    at = (c if row is None else row) * 2 * tops
    for half in range(2):
        ref[pl.ds(at + half, tops, stride=2)] += sums[
            c * tops : (c + 1) * tops, half * lanes : (half + 1) * lanes
        ]


def pack_kernel(
    cap, region_hbm, slot_hbm, coords_hbm, disp_hbm, surf_hbm, out_ref,
    stage, region_ref, slot_ref, coords_ref, disp_ref, surf_ref, sems,
):
    sources = (coords_hbm, disp_hbm, slot_hbm, surf_hbm, region_hbm)
    places = (coords_ref, disp_ref, slot_ref, surf_ref, region_ref)
    copies = [
        pltpu.make_async_copy(a, b, sems.at[i]) for i, (a, b) in enumerate(zip(sources, places))
    ]
    for copy in copies:
        copy.start()
    parts, rows, _ = out_ref.shape
    nblk = surf_ref.shape[1]
    tiles = slot_ref.shape[1]
    tops = coords_ref.shape[0] // 6
    for copy in copies:
        copy.wait()
    rest = (rows - 3 * cap, lanes)
    lane = lax.broadcasted_iota(jnp.int32, rest, 1)
    line = lax.broadcasted_iota(jnp.int32, rest, 0)
    tail = jnp.zeros(rest, f32)
    for t in range(tiles):
        tail = jnp.where((lane == t) & (line == 0), slot_ref[0, t].astype(f32), tail)
    for q in range(nblk // cap):
        stage[q, 3 * cap :] = tail
    empty = jnp.concatenate([jnp.zeros((3 * cap, lanes), f32), tail], axis=0).astype(bf16)
    for j in range(parts):
        out_ref[j] = empty
    tables = [
        [(halves(coords_ref, c, tops) + halves(disp_ref, c, tops)).astype(bf16)] for c in range(3)
    ]
    size = min(cap, 8)
    for first in range(0, nblk, 8):
        values = lookup(tables, [surf_ref[0, first + i : first + i + 1] for i in range(8)])
        for b in range(first, first + 8, size):
            for c in range(3):
                at = c * cap + b % cap
                stage[b // cap, at : at + size] = values[c][b - first : b - first + size]
    for q in range(nblk // cap):
        out_ref[region_ref[0, q * cap]] = stage[q].astype(bf16)


def element_kernel(
    slot_ref, face_ref, disp_ref, stiff_ref, modulus_ref, nodes_ref, mass_ref, lo_ref, hi_ref, surf_ref, region_ref,
    out_ref, first_ref, second_ref, tiles_ref, local, sums,
):
    for t in range(slot_ref.shape[1]):
        tiles_ref[0, t] = slot_ref[0, t]
        tiles_ref[1, t] = face_ref[0, t]
    corners, count = nodes_ref.shape[1:]
    tops = disp_ref.shape[0] // 6
    tables = [two_parts(halves(disp_ref, c, tops)) for c in range(3)]
    cuts = [slice(g * lanes, (g + 1) * lanes) for g in range(count // lanes)]
    nodes = [[nodes_ref[0, a : a + 1, cut] for a in range(corners)] for cut in cuts]
    for cut, here in zip(cuts, nodes):
        values = lookup(tables, here)
        for c in range(3):
            local[c * corners : (c + 1) * corners, cut] = values[c]
    force = jnp.dot(
        stiff_ref[...], local[...], precision=lax.Precision.HIGHEST, preferred_element_type=f32
    )
    local[...] = -(force * modulus_ref[...])
    for g, (cut, here) in enumerate(zip(cuts, nodes)):
        values = [
            [local[c * corners + a : c * corners + a + 1, cut] for a in range(corners)]
            for c in range(3)
        ]
        added = node_sums(here, values, tops)
        sums[...] = added if g == 0 else sums[...] + added
    out_ref[...] = jnp.zeros_like(out_ref)
    for c in range(3):
        add_halves(out_ref, sums[...], c, tops)
    even = lax.axis_index("dom") % 2 == 0
    nblk = surf_ref.shape[1]
    shared = lo_ref.shape[0]
    head = first_ref.shape[0] - 4 * shared
    tables = [two_parts(sums[c * tops : (c + 1) * tops]) for c in range(3)]
    tables.append(two_parts(halves(mass_ref, 0, tops)))
    values = lookup(tables, [ref[k : k + 1] for ref in (lo_ref, hi_ref) for k in range(shared)])
    lower_list, upper_list = lo_ref[...].astype(f32), hi_ref[...].astype(f32)
    for ref, up in ((first_ref, even), (second_ref, jnp.logical_not(even))):
        ref[:nblk] = surf_ref[0].astype(f32)
        ref[nblk : nblk + shared] = jnp.where(up, upper_list, lower_list)
        ref[nblk + shared : nblk + shared + 1] = region_ref[...].astype(f32)
        ref[nblk + shared + 1 : head] = jnp.zeros((head - nblk - shared - 1, lanes), f32)
        for c in range(4):
            below, above = values[c][:shared], values[c][shared:]
            ref[head + c * shared : head + (c + 1) * shared] = jnp.where(up, above, below)


def neighbour_kernel(
    part_ref, mass_ref, lo_ref, hi_ref, own_surf_ref, region_ref, first_ref, second_ref,
    out_ref, out_mass_ref, surf_ref, nodes_ref, regions_ref,
):
    even = lax.axis_index("dom") % 2 == 0
    tops = mass_ref.shape[0] // 2
    nblk = own_surf_ref.shape[1]
    nodes_all = mass_ref.shape[0] * lanes
    shared = lo_ref.shape[0]
    head = first_ref.shape[0] - 4 * shared
    out_ref[...] = part_ref[...]
    out_mass_ref[...] = mass_ref[...]
    first, second = first_ref[...], second_ref[...]
    packs = [jnp.where(even, second, first), jnp.where(even, first, second)]
    for i, pack in enumerate(packs):
        surf_ref[2 * i * nblk : (2 * i + 1) * nblk] = pack[:nblk].astype(jnp.int32) + 2 * i * nodes_all
        nodes_ref[(2 + i) * shared : (3 + i) * shared] = pack[nblk : nblk + shared].astype(jnp.int32)
        regions_ref[2 * i : 2 * i + 1] = pack[nblk + shared : nblk + shared + 1].astype(jnp.int32)
    surf_ref[nblk : 2 * nblk] = own_surf_ref[0] + nodes_all
    regions_ref[1:2] = region_ref[...]
    nodes_ref[:shared] = lo_ref[...]
    nodes_ref[shared : 2 * shared] = hi_ref[...]
    nodes = [ref[k : k + 1] for ref in (lo_ref, hi_ref) for k in range(shared)]
    values = [
        [pack[head + c * shared + k : head + c * shared + k + 1] for pack in packs for k in range(shared)]
        for c in range(4)
    ]
    sums = node_sums(nodes, values, tops)
    for c in range(3):
        add_halves(out_ref, sums, c, tops)
    add_halves(out_mass_ref, sums, 3, tops, 0)


def tile_kernel(cap, tiles_ref, got_ref, pos_ref, normal_ref, weight_ref, out_ref, slots_ref, flat):
    parts, rows, _ = got_ref.shape
    tiles = tiles_ref.shape[1]
    shift = cap.bit_length() - 1
    faces = [tiles_ref[1, t] for t in range(tiles)]
    starts = [(tiles_ref[0, t] >> shift) * rows + (tiles_ref[0, t] & (cap - 1)) for t in range(tiles)]
    for j in range(parts):
        flat[j * rows : (j + 1) * rows] = got_ref[j].astype(f32)
    slots_ref[...] = jnp.concatenate(
        [flat[j * rows + 3 * cap : j * rows + 3 * cap + 1] for j in range(parts)], axis=0
    ).astype(jnp.int32)
    x = jnp.concatenate(
        [flat[pl.ds(at + c * cap, 1)] for c in range(3) for at in starts], axis=0
    )
    weights = weight_ref[0].reshape(tiles * lanes, lanes)
    crossed = lax.dot_general(
        x.astype(bf16), weights, (((1,), (1,)), ((), ())), preferred_element_type=f32
    )
    line = lax.broadcasted_iota(jnp.int32, (tiles, lanes), 0)
    gap = jnp.zeros((tiles, lanes), f32)
    normals = []
    for c in range(3):
        interp = jnp.zeros((tiles, lanes), f32)
        for t in range(tiles):
            here = crossed[c * tiles : (c + 1) * tiles, t * lanes : (t + 1) * lanes]
            interp = jnp.where(line == t, here, interp)
        normal = jnp.concatenate([normal_ref[0, c, pl.ds(f, 1)] for f in faces], axis=0)
        pos = jnp.concatenate([pos_ref[0, c, pl.ds(f, 1)] for f in faces], axis=0)
        gap += normal * (interp - pos)
        normals.append(normal)
    pressure = penalty * jnp.maximum(-gap, 0.0)
    push = [pressure * normal for normal in normals]
    spread = jnp.concatenate(
        [
            jnp.concatenate([jnp.where(line == t, p, 0.0) for p in push], axis=0).astype(bf16)
            for t in range(tiles)
        ],
        axis=1,
    )
    forces = jnp.dot(spread, weights, preferred_element_type=f32).astype(bf16)
    pad = out_ref.shape[0] - forces.shape[0]
    if pad:
        forces = jnp.concatenate([forces, jnp.zeros((pad, lanes), bf16)], axis=0)
    out_ref[...] = forces


def list_kernel(cap, tiles, force_rows, slots_ref, regions_ref, list_ref, run_of):
    parts = slots_ref.shape[0]
    nblk = regions_ref.shape[1]
    shift = cap.bit_length() - 1
    me = lax.axis_index("dom")
    for p in range(3):
        for q in range(nblk // cap):
            run_of[p * parts + regions_ref[p, q * cap]] = p * nblk + q * cap

    def pick(place, filled):
        j = me ^ place
        slots = [slots_ref[j, t] for t in range(tiles)]
        which = [(slot >> shift) - me + 1 for slot in slots]
        kept = [(p >= 0) & (p <= 2) for p in which]
        runs = [run_of[jnp.where(own, p, 0) * parts + j] for own, p in zip(kept, which)]
        places = []
        for own in kept:
            places.append(filled)
            filled = filled + jnp.where(own, 1, 0)
        for t in range(tiles):
            entry = (place * force_rows + t) * code + (slots[t] & (cap - 1)) + runs[t]
            list_ref[0, places[t]] = entry
        return filled

    filled = lax.fori_loop(0, parts, pick, jnp.int32(0))
    for i in range(8):
        list_ref[0, filled + i] = 0
    list_ref[0, list_ref.shape[1] - 1] = filled


def contact_kernel(tiles, list_ref, surf_ref, nodes_ref, part_ref, *refs):
    back_refs, out_ref, back, sums, total = refs[:-4], refs[-4], refs[-3], refs[-2], refs[-1]
    size = back_refs[0].shape[0]
    tops = part_ref.shape[0] // 6
    shared = nodes_ref.shape[0] // 4
    total[...] = part_ref[...]
    for i, ref in enumerate(back_refs):
        back[i * size : (i + 1) * size] = ref[...].astype(f32)
    filled = list_ref[0, list_ref.shape[1] - 1]
    sums[...] = jnp.zeros_like(sums)

    def spread(g, _):
        nodes, values = [], [[], [], []]
        for i in range(8):
            entry = list_ref[0, g * 8 + i]
            row = surf_ref[pl.ds(entry & (code - 1), 1)]
            nodes.append(jnp.where(g * 8 + i < filled, row, -1))
            for c in range(3):
                values[c].append(back[pl.ds((entry >> code_bits) + c * tiles, 1)])
        sums[...] += node_sums(nodes, values, 3 * tops, 1)
        return 0

    lax.fori_loop(0, (filled + 7) // 8, spread, 0)
    pieces = [[sums[(c * 3 + p) * tops : (c * 3 + p + 1) * tops] for c in range(3)] for p in range(3)]
    found = []
    for p in (0, 2):
        at = (2 + p // 2) * shared
        found.append(
            lookup(
                [two_parts(piece) for piece in pieces[p]],
                [nodes_ref[at + k : at + k + 1] for k in range(shared)],
            )
        )
    added = node_sums(
        [nodes_ref[k : k + 1] for k in range(2 * shared)],
        [[near[c][k : k + 1] for near in found for k in range(shared)] for c in range(3)],
        tops,
    )
    added += jnp.concatenate(pieces[1], axis=0)
    for c in range(3):
        add_halves(total, added, c, tops)
    out_ref[...] = total[...].astype(bf16)


def accel_kernel(mass_ref, *refs):
    out_ref = refs[-1]
    terms = [ref[...].astype(f32) for ref in refs[:-1]]
    while len(terms) > 1:
        terms = [a + b for a, b in zip(terms[::2], terms[1::2])]
    size = mass_ref.shape[0]
    for c in range(3):
        at = slice(c * size, (c + 1) * size)
        out_ref[at] = terms[0][at] / mass_ref[...]


def swapped(block, start):
    lows = range(start, lax.axis_size("dom") - 1, 2)
    return lax.ppermute(block, "dom", [(s, s + 1) for s in lows] + [(s + 1, s) for s in lows])


def from_mate(block, distance):
    return lax.ppermute(
        block, "rep", [(i, i ^ distance) for i in range(lax.axis_size("rep"))]
    )


def across(block, distance):
    return lax.ppermute(
        block, "dom", [(s, s ^ distance) for s in range(lax.axis_size("dom"))]
    )


def on_device(
    coords,
    disp,
    mass,
    stiffness,
    elem_nodes,
    modulus,
    surf_nodes,
    block_region,
    face_pos,
    face_normal,
    tile_slot,
    tile_face,
    tile_weight,
    shared_lo,
    shared_hi,
):
    parts = lax.axis_size("dom")
    assert lax.axis_size("rep") == 4
    nodes_all = disp.shape[2]
    nblk = surf_nodes.shape[1]
    tiles = tile_slot.shape[1]
    cap = max(2, 2 * nblk // parts)
    rows = (3 * cap + 1 + 15) // 16 * 16
    force_rows = (3 * tiles + 15) // 16 * 16
    node_array = jax.ShapeDtypeStruct((3 * nodes_all // lanes, lanes), f32)
    mass_array = jax.ShapeDtypeStruct((nodes_all // lanes, lanes), f32)
    coords = coords.reshape(node_array.shape)
    disp = disp.reshape(node_array.shape)
    mass = mass.reshape(mass_array.shape)
    shared_lo = shared_lo.reshape(-1, lanes)
    shared_hi = shared_hi.reshape(-1, lanes)
    shared = shared_lo.shape[0]
    payload = jax.ShapeDtypeStruct((nblk + (shared + 8) // 8 * 8 + 4 * shared, lanes), f32)

    outgoing = call(
        functools.partial(pack_kernel, cap),
        jax.ShapeDtypeStruct((parts, rows, lanes), bf16),
        [hbm] * 5,
        vmem,
        [
            pltpu.VMEM((nblk // cap, rows, lanes), f32),
            pltpu.SMEM(block_region.shape, jnp.int32),
            pltpu.SMEM(tile_slot.shape, jnp.int32),
            pltpu.VMEM(coords.shape, f32),
            pltpu.VMEM(disp.shape, f32),
            pltpu.VMEM(surf_nodes.shape, jnp.int32),
            pltpu.SemaphoreType.DMA((5,)),
        ],
        1 << 30,
        60,
    )(block_region, tile_slot, coords, disp, surf_nodes)
    arrived = lax.all_to_all(outgoing, "dom", split_axis=0, concat_axis=0, tiled=True)

    part, first, second, tile_ids = call(
        element_kernel,
        (node_array, payload, payload, jax.ShapeDtypeStruct((2, tiles), jnp.int32)),
        [smem] * 2 + [vmem] * 9,
        (vmem, vmem, vmem, smem),
        [
            pltpu.VMEM((24, modulus.shape[1]), f32),
            pltpu.VMEM((3 * nodes_all // wide, wide), f32),
        ],
        1 << 32,
    )(
        tile_slot,
        tile_face,
        disp,
        stiffness,
        modulus,
        elem_nodes,
        mass,
        shared_lo,
        shared_hi,
        surf_nodes,
        block_region,
    )
    first = swapped(first, 0)
    arrived, part = lax.optimization_barrier((arrived, part))
    forces, slots = call(
        functools.partial(tile_kernel, cap),
        (
            jax.ShapeDtypeStruct((force_rows, lanes), bf16),
            jax.ShapeDtypeStruct((parts, lanes), jnp.int32),
        ),
        [smem] + [vmem] * 4,
        (vmem, vmem),
        [pltpu.VMEM((parts * rows, lanes), f32)],
        1 << 28,
    )(
        tile_ids,
        arrived,
        jnp.swapaxes(face_pos, 1, 2),
        jnp.swapaxes(face_normal, 1, 2),
        tile_weight,
    )
    forces, second = lax.optimization_barrier((forces, second))
    held, distance = forces, 1
    while 4 * distance < parts:
        held = jnp.concatenate([held, across(held, distance)], axis=0)
        distance *= 2
    back = [held] + [across(held, d) for d in range(distance, parts, distance)]
    second = swapped(second, 1)
    part, mass, surf, nodes, regions = call(
        neighbour_kernel,
        (
            node_array,
            mass_array,
            jax.ShapeDtypeStruct((3 * nblk, lanes), jnp.int32),
            jax.ShapeDtypeStruct((4 * shared, lanes), jnp.int32),
            jax.ShapeDtypeStruct((3, nblk), jnp.int32),
        ),
        [vmem] * 8,
        (vmem,) * 5,
        [],
        1 << 26,
    )(part, mass, shared_lo, shared_hi, surf_nodes, block_region, first, second)
    picks = call(
        functools.partial(list_kernel, cap, tiles, force_rows),
        jax.ShapeDtypeStruct((1, parts * tiles + 16), jnp.int32),
        [smem, smem],
        smem,
        [pltpu.SMEM((3 * parts,), jnp.int32)],
        1 << 24,
    )(slots, regions)
    own = call(
        functools.partial(contact_kernel, tiles),
        jax.ShapeDtypeStruct(node_array.shape, bf16),
        [smem] + [vmem] * (3 + len(back)),
        vmem,
        [
            pltpu.VMEM((parts * force_rows, lanes), f32),
            pltpu.VMEM((9 * nodes_all // wide, wide), f32),
            pltpu.VMEM(node_array.shape, f32),
        ],
        1 << 28,
    )(picks, surf, nodes, part, *back)
    accel = call(accel_kernel, node_array, [vmem] * 5, vmem, [], 1 << 24)(
        mass, own, *[from_mate(own, k) for k in (1, 2, 3)]
    )
    return accel.reshape(1, 3, nodes_all)


def solution(mesh):
    in_specs = (
        P("dom", None, None),
        P("dom", None, None),
        P("dom", None),
        P(),
        P("dom", None, "rep"),
        P("dom", "rep"),
        P("dom", None, None),
        P("dom", None),
        P("dom", None, None, None),
        P("dom", None, None, None),
        P("dom", "rep"),
        P("dom", "rep"),
        P("dom", "rep", None, None),
        P("dom", None),
        P("dom", None),
    )
    out_specs = P("dom", None, None)
    return jax.shard_map(
        on_device, mesh=mesh, in_specs=in_specs, out_specs=out_specs, check_vma=False
    )
```

```python
import functools

import jax
import jax.numpy as jnp
from jax import lax
from jax.experimental import pallas as pl
from jax.experimental.pallas import tpu as pltpu
from jax.sharding import PartitionSpec as P

penalty = 4.0
lanes = 128
wide = 256
code_bits = 12
code = 1 << code_bits
vmem = pl.BlockSpec(memory_space=pltpu.VMEM)
smem = pl.BlockSpec(memory_space=pltpu.SMEM)
hbm = pl.BlockSpec(memory_space=pltpu.HBM)
f32 = jnp.float32
bf16 = jnp.bfloat16


def call(body, out_shape, in_specs, out_specs, scratch, flops, vmem_mib=32):
    return pl.pallas_call(
        body,
        out_shape=out_shape,
        in_specs=in_specs,
        out_specs=out_specs,
        scratch_shapes=scratch,
        compiler_params=pltpu.CompilerParams(vmem_limit_bytes=vmem_mib * 1024 * 1024),
        cost_estimate=pl.CostEstimate(flops=flops, bytes_accessed=1 << 20, transcendentals=0),
    )


def rows_like(count):
    return lax.broadcasted_iota(jnp.int32, (count, lanes), 0).astype(f32).astype(bf16)


def pick(match, values):
    return jnp.where(match, values, jnp.zeros((), bf16))


def upper(nodes):
    return [(row >> 8).astype(f32).astype(bf16) for row in nodes]


def one_hot(nodes):
    line = lax.broadcasted_iota(jnp.int32, (wide, lanes), 0).astype(f32).astype(bf16)
    low = [(row & (wide - 1)).astype(f32).astype(bf16) for row in nodes]
    one, zero = jnp.ones((), bf16), jnp.zeros((), bf16)
    return jnp.concatenate([jnp.where(line == row, one, zero) for row in low], axis=1)


def halves(ref, c, tops):
    at = c * 2 * tops
    return jnp.concatenate(
        [ref[pl.ds(at, tops, stride=2)], ref[pl.ds(at + 1, tops, stride=2)]], axis=1
    )


def two_parts(x):
    coarse = x.astype(bf16)
    return [coarse, (x - coarse.astype(f32)).astype(bf16)]


def row_sums(rows):
    line = lax.broadcasted_iota(jnp.int32, rows[0].shape, 0)
    for step in (4, 2, 1):
        first = (line & step) == 0
        rows = [
            jnp.where(first, a, b)
            + jnp.where(first, pltpu.roll(a, 8 - step, 0), pltpu.roll(b, step, 0))
            for a, b in zip(rows[:step], rows[step:])
        ]
    return rows[0]


def lookup(tables, nodes):
    tops = tables[0][0].shape[0]
    stacked = jnp.concatenate([part for table in tables for part in table], axis=0)
    found = jnp.dot(stacked, one_hot(nodes), preferred_element_type=f32)
    line = lax.broadcasted_iota(jnp.int32, (tops, lanes), 0)
    rows = [[] for _ in tables]
    for i, row in enumerate(nodes):
        match = line == (row >> 8)
        at = 0
        for c, table in enumerate(tables):
            here = found[at : at + tops, i * lanes : (i + 1) * lanes]
            for p in range(1, len(table)):
                here += found[at + p * tops : at + (p + 1) * tops, i * lanes : (i + 1) * lanes]
            at += len(table) * tops
            here = jnp.where(match, here, 0.0)
            rows[c].append(sum(here[k : k + 8] for k in range(8, tops, 8)) + here[:8])
    if len(nodes) == 8:
        return [row_sums(held) for held in rows]
    return [
        jnp.concatenate([jnp.sum(row, axis=0, keepdims=True) for row in held], axis=0) for held in rows
    ]


def node_sums(nodes, values, tops, parts=2):
    line = rows_like(tops)
    comps = len(values)
    left = []
    for i, top in enumerate(upper(nodes)):
        match = line == top
        pieces = [v[i].astype(bf16) for v in values]
        if parts == 2:
            pieces += [(v[i] - w.astype(f32)).astype(bf16) for v, w in zip(values, pieces)]
        left.append(jnp.concatenate([pick(match, piece) for piece in pieces], axis=0))
    both = lax.dot_general(
        jnp.concatenate(left, axis=1),
        one_hot(nodes),
        (((1,), (1,)), ((), ())),
        preferred_element_type=f32,
    )
    return both if parts == 1 else both[: comps * tops] + both[comps * tops :]


def add_halves(ref, sums, c, tops, row=None):
    at = (c if row is None else row) * 2 * tops
    for half in range(2):
        ref[pl.ds(at + half, tops, stride=2)] += sums[
            c * tops : (c + 1) * tops, half * lanes : (half + 1) * lanes
        ]


def pack_kernel(
    cap, region_hbm, slot_hbm, coords_hbm, disp_hbm, surf_hbm, out_ref,
    stage, region_ref, slot_ref, coords_ref, disp_ref, surf_ref, sems,
):
    sources = (coords_hbm, disp_hbm, slot_hbm, surf_hbm, region_hbm)
    places = (coords_ref, disp_ref, slot_ref, surf_ref, region_ref)
    copies = [
        pltpu.make_async_copy(a, b, sems.at[i]) for i, (a, b) in enumerate(zip(sources, places))
    ]
    for copy in copies:
        copy.start()
    parts, rows, _ = out_ref.shape
    nblk = surf_ref.shape[1]
    tiles = slot_ref.shape[1]
    tops = coords_ref.shape[0] // 6
    for copy in copies:
        copy.wait()
    rest = (rows - 3 * cap, lanes)
    lane = lax.broadcasted_iota(jnp.int32, rest, 1)
    line = lax.broadcasted_iota(jnp.int32, rest, 0)
    tail = jnp.zeros(rest, f32)
    for t in range(tiles):
        tail = jnp.where((lane == t) & (line == 0), slot_ref[0, t].astype(f32), tail)
    for q in range(nblk // cap):
        stage[q, 3 * cap :] = tail
    empty = jnp.concatenate([jnp.zeros((3 * cap, lanes), f32), tail], axis=0).astype(bf16)
    for j in range(parts):
        out_ref[j] = empty
    tables = [
        [(halves(coords_ref, c, tops) + halves(disp_ref, c, tops)).astype(bf16)] for c in range(3)
    ]
    size = min(cap, 8)
    for first in range(0, nblk, 8):
        values = lookup(tables, [surf_ref[0, first + i : first + i + 1] for i in range(8)])
        for b in range(first, first + 8, size):
            for c in range(3):
                at = c * cap + b % cap
                stage[b // cap, at : at + size] = values[c][b - first : b - first + size]
    for q in range(nblk // cap):
        out_ref[region_ref[0, q * cap]] = stage[q].astype(bf16)


def element_kernel(
    slot_ref, face_ref, disp_ref, stiff_ref, modulus_ref, nodes_ref, mass_ref, lo_ref, hi_ref, surf_ref, region_ref,
    out_ref, first_ref, second_ref, tiles_ref, local, sums,
):
    for t in range(slot_ref.shape[1]):
        tiles_ref[0, t] = slot_ref[0, t]
        tiles_ref[1, t] = face_ref[0, t]
    corners, count = nodes_ref.shape[1:]
    tops = disp_ref.shape[0] // 6
    tables = [two_parts(halves(disp_ref, c, tops)) for c in range(3)]
    cuts = [slice(g * lanes, (g + 1) * lanes) for g in range(count // lanes)]
    nodes = [[nodes_ref[0, a : a + 1, cut] for a in range(corners)] for cut in cuts]
    for cut, here in zip(cuts, nodes):
        values = lookup(tables, here)
        for c in range(3):
            local[c * corners : (c + 1) * corners, cut] = values[c]
    force = jnp.dot(
        stiff_ref[...], local[...], precision=lax.Precision.HIGHEST, preferred_element_type=f32
    )
    local[...] = -(force * modulus_ref[...])
    for g, (cut, here) in enumerate(zip(cuts, nodes)):
        values = [
            [local[c * corners + a : c * corners + a + 1, cut] for a in range(corners)]
            for c in range(3)
        ]
        added = node_sums(here, values, tops)
        sums[...] = added if g == 0 else sums[...] + added
    out_ref[...] = jnp.zeros_like(out_ref)
    for c in range(3):
        add_halves(out_ref, sums[...], c, tops)
    even = lax.axis_index("dom") % 2 == 0
    nblk = surf_ref.shape[1]
    shared = lo_ref.shape[0]
    head = first_ref.shape[0] - 4 * shared
    tables = [two_parts(sums[c * tops : (c + 1) * tops]) for c in range(3)]
    tables.append(two_parts(halves(mass_ref, 0, tops)))
    values = lookup(tables, [ref[k : k + 1] for ref in (lo_ref, hi_ref) for k in range(shared)])
    lower_list, upper_list = lo_ref[...].astype(f32), hi_ref[...].astype(f32)
    for ref, up in ((first_ref, even), (second_ref, jnp.logical_not(even))):
        ref[:nblk] = surf_ref[0].astype(f32)
        ref[nblk : nblk + shared] = jnp.where(up, upper_list, lower_list)
        ref[nblk + shared : nblk + shared + 1] = region_ref[...].astype(f32)
        ref[nblk + shared + 1 : head] = jnp.zeros((head - nblk - shared - 1, lanes), f32)
        for c in range(4):
            below, above = values[c][:shared], values[c][shared:]
            ref[head + c * shared : head + (c + 1) * shared] = jnp.where(up, above, below)


def neighbour_kernel(
    part_ref, mass_ref, lo_ref, hi_ref, own_surf_ref, region_ref, first_ref, second_ref,
    out_ref, out_mass_ref, surf_ref, nodes_ref, regions_ref,
):
    even = lax.axis_index("dom") % 2 == 0
    tops = mass_ref.shape[0] // 2
    nblk = own_surf_ref.shape[1]
    nodes_all = mass_ref.shape[0] * lanes
    shared = lo_ref.shape[0]
    head = first_ref.shape[0] - 4 * shared
    out_ref[...] = part_ref[...]
    out_mass_ref[...] = mass_ref[...]
    first, second = first_ref[...], second_ref[...]
    packs = [jnp.where(even, second, first), jnp.where(even, first, second)]
    for i, pack in enumerate(packs):
        surf_ref[2 * i * nblk : (2 * i + 1) * nblk] = pack[:nblk].astype(jnp.int32) + 2 * i * nodes_all
        nodes_ref[(2 + i) * shared : (3 + i) * shared] = pack[nblk : nblk + shared].astype(jnp.int32)
        regions_ref[2 * i : 2 * i + 1] = pack[nblk + shared : nblk + shared + 1].astype(jnp.int32)
    surf_ref[nblk : 2 * nblk] = own_surf_ref[0] + nodes_all
    regions_ref[1:2] = region_ref[...]
    nodes_ref[:shared] = lo_ref[...]
    nodes_ref[shared : 2 * shared] = hi_ref[...]
    nodes = [ref[k : k + 1] for ref in (lo_ref, hi_ref) for k in range(shared)]
    values = [
        [pack[head + c * shared + k : head + c * shared + k + 1] for pack in packs for k in range(shared)]
        for c in range(4)
    ]
    sums = node_sums(nodes, values, tops)
    for c in range(3):
        add_halves(out_ref, sums, c, tops)
    add_halves(out_mass_ref, sums, 3, tops, 0)


def tile_kernel(cap, tiles_ref, got_ref, pos_ref, normal_ref, weight_ref, out_ref, slots_ref, flat):
    parts, rows, _ = got_ref.shape
    tiles = tiles_ref.shape[1]
    shift = cap.bit_length() - 1
    faces = [tiles_ref[1, t] for t in range(tiles)]
    starts = [(tiles_ref[0, t] >> shift) * rows + (tiles_ref[0, t] & (cap - 1)) for t in range(tiles)]
    for j in range(parts):
        flat[j * rows : (j + 1) * rows] = got_ref[j].astype(f32)
    slots_ref[...] = jnp.concatenate(
        [flat[j * rows + 3 * cap : j * rows + 3 * cap + 1] for j in range(parts)], axis=0
    ).astype(jnp.int32)
    x = jnp.concatenate(
        [flat[pl.ds(at + c * cap, 1)] for c in range(3) for at in starts], axis=0
    )
    weights = weight_ref[0].reshape(tiles * lanes, lanes)
    crossed = lax.dot_general(
        x.astype(bf16), weights, (((1,), (1,)), ((), ())), preferred_element_type=f32
    )
    line = lax.broadcasted_iota(jnp.int32, (tiles, lanes), 0)
    gap = jnp.zeros((tiles, lanes), f32)
    normals = []
    for c in range(3):
        interp = jnp.zeros((tiles, lanes), f32)
        for t in range(tiles):
            here = crossed[c * tiles : (c + 1) * tiles, t * lanes : (t + 1) * lanes]
            interp = jnp.where(line == t, here, interp)
        normal = jnp.concatenate([normal_ref[0, c, pl.ds(f, 1)] for f in faces], axis=0)
        pos = jnp.concatenate([pos_ref[0, c, pl.ds(f, 1)] for f in faces], axis=0)
        gap += normal * (interp - pos)
        normals.append(normal)
    pressure = penalty * jnp.maximum(-gap, 0.0)
    push = [pressure * normal for normal in normals]
    spread = jnp.concatenate(
        [
            jnp.concatenate([jnp.where(line == t, p, 0.0) for p in push], axis=0).astype(bf16)
            for t in range(tiles)
        ],
        axis=1,
    )
    forces = jnp.dot(spread, weights, preferred_element_type=f32).astype(bf16)
    pad = out_ref.shape[0] - forces.shape[0]
    if pad:
        forces = jnp.concatenate([forces, jnp.zeros((pad, lanes), bf16)], axis=0)
    out_ref[...] = forces


def list_kernel(cap, tiles, force_rows, slots_ref, regions_ref, list_ref, run_of):
    parts = slots_ref.shape[0]
    nblk = regions_ref.shape[1]
    shift = cap.bit_length() - 1
    me = lax.axis_index("dom")
    for p in range(3):
        for q in range(nblk // cap):
            run_of[p * parts + regions_ref[p, q * cap]] = p * nblk + q * cap

    def pick(place, filled):
        j = me ^ place
        slots = [slots_ref[j, t] for t in range(tiles)]
        which = [(slot >> shift) - me + 1 for slot in slots]
        kept = [(p >= 0) & (p <= 2) for p in which]
        runs = [run_of[jnp.where(own, p, 0) * parts + j] for own, p in zip(kept, which)]
        places = []
        for own in kept:
            places.append(filled)
            filled = filled + jnp.where(own, 1, 0)
        for t in range(tiles):
            entry = (place * force_rows + t) * code + (slots[t] & (cap - 1)) + runs[t]
            list_ref[0, places[t]] = entry
        return filled

    filled = lax.fori_loop(0, parts, pick, jnp.int32(0))
    for i in range(8):
        list_ref[0, filled + i] = 0
    list_ref[0, list_ref.shape[1] - 1] = filled


def contact_kernel(tiles, list_ref, surf_ref, nodes_ref, part_ref, *refs):
    back_refs, out_ref, back, sums, total = refs[:-4], refs[-4], refs[-3], refs[-2], refs[-1]
    size = back_refs[0].shape[0]
    tops = part_ref.shape[0] // 6
    shared = nodes_ref.shape[0] // 4
    total[...] = part_ref[...]
    for i, ref in enumerate(back_refs):
        back[i * size : (i + 1) * size] = ref[...].astype(f32)
    filled = list_ref[0, list_ref.shape[1] - 1]
    sums[...] = jnp.zeros_like(sums)

    def spread(g, _):
        nodes, values = [], [[], [], []]
        for i in range(8):
            entry = list_ref[0, g * 8 + i]
            row = surf_ref[pl.ds(entry & (code - 1), 1)]
            nodes.append(jnp.where(g * 8 + i < filled, row, -1))
            for c in range(3):
                values[c].append(back[pl.ds((entry >> code_bits) + c * tiles, 1)])
        sums[...] += node_sums(nodes, values, 3 * tops, 1)
        return 0

    lax.fori_loop(0, (filled + 7) // 8, spread, 0)
    pieces = [[sums[(c * 3 + p) * tops : (c * 3 + p + 1) * tops] for c in range(3)] for p in range(3)]
    found = []
    for p in (0, 2):
        at = (2 + p // 2) * shared
        found.append(
            lookup(
                [two_parts(piece) for piece in pieces[p]],
                [nodes_ref[at + k : at + k + 1] for k in range(shared)],
            )
        )
    added = node_sums(
        [nodes_ref[k : k + 1] for k in range(2 * shared)],
        [[near[c][k : k + 1] for near in found for k in range(shared)] for c in range(3)],
        tops,
    )
    added += jnp.concatenate(pieces[1], axis=0)
    for c in range(3):
        add_halves(total, added, c, tops)
    out_ref[...] = total[...].astype(bf16)


def accel_kernel(mass_ref, *refs):
    out_ref = refs[-1]
    terms = [ref[...].astype(f32) for ref in refs[:-1]]
    while len(terms) > 1:
        terms = [a + b for a, b in zip(terms[::2], terms[1::2])]
    size = mass_ref.shape[0]
    for c in range(3):
        at = slice(c * size, (c + 1) * size)
        out_ref[at] = terms[0][at] / mass_ref[...]


def swapped(block, start):
    lows = range(start, lax.axis_size("dom") - 1, 2)
    return lax.ppermute(block, "dom", [(s, s + 1) for s in lows] + [(s + 1, s) for s in lows])


def from_mate(block, distance):
    return lax.ppermute(
        block, "rep", [(i, i ^ distance) for i in range(lax.axis_size("rep"))]
    )


def across(block, distance):
    return lax.ppermute(
        block, "dom", [(s, s ^ distance) for s in range(lax.axis_size("dom"))]
    )


def on_device(
    coords,
    disp,
    mass,
    stiffness,
    elem_nodes,
    modulus,
    surf_nodes,
    block_region,
    face_pos,
    face_normal,
    tile_slot,
    tile_face,
    tile_weight,
    shared_lo,
    shared_hi,
):
    parts = lax.axis_size("dom")
    assert lax.axis_size("rep") == 4
    nodes_all = disp.shape[2]
    nblk = surf_nodes.shape[1]
    tiles = tile_slot.shape[1]
    cap = max(2, 2 * nblk // parts)
    rows = (3 * cap + 1 + 15) // 16 * 16
    force_rows = (3 * tiles + 15) // 16 * 16
    node_array = jax.ShapeDtypeStruct((3 * nodes_all // lanes, lanes), f32)
    mass_array = jax.ShapeDtypeStruct((nodes_all // lanes, lanes), f32)
    coords = coords.reshape(node_array.shape)
    disp = disp.reshape(node_array.shape)
    mass = mass.reshape(mass_array.shape)
    shared_lo = shared_lo.reshape(-1, lanes)
    shared_hi = shared_hi.reshape(-1, lanes)
    shared = shared_lo.shape[0]
    payload = jax.ShapeDtypeStruct((nblk + (shared + 8) // 8 * 8 + 4 * shared, lanes), f32)

    outgoing = call(
        functools.partial(pack_kernel, cap),
        jax.ShapeDtypeStruct((parts, rows, lanes), bf16),
        [hbm] * 5,
        vmem,
        [
            pltpu.VMEM((nblk // cap, rows, lanes), f32),
            pltpu.SMEM(block_region.shape, jnp.int32),
            pltpu.SMEM(tile_slot.shape, jnp.int32),
            pltpu.VMEM(coords.shape, f32),
            pltpu.VMEM(disp.shape, f32),
            pltpu.VMEM(surf_nodes.shape, jnp.int32),
            pltpu.SemaphoreType.DMA((5,)),
        ],
        1 << 30,
        60,
    )(block_region, tile_slot, coords, disp, surf_nodes)
    arrived = lax.all_to_all(outgoing, "dom", split_axis=0, concat_axis=0, tiled=True)

    part, first, second, tile_ids = call(
        element_kernel,
        (node_array, payload, payload, jax.ShapeDtypeStruct((2, tiles), jnp.int32)),
        [smem] * 2 + [vmem] * 9,
        (vmem, vmem, vmem, smem),
        [
            pltpu.VMEM((24, modulus.shape[1]), f32),
            pltpu.VMEM((3 * nodes_all // wide, wide), f32),
        ],
        1 << 32,
    )(
        tile_slot,
        tile_face,
        disp,
        stiffness,
        modulus,
        elem_nodes,
        mass,
        shared_lo,
        shared_hi,
        surf_nodes,
        block_region,
    )
    first = swapped(first, 0)
    arrived, part = lax.optimization_barrier((arrived, part))
    forces, slots = call(
        functools.partial(tile_kernel, cap),
        (
            jax.ShapeDtypeStruct((force_rows, lanes), bf16),
            jax.ShapeDtypeStruct((parts, lanes), jnp.int32),
        ),
        [smem] + [vmem] * 4,
        (vmem, vmem),
        [pltpu.VMEM((parts * rows, lanes), f32)],
        1 << 28,
    )(
        tile_ids,
        arrived,
        jnp.swapaxes(face_pos, 1, 2),
        jnp.swapaxes(face_normal, 1, 2),
        tile_weight,
    )
    forces, second = lax.optimization_barrier((forces, second))
    held, distance = forces, 1
    while 4 * distance < parts:
        held = jnp.concatenate([held, across(held, distance)], axis=0)
        distance *= 2
    back = [held] + [across(held, d) for d in range(distance, parts, distance)]
    second = swapped(second, 1)
    part, mass, surf, nodes, regions = call(
        neighbour_kernel,
        (
            node_array,
            mass_array,
            jax.ShapeDtypeStruct((3 * nblk, lanes), jnp.int32),
            jax.ShapeDtypeStruct((4 * shared, lanes), jnp.int32),
            jax.ShapeDtypeStruct((3, nblk), jnp.int32),
        ),
        [vmem] * 8,
        (vmem,) * 5,
        [],
        1 << 26,
    )(part, mass, shared_lo, shared_hi, surf_nodes, block_region, first, second)
    picks = call(
        functools.partial(list_kernel, cap, tiles, force_rows),
        jax.ShapeDtypeStruct((1, parts * tiles + 16), jnp.int32),
        [smem, smem],
        smem,
        [pltpu.SMEM((3 * parts,), jnp.int32)],
        1 << 24,
    )(slots, regions)
    own = call(
        functools.partial(contact_kernel, tiles),
        jax.ShapeDtypeStruct(node_array.shape, bf16),
        [smem] + [vmem] * (3 + len(back)),
        vmem,
        [
            pltpu.VMEM((parts * force_rows, lanes), f32),
            pltpu.VMEM((9 * nodes_all // wide, wide), f32),
            pltpu.VMEM(node_array.shape, f32),
        ],
        1 << 28,
    )(picks, surf, nodes, part, *back)
    accel = call(accel_kernel, node_array, [vmem] * 5, vmem, [], 1 << 24)(
        mass, own, *[from_mate(own, k) for k in (3, 2, 1)]
    )
    return accel.reshape(1, 3, nodes_all)


def solution(mesh):
    in_specs = (
        P("dom", None, None),
        P("dom", None, None),
        P("dom", None),
        P(),
        P("dom", None, "rep"),
        P("dom", "rep"),
        P("dom", None, None),
        P("dom", None),
        P("dom", None, None, None),
        P("dom", None, None, None),
        P("dom", "rep"),
        P("dom", "rep"),
        P("dom", "rep", None, None),
        P("dom", None),
        P("dom", None),
    )
    out_specs = P("dom", None, None)
    return jax.shard_map(
        on_device, mesh=mesh, in_specs=in_specs, out_specs=out_specs, check_vma=False
    )
```

```python
import functools

import jax
import jax.numpy as jnp
from jax import lax
from jax.experimental import pallas as pl
from jax.experimental.pallas import tpu as pltpu
from jax.sharding import PartitionSpec as P

penalty = 4.0
lanes = 128
wide = 256
code_bits = 12
code = 1 << code_bits
vmem = pl.BlockSpec(memory_space=pltpu.VMEM)
smem = pl.BlockSpec(memory_space=pltpu.SMEM)
hbm = pl.BlockSpec(memory_space=pltpu.HBM)
f32 = jnp.float32
bf16 = jnp.bfloat16


def call(body, out_shape, in_specs, out_specs, scratch, flops, vmem_mib=32):
    return pl.pallas_call(
        body,
        out_shape=out_shape,
        in_specs=in_specs,
        out_specs=out_specs,
        scratch_shapes=scratch,
        compiler_params=pltpu.CompilerParams(vmem_limit_bytes=vmem_mib * 1024 * 1024),
        cost_estimate=pl.CostEstimate(flops=flops, bytes_accessed=1 << 20, transcendentals=0),
    )


def rows_like(count):
    return lax.broadcasted_iota(jnp.int32, (count, lanes), 0).astype(f32).astype(bf16)


def pick(match, values):
    return jnp.where(match, values, jnp.zeros((), bf16))


def upper(nodes):
    return [(row >> 8).astype(f32).astype(bf16) for row in nodes]


def one_hot(nodes):
    line = lax.broadcasted_iota(jnp.int32, (wide, lanes), 0).astype(f32).astype(bf16)
    low = [(row & (wide - 1)).astype(f32).astype(bf16) for row in nodes]
    one, zero = jnp.ones((), bf16), jnp.zeros((), bf16)
    return jnp.concatenate([jnp.where(line == row, one, zero) for row in low], axis=1)


def halves(ref, c, tops):
    at = c * 2 * tops
    return jnp.concatenate(
        [ref[pl.ds(at, tops, stride=2)], ref[pl.ds(at + 1, tops, stride=2)]], axis=1
    )


def two_parts(x):
    coarse = x.astype(bf16)
    return [coarse, (x - coarse.astype(f32)).astype(bf16)]


def row_sums(rows):
    line = lax.broadcasted_iota(jnp.int32, rows[0].shape, 0)
    for step in (4, 2, 1):
        first = (line & step) == 0
        rows = [
            jnp.where(first, a, b)
            + jnp.where(first, pltpu.roll(a, 8 - step, 0), pltpu.roll(b, step, 0))
            for a, b in zip(rows[:step], rows[step:])
        ]
    return rows[0]


def lookup(tables, nodes):
    tops = tables[0][0].shape[0]
    stacked = jnp.concatenate([part for table in tables for part in table], axis=0)
    found = jnp.dot(stacked, one_hot(nodes), preferred_element_type=f32)
    line = lax.broadcasted_iota(jnp.int32, (tops, lanes), 0)
    rows = [[] for _ in tables]
    for i, row in enumerate(nodes):
        match = line == (row >> 8)
        at = 0
        for c, table in enumerate(tables):
            here = found[at : at + tops, i * lanes : (i + 1) * lanes]
            for p in range(1, len(table)):
                here += found[at + p * tops : at + (p + 1) * tops, i * lanes : (i + 1) * lanes]
            at += len(table) * tops
            here = jnp.where(match, here, 0.0)
            rows[c].append(sum(here[k : k + 8] for k in range(8, tops, 8)) + here[:8])
    if len(nodes) == 8:
        return [row_sums(held) for held in rows]
    return [
        jnp.concatenate([jnp.sum(row, axis=0, keepdims=True) for row in held], axis=0) for held in rows
    ]


def node_sums(nodes, values, tops, parts=2):
    line = rows_like(tops)
    comps = len(values)
    left = []
    for i, top in enumerate(upper(nodes)):
        match = line == top
        pieces = [v[i].astype(bf16) for v in values]
        if parts == 2:
            pieces += [(v[i] - w.astype(f32)).astype(bf16) for v, w in zip(values, pieces)]
        left.append(jnp.concatenate([pick(match, piece) for piece in pieces], axis=0))
    both = lax.dot_general(
        jnp.concatenate(left, axis=1),
        one_hot(nodes),
        (((1,), (1,)), ((), ())),
        preferred_element_type=f32,
    )
    return both if parts == 1 else both[: comps * tops] + both[comps * tops :]


def add_halves(ref, sums, c, tops, row=None):
    at = (c if row is None else row) * 2 * tops
    for half in range(2):
        ref[pl.ds(at + half, tops, stride=2)] += sums[
            c * tops : (c + 1) * tops, half * lanes : (half + 1) * lanes
        ]


def pack_kernel(
    cap, region_hbm, slot_hbm, coords_hbm, disp_hbm, surf_hbm, out_ref,
    stage, region_ref, slot_ref, coords_ref, disp_ref, surf_ref, sems,
):
    sources = (coords_hbm, disp_hbm, slot_hbm, surf_hbm, region_hbm)
    places = (coords_ref, disp_ref, slot_ref, surf_ref, region_ref)
    copies = [
        pltpu.make_async_copy(a, b, sems.at[i]) for i, (a, b) in enumerate(zip(sources, places))
    ]
    for copy in copies:
        copy.start()
    parts, rows, _ = out_ref.shape
    nblk = surf_ref.shape[1]
    tiles = slot_ref.shape[1]
    tops = coords_ref.shape[0] // 6
    for copy in copies:
        copy.wait()
    rest = (rows - 3 * cap, lanes)
    lane = lax.broadcasted_iota(jnp.int32, rest, 1)
    line = lax.broadcasted_iota(jnp.int32, rest, 0)
    tail = jnp.zeros(rest, f32)
    for t in range(tiles):
        tail = jnp.where((lane == t) & (line == 0), slot_ref[0, t].astype(f32), tail)
    for q in range(nblk // cap):
        stage[q, 3 * cap :] = tail
    empty = jnp.concatenate([jnp.zeros((3 * cap, lanes), f32), tail], axis=0).astype(bf16)
    for j in range(parts):
        out_ref[j] = empty
    tables = [
        [(halves(coords_ref, c, tops) + halves(disp_ref, c, tops)).astype(bf16)] for c in range(3)
    ]
    size = min(cap, 8)
    for first in range(0, nblk, 8):
        values = lookup(tables, [surf_ref[0, first + i : first + i + 1] for i in range(8)])
        for b in range(first, first + 8, size):
            for c in range(3):
                at = c * cap + b % cap
                stage[b // cap, at : at + size] = values[c][b - first : b - first + size]
    for q in range(nblk // cap):
        out_ref[region_ref[0, q * cap]] = stage[q].astype(bf16)


def element_kernel(
    slot_ref, face_ref, disp_ref, stiff_ref, modulus_ref, nodes_ref, mass_ref, lo_ref, hi_ref, surf_ref, region_ref,
    out_ref, first_ref, second_ref, tiles_ref, local, sums,
):
    tiles_ref[0:1] = slot_ref[...]
    tiles_ref[1:2] = face_ref[...]
    corners, count = nodes_ref.shape[1:]
    tops = disp_ref.shape[0] // 6
    tables = [two_parts(halves(disp_ref, c, tops)) for c in range(3)]
    cuts = [slice(g * lanes, (g + 1) * lanes) for g in range(count // lanes)]
    nodes = [[nodes_ref[0, a : a + 1, cut] for a in range(corners)] for cut in cuts]
    for cut, here in zip(cuts, nodes):
        values = lookup(tables, here)
        for c in range(3):
            local[c * corners : (c + 1) * corners, cut] = values[c]
    force = jnp.dot(
        stiff_ref[...], local[...], precision=lax.Precision.HIGHEST, preferred_element_type=f32
    )
    local[...] = -(force * modulus_ref[...])
    for g, (cut, here) in enumerate(zip(cuts, nodes)):
        values = [
            [local[c * corners + a : c * corners + a + 1, cut] for a in range(corners)]
            for c in range(3)
        ]
        added = node_sums(here, values, tops)
        sums[...] = added if g == 0 else sums[...] + added
    out_ref[...] = jnp.zeros_like(out_ref)
    for c in range(3):
        add_halves(out_ref, sums[...], c, tops)
    even = lax.axis_index("dom") % 2 == 0
    nblk = surf_ref.shape[1]
    shared = lo_ref.shape[0]
    head = first_ref.shape[0] - 4 * shared
    tables = [two_parts(sums[c * tops : (c + 1) * tops]) for c in range(3)]
    tables.append(two_parts(halves(mass_ref, 0, tops)))
    values = lookup(tables, [ref[k : k + 1] for ref in (lo_ref, hi_ref) for k in range(shared)])
    lower_list, upper_list = lo_ref[...].astype(f32), hi_ref[...].astype(f32)
    for ref, up in ((first_ref, even), (second_ref, jnp.logical_not(even))):
        ref[:nblk] = surf_ref[0].astype(f32)
        ref[nblk : nblk + shared] = jnp.where(up, upper_list, lower_list)
        ref[nblk + shared : nblk + shared + 1] = region_ref[...].astype(f32)
        ref[nblk + shared + 1 : head] = jnp.zeros((head - nblk - shared - 1, lanes), f32)
        for c in range(4):
            below, above = values[c][:shared], values[c][shared:]
            ref[head + c * shared : head + (c + 1) * shared] = jnp.where(up, above, below)


def neighbour_kernel(
    part_ref, mass_ref, lo_ref, hi_ref, own_surf_ref, region_ref, first_ref, second_ref,
    out_ref, out_mass_ref, surf_ref, nodes_ref, regions_ref,
):
    even = lax.axis_index("dom") % 2 == 0
    tops = mass_ref.shape[0] // 2
    nblk = own_surf_ref.shape[1]
    nodes_all = mass_ref.shape[0] * lanes
    shared = lo_ref.shape[0]
    head = first_ref.shape[0] - 4 * shared
    out_ref[...] = part_ref[...]
    out_mass_ref[...] = mass_ref[...]
    first, second = first_ref[...], second_ref[...]
    packs = [jnp.where(even, second, first), jnp.where(even, first, second)]
    for i, pack in enumerate(packs):
        surf_ref[2 * i * nblk : (2 * i + 1) * nblk] = pack[:nblk].astype(jnp.int32) + 2 * i * nodes_all
        nodes_ref[(2 + i) * shared : (3 + i) * shared] = pack[nblk : nblk + shared].astype(jnp.int32)
        regions_ref[2 * i : 2 * i + 1] = pack[nblk + shared : nblk + shared + 1].astype(jnp.int32)
    surf_ref[nblk : 2 * nblk] = own_surf_ref[0] + nodes_all
    regions_ref[1:2] = region_ref[...]
    nodes_ref[:shared] = lo_ref[...]
    nodes_ref[shared : 2 * shared] = hi_ref[...]
    nodes = [ref[k : k + 1] for ref in (lo_ref, hi_ref) for k in range(shared)]
    values = [
        [pack[head + c * shared + k : head + c * shared + k + 1] for pack in packs for k in range(shared)]
        for c in range(4)
    ]
    sums = node_sums(nodes, values, tops)
    for c in range(3):
        add_halves(out_ref, sums, c, tops)
    add_halves(out_mass_ref, sums, 3, tops, 0)


def tile_kernel(cap, tiles_ref, got_ref, pos_ref, normal_ref, weight_ref, out_ref, slots_ref, flat):
    parts, rows, _ = got_ref.shape
    tiles = tiles_ref.shape[1]
    shift = cap.bit_length() - 1
    faces = [tiles_ref[1, t] for t in range(tiles)]
    starts = [(tiles_ref[0, t] >> shift) * rows + (tiles_ref[0, t] & (cap - 1)) for t in range(tiles)]
    for j in range(parts):
        flat[j * rows : (j + 1) * rows] = got_ref[j].astype(f32)
    slots_ref[...] = jnp.concatenate(
        [flat[j * rows + 3 * cap : j * rows + 3 * cap + 1] for j in range(parts)], axis=0
    ).astype(jnp.int32)
    x = jnp.concatenate(
        [flat[pl.ds(at + c * cap, 1)] for c in range(3) for at in starts], axis=0
    )
    weights = weight_ref[0].reshape(tiles * lanes, lanes)
    crossed = lax.dot_general(
        x.astype(bf16), weights, (((1,), (1,)), ((), ())), preferred_element_type=f32
    )
    line = lax.broadcasted_iota(jnp.int32, (tiles, lanes), 0)
    gap = jnp.zeros((tiles, lanes), f32)
    normals = []
    for c in range(3):
        interp = jnp.zeros((tiles, lanes), f32)
        for t in range(tiles):
            here = crossed[c * tiles : (c + 1) * tiles, t * lanes : (t + 1) * lanes]
            interp = jnp.where(line == t, here, interp)
        normal = jnp.concatenate([normal_ref[0, c, pl.ds(f, 1)] for f in faces], axis=0)
        pos = jnp.concatenate([pos_ref[0, c, pl.ds(f, 1)] for f in faces], axis=0)
        gap += normal * (interp - pos)
        normals.append(normal)
    pressure = penalty * jnp.maximum(-gap, 0.0)
    push = [pressure * normal for normal in normals]
    spread = jnp.concatenate(
        [
            jnp.concatenate([jnp.where(line == t, p, 0.0) for p in push], axis=0).astype(bf16)
            for t in range(tiles)
        ],
        axis=1,
    )
    forces = jnp.dot(spread, weights, preferred_element_type=f32).astype(bf16)
    pad = out_ref.shape[0] - forces.shape[0]
    if pad:
        forces = jnp.concatenate([forces, jnp.zeros((pad, lanes), bf16)], axis=0)
    out_ref[...] = forces


def list_kernel(cap, tiles, force_rows, slots_ref, regions_ref, list_ref, run_of):
    parts = slots_ref.shape[0]
    nblk = regions_ref.shape[1]
    shift = cap.bit_length() - 1
    me = lax.axis_index("dom")
    for p in range(3):
        for q in range(nblk // cap):
            run_of[p * parts + regions_ref[p, q * cap]] = p * nblk + q * cap

    def pick(place, filled):
        j = me ^ place
        slots = [slots_ref[j, t] for t in range(tiles)]
        which = [(slot >> shift) - me + 1 for slot in slots]
        kept = [(p >= 0) & (p <= 2) for p in which]
        runs = [run_of[jnp.where(own, p, 0) * parts + j] for own, p in zip(kept, which)]
        places = []
        for own in kept:
            places.append(filled)
            filled = filled + jnp.where(own, 1, 0)
        for t in range(tiles):
            entry = (place * force_rows + t) * code + (slots[t] & (cap - 1)) + runs[t]
            list_ref[0, places[t]] = entry
        return filled

    filled = lax.fori_loop(0, parts, pick, jnp.int32(0))
    for i in range(8):
        list_ref[0, filled + i] = 0
    list_ref[0, list_ref.shape[1] - 1] = filled


def contact_kernel(tiles, list_ref, surf_ref, nodes_ref, part_ref, *refs):
    back_refs, out_ref, back, sums, total = refs[:-4], refs[-4], refs[-3], refs[-2], refs[-1]
    size = back_refs[0].shape[0]
    tops = part_ref.shape[0] // 6
    shared = nodes_ref.shape[0] // 4
    total[...] = part_ref[...]
    for i, ref in enumerate(back_refs):
        back[i * size : (i + 1) * size] = ref[...].astype(f32)
    filled = list_ref[0, list_ref.shape[1] - 1]
    sums[...] = jnp.zeros_like(sums)

    def spread(g, _):
        nodes, values = [], [[], [], []]
        for i in range(8):
            entry = list_ref[0, g * 8 + i]
            row = surf_ref[pl.ds(entry & (code - 1), 1)]
            nodes.append(jnp.where(g * 8 + i < filled, row, -1))
            for c in range(3):
                values[c].append(back[pl.ds((entry >> code_bits) + c * tiles, 1)])
        sums[...] += node_sums(nodes, values, 3 * tops, 1)
        return 0

    lax.fori_loop(0, (filled + 7) // 8, spread, 0)
    pieces = [[sums[(c * 3 + p) * tops : (c * 3 + p + 1) * tops] for c in range(3)] for p in range(3)]
    found = []
    for p in (0, 2):
        at = (2 + p // 2) * shared
        found.append(
            lookup(
                [two_parts(piece) for piece in pieces[p]],
                [nodes_ref[at + k : at + k + 1] for k in range(shared)],
            )
        )
    added = node_sums(
        [nodes_ref[k : k + 1] for k in range(2 * shared)],
        [[near[c][k : k + 1] for near in found for k in range(shared)] for c in range(3)],
        tops,
    )
    added += jnp.concatenate(pieces[1], axis=0)
    for c in range(3):
        add_halves(total, added, c, tops)
    out_ref[...] = total[...].astype(bf16)


def accel_kernel(mass_ref, *refs):
    out_ref = refs[-1]
    terms = [ref[...].astype(f32) for ref in refs[:-1]]
    while len(terms) > 1:
        terms = [a + b for a, b in zip(terms[::2], terms[1::2])]
    size = mass_ref.shape[0]
    for c in range(3):
        at = slice(c * size, (c + 1) * size)
        out_ref[at] = terms[0][at] / mass_ref[...]


def swapped(block, start):
    lows = range(start, lax.axis_size("dom") - 1, 2)
    return lax.ppermute(block, "dom", [(s, s + 1) for s in lows] + [(s + 1, s) for s in lows])


def from_mate(block, distance):
    return lax.ppermute(
        block, "rep", [(i, i ^ distance) for i in range(lax.axis_size("rep"))]
    )


def across(block, distance):
    return lax.ppermute(
        block, "dom", [(s, s ^ distance) for s in range(lax.axis_size("dom"))]
    )


def on_device(
    coords,
    disp,
    mass,
    stiffness,
    elem_nodes,
    modulus,
    surf_nodes,
    block_region,
    face_pos,
    face_normal,
    tile_slot,
    tile_face,
    tile_weight,
    shared_lo,
    shared_hi,
):
    parts = lax.axis_size("dom")
    assert lax.axis_size("rep") == 4
    nodes_all = disp.shape[2]
    nblk = surf_nodes.shape[1]
    tiles = tile_slot.shape[1]
    cap = max(2, 2 * nblk // parts)
    rows = (3 * cap + 1 + 15) // 16 * 16
    force_rows = (3 * tiles + 15) // 16 * 16
    node_array = jax.ShapeDtypeStruct((3 * nodes_all // lanes, lanes), f32)
    mass_array = jax.ShapeDtypeStruct((nodes_all // lanes, lanes), f32)
    coords = coords.reshape(node_array.shape)
    disp = disp.reshape(node_array.shape)
    mass = mass.reshape(mass_array.shape)
    shared_lo = shared_lo.reshape(-1, lanes)
    shared_hi = shared_hi.reshape(-1, lanes)
    shared = shared_lo.shape[0]
    payload = jax.ShapeDtypeStruct((nblk + (shared + 8) // 8 * 8 + 4 * shared, lanes), f32)

    outgoing = call(
        functools.partial(pack_kernel, cap),
        jax.ShapeDtypeStruct((parts, rows, lanes), bf16),
        [hbm] * 5,
        vmem,
        [
            pltpu.VMEM((nblk // cap, rows, lanes), f32),
            pltpu.SMEM(block_region.shape, jnp.int32),
            pltpu.SMEM(tile_slot.shape, jnp.int32),
            pltpu.VMEM(coords.shape, f32),
            pltpu.VMEM(disp.shape, f32),
            pltpu.VMEM(surf_nodes.shape, jnp.int32),
            pltpu.SemaphoreType.DMA((5,)),
        ],
        1 << 30,
        60,
    )(block_region, tile_slot, coords, disp, surf_nodes)
    arrived = lax.all_to_all(outgoing, "dom", split_axis=0, concat_axis=0, tiled=True)

    part, first, second, tile_ids = call(
        element_kernel,
        (node_array, payload, payload, jax.ShapeDtypeStruct((2, tiles), jnp.int32)),
        [vmem] * 11,
        (vmem,) * 4,
        [
            pltpu.VMEM((24, modulus.shape[1]), f32),
            pltpu.VMEM((3 * nodes_all // wide, wide), f32),
        ],
        1 << 32,
    )(
        tile_slot,
        tile_face,
        disp,
        stiffness,
        modulus,
        elem_nodes,
        mass,
        shared_lo,
        shared_hi,
        surf_nodes,
        block_region,
    )
    first = swapped(first, 0)
    arrived, part = lax.optimization_barrier((arrived, part))
    forces, slots = call(
        functools.partial(tile_kernel, cap),
        (
            jax.ShapeDtypeStruct((force_rows, lanes), bf16),
            jax.ShapeDtypeStruct((parts, lanes), jnp.int32),
        ),
        [smem] + [vmem] * 4,
        (vmem, vmem),
        [pltpu.VMEM((parts * rows, lanes), f32)],
        1 << 28,
    )(
        tile_ids,
        arrived,
        jnp.swapaxes(face_pos, 1, 2),
        jnp.swapaxes(face_normal, 1, 2),
        tile_weight,
    )
    forces, second = lax.optimization_barrier((forces, second))
    held, distance = forces, 1
    while 4 * distance < parts:
        held = jnp.concatenate([held, across(held, distance)], axis=0)
        distance *= 2
    back = [held] + [across(held, d) for d in range(distance, parts, distance)]
    second = swapped(second, 1)
    part, mass, surf, nodes, regions = call(
        neighbour_kernel,
        (
            node_array,
            mass_array,
            jax.ShapeDtypeStruct((3 * nblk, lanes), jnp.int32),
            jax.ShapeDtypeStruct((4 * shared, lanes), jnp.int32),
            jax.ShapeDtypeStruct((3, nblk), jnp.int32),
        ),
        [vmem] * 8,
        (vmem,) * 5,
        [],
        1 << 26,
    )(part, mass, shared_lo, shared_hi, surf_nodes, block_region, first, second)
    picks = call(
        functools.partial(list_kernel, cap, tiles, force_rows),
        jax.ShapeDtypeStruct((1, parts * tiles + 16), jnp.int32),
        [smem, smem],
        smem,
        [pltpu.SMEM((3 * parts,), jnp.int32)],
        1 << 24,
    )(slots, regions)
    own = call(
        functools.partial(contact_kernel, tiles),
        jax.ShapeDtypeStruct(node_array.shape, bf16),
        [smem] + [vmem] * (3 + len(back)),
        vmem,
        [
            pltpu.VMEM((parts * force_rows, lanes), f32),
            pltpu.VMEM((9 * nodes_all // wide, wide), f32),
            pltpu.VMEM(node_array.shape, f32),
        ],
        1 << 28,
    )(picks, surf, nodes, part, *back)
    accel = call(accel_kernel, node_array, [vmem] * 5, vmem, [], 1 << 24)(
        mass, own, *[from_mate(own, k) for k in (3, 2, 1)]
    )
    return accel.reshape(1, 3, nodes_all)


def solution(mesh):
    in_specs = (
        P("dom", None, None),
        P("dom", None, None),
        P("dom", None),
        P(),
        P("dom", None, "rep"),
        P("dom", "rep"),
        P("dom", None, None),
        P("dom", None),
        P("dom", None, None, None),
        P("dom", None, None, None),
        P("dom", "rep"),
        P("dom", "rep"),
        P("dom", "rep", None, None),
        P("dom", None),
        P("dom", None),
    )
    out_specs = P("dom", None, None)
    return jax.shard_map(
        on_device, mesh=mesh, in_specs=in_specs, out_specs=out_specs, check_vma=False
    )
```

```python
import functools

import jax
import jax.numpy as jnp
from jax import lax
from jax.experimental import pallas as pl
from jax.experimental.pallas import tpu as pltpu
from jax.sharding import PartitionSpec as P

penalty = 4.0
lanes = 128
wide = 256
code_bits = 12
code = 1 << code_bits
vmem = pl.BlockSpec(memory_space=pltpu.VMEM)
smem = pl.BlockSpec(memory_space=pltpu.SMEM)
hbm = pl.BlockSpec(memory_space=pltpu.HBM)
f32 = jnp.float32
bf16 = jnp.bfloat16


def call(body, out_shape, in_specs, out_specs, scratch, flops, vmem_mib=32):
    return pl.pallas_call(
        body,
        out_shape=out_shape,
        in_specs=in_specs,
        out_specs=out_specs,
        scratch_shapes=scratch,
        compiler_params=pltpu.CompilerParams(vmem_limit_bytes=vmem_mib * 1024 * 1024),
        cost_estimate=pl.CostEstimate(flops=flops, bytes_accessed=1 << 20, transcendentals=0),
    )


def rows_like(count):
    return lax.broadcasted_iota(jnp.int32, (count, lanes), 0).astype(f32).astype(bf16)


def pick(match, values):
    return jnp.where(match, values, jnp.zeros((), bf16))


def upper(nodes):
    return [(row >> 8).astype(f32).astype(bf16) for row in nodes]


def one_hot(nodes):
    line = lax.broadcasted_iota(jnp.int32, (wide, lanes), 0).astype(f32).astype(bf16)
    low = [(row & (wide - 1)).astype(f32).astype(bf16) for row in nodes]
    one, zero = jnp.ones((), bf16), jnp.zeros((), bf16)
    return jnp.concatenate([jnp.where(line == row, one, zero) for row in low], axis=1)


def halves(ref, c, tops):
    at = c * 2 * tops
    return jnp.concatenate(
        [ref[pl.ds(at, tops, stride=2)], ref[pl.ds(at + 1, tops, stride=2)]], axis=1
    )


def two_parts(x):
    coarse = x.astype(bf16)
    return [coarse, (x - coarse.astype(f32)).astype(bf16)]


def row_sums(rows):
    line = lax.broadcasted_iota(jnp.int32, rows[0].shape, 0)
    for step in (4, 2, 1):
        first = (line & step) == 0
        rows = [
            jnp.where(first, a, b)
            + jnp.where(first, pltpu.roll(a, 8 - step, 0), pltpu.roll(b, step, 0))
            for a, b in zip(rows[:step], rows[step:])
        ]
    return rows[0]


def lookup(tables, nodes):
    tops = tables[0][0].shape[0]
    stacked = jnp.concatenate([part for table in tables for part in table], axis=0)
    found = jnp.dot(stacked, one_hot(nodes), preferred_element_type=f32)
    line = lax.broadcasted_iota(jnp.int32, (tops, lanes), 0)
    rows = [[] for _ in tables]
    for i, row in enumerate(nodes):
        match = line == (row >> 8)
        at = 0
        for c, table in enumerate(tables):
            here = found[at : at + tops, i * lanes : (i + 1) * lanes]
            for p in range(1, len(table)):
                here += found[at + p * tops : at + (p + 1) * tops, i * lanes : (i + 1) * lanes]
            at += len(table) * tops
            here = jnp.where(match, here, 0.0)
            rows[c].append(sum(here[k : k + 8] for k in range(8, tops, 8)) + here[:8])
    if len(nodes) == 8:
        return [row_sums(held) for held in rows]
    return [
        jnp.concatenate([jnp.sum(row, axis=0, keepdims=True) for row in held], axis=0) for held in rows
    ]


def node_sums(nodes, values, tops, parts=2):
    line = rows_like(tops)
    comps = len(values)
    left = []
    for i, top in enumerate(upper(nodes)):
        match = line == top
        pieces = [v[i].astype(bf16) for v in values]
        if parts == 2:
            pieces += [(v[i] - w.astype(f32)).astype(bf16) for v, w in zip(values, pieces)]
        left.append(jnp.concatenate([pick(match, piece) for piece in pieces], axis=0))
    both = lax.dot_general(
        jnp.concatenate(left, axis=1),
        one_hot(nodes),
        (((1,), (1,)), ((), ())),
        preferred_element_type=f32,
    )
    return both if parts == 1 else both[: comps * tops] + both[comps * tops :]


def add_halves(ref, sums, c, tops, row=None):
    at = (c if row is None else row) * 2 * tops
    for half in range(2):
        ref[pl.ds(at + half, tops, stride=2)] += sums[
            c * tops : (c + 1) * tops, half * lanes : (half + 1) * lanes
        ]


def pack_kernel(
    cap, region_hbm, slot_hbm, coords_hbm, disp_hbm, surf_hbm, out_ref,
    stage, region_ref, slot_ref, coords_ref, disp_ref, surf_ref, sems,
):
    sources = (coords_hbm, disp_hbm, slot_hbm, surf_hbm, region_hbm)
    places = (coords_ref, disp_ref, slot_ref, surf_ref, region_ref)
    copies = [
        pltpu.make_async_copy(a, b, sems.at[i]) for i, (a, b) in enumerate(zip(sources, places))
    ]
    for copy in copies:
        copy.start()
    parts, rows, _ = out_ref.shape
    nblk = surf_ref.shape[1]
    tiles = slot_ref.shape[1]
    tops = coords_ref.shape[0] // 6
    for copy in copies:
        copy.wait()
    rest = (rows - 3 * cap, lanes)
    lane = lax.broadcasted_iota(jnp.int32, rest, 1)
    line = lax.broadcasted_iota(jnp.int32, rest, 0)
    tail = jnp.zeros(rest, f32)
    for t in range(tiles):
        tail = jnp.where((lane == t) & (line == 0), slot_ref[0, t].astype(f32), tail)
    for q in range(nblk // cap):
        stage[q, 3 * cap :] = tail
    empty = jnp.concatenate([jnp.zeros((3 * cap, lanes), f32), tail], axis=0).astype(bf16)
    for j in range(parts):
        out_ref[j] = empty
    tables = [
        [(halves(coords_ref, c, tops) + halves(disp_ref, c, tops)).astype(bf16)] for c in range(3)
    ]
    size = min(cap, 8)
    for first in range(0, nblk, 8):
        values = lookup(tables, [surf_ref[0, first + i : first + i + 1] for i in range(8)])
        for b in range(first, first + 8, size):
            for c in range(3):
                at = c * cap + b % cap
                stage[b // cap, at : at + size] = values[c][b - first : b - first + size]
    for q in range(nblk // cap):
        out_ref[region_ref[0, q * cap]] = stage[q].astype(bf16)


def element_kernel(
    slot_ref, face_ref, disp_ref, stiff_ref, modulus_ref, nodes_ref, mass_ref, lo_ref, hi_ref, surf_ref, region_ref,
    out_ref, first_ref, second_ref, tiles_ref, local, sums,
):
    tiles_ref[0:1] = slot_ref[...]
    tiles_ref[1:2] = face_ref[...]
    corners, count = nodes_ref.shape[1:]
    tops = disp_ref.shape[0] // 6
    tables = [two_parts(halves(disp_ref, c, tops)) for c in range(3)]
    cuts = [slice(g * lanes, (g + 1) * lanes) for g in range(count // lanes)]
    nodes = [[nodes_ref[0, a : a + 1, cut] for a in range(corners)] for cut in cuts]
    for cut, here in zip(cuts, nodes):
        values = lookup(tables, here)
        for c in range(3):
            local[c * corners : (c + 1) * corners, cut] = values[c]
    force = jnp.dot(
        stiff_ref[...], local[...], precision=lax.Precision.HIGHEST, preferred_element_type=f32
    )
    local[...] = -(force * modulus_ref[...])
    for g, (cut, here) in enumerate(zip(cuts, nodes)):
        values = [
            [local[c * corners + a : c * corners + a + 1, cut] for a in range(corners)]
            for c in range(3)
        ]
        added = node_sums(here, values, tops)
        sums[...] = added if g == 0 else sums[...] + added
    out_ref[...] = jnp.zeros_like(out_ref)
    for c in range(3):
        add_halves(out_ref, sums[...], c, tops)
    even = lax.axis_index("dom") % 2 == 0
    nblk = surf_ref.shape[1]
    shared = lo_ref.shape[0]
    head = first_ref.shape[0] - 4 * shared
    tables = [two_parts(sums[c * tops : (c + 1) * tops]) for c in range(3)]
    tables.append(two_parts(halves(mass_ref, 0, tops)))
    values = lookup(tables, [ref[k : k + 1] for ref in (lo_ref, hi_ref) for k in range(shared)])
    lower_list, upper_list = lo_ref[...].astype(f32), hi_ref[...].astype(f32)
    for ref, up in ((first_ref, even), (second_ref, jnp.logical_not(even))):
        ref[:nblk] = surf_ref[0].astype(f32)
        ref[nblk : nblk + shared] = jnp.where(up, upper_list, lower_list)
        ref[nblk + shared : nblk + shared + 1] = region_ref[...].astype(f32)
        ref[nblk + shared + 1 : head] = jnp.zeros((head - nblk - shared - 1, lanes), f32)
        for c in range(4):
            below, above = values[c][:shared], values[c][shared:]
            ref[head + c * shared : head + (c + 1) * shared] = jnp.where(up, above, below)


def neighbour_kernel(
    part_ref, mass_ref, lo_ref, hi_ref, own_surf_ref, region_ref, first_ref, second_ref,
    out_ref, out_mass_ref, surf_ref, nodes_ref, regions_ref,
):
    even = lax.axis_index("dom") % 2 == 0
    tops = mass_ref.shape[0] // 2
    nblk = own_surf_ref.shape[1]
    nodes_all = mass_ref.shape[0] * lanes
    shared = lo_ref.shape[0]
    head = first_ref.shape[0] - 4 * shared
    out_ref[...] = part_ref[...]
    out_mass_ref[...] = mass_ref[...]
    first, second = first_ref[...], second_ref[...]
    packs = [jnp.where(even, second, first), jnp.where(even, first, second)]
    for i, pack in enumerate(packs):
        surf_ref[2 * i * nblk : (2 * i + 1) * nblk] = pack[:nblk].astype(jnp.int32) + 2 * i * nodes_all
        nodes_ref[(2 + i) * shared : (3 + i) * shared] = pack[nblk : nblk + shared].astype(jnp.int32)
        regions_ref[2 * i : 2 * i + 1] = pack[nblk + shared : nblk + shared + 1].astype(jnp.int32)
    surf_ref[nblk : 2 * nblk] = own_surf_ref[0] + nodes_all
    regions_ref[1:2] = region_ref[...]
    nodes_ref[:shared] = lo_ref[...]
    nodes_ref[shared : 2 * shared] = hi_ref[...]
    nodes = [ref[k : k + 1] for ref in (lo_ref, hi_ref) for k in range(shared)]
    values = [
        [pack[head + c * shared + k : head + c * shared + k + 1] for pack in packs for k in range(shared)]
        for c in range(4)
    ]
    sums = node_sums(nodes, values, tops)
    for c in range(3):
        add_halves(out_ref, sums, c, tops)
    add_halves(out_mass_ref, sums, 3, tops, 0)


def tile_kernel(cap, tiles_ref, got_ref, pos_ref, normal_ref, weight_ref, out_ref, slots_ref, flat):
    parts, rows, _ = got_ref.shape
    tiles = tiles_ref.shape[1]
    shift = cap.bit_length() - 1
    faces = [tiles_ref[1, t] for t in range(tiles)]
    starts = [(tiles_ref[0, t] >> shift) * rows + (tiles_ref[0, t] & (cap - 1)) for t in range(tiles)]
    for j in range(parts):
        flat[j * rows : (j + 1) * rows] = got_ref[j].astype(f32)
    slots_ref[...] = jnp.concatenate(
        [flat[j * rows + 3 * cap : j * rows + 3 * cap + 1] for j in range(parts)], axis=0
    ).astype(jnp.int32)
    x = jnp.concatenate(
        [flat[pl.ds(at + c * cap, 1)] for c in range(3) for at in starts], axis=0
    )
    weights = weight_ref[0].reshape(tiles * lanes, lanes)
    crossed = lax.dot_general(
        x.astype(bf16), weights, (((1,), (1,)), ((), ())), preferred_element_type=f32
    )
    line = lax.broadcasted_iota(jnp.int32, (tiles, lanes), 0)
    gap = jnp.zeros((tiles, lanes), f32)
    normals = []
    for c in range(3):
        interp = jnp.zeros((tiles, lanes), f32)
        for t in range(tiles):
            here = crossed[c * tiles : (c + 1) * tiles, t * lanes : (t + 1) * lanes]
            interp = jnp.where(line == t, here, interp)
        normal = jnp.concatenate([normal_ref[0, c, pl.ds(f, 1)] for f in faces], axis=0)
        pos = jnp.concatenate([pos_ref[0, c, pl.ds(f, 1)] for f in faces], axis=0)
        gap += normal * (interp - pos)
        normals.append(normal)
    pressure = penalty * jnp.maximum(-gap, 0.0)
    push = [pressure * normal for normal in normals]
    spread = jnp.concatenate(
        [
            jnp.concatenate([jnp.where(line == t, p, 0.0) for p in push], axis=0).astype(bf16)
            for t in range(tiles)
        ],
        axis=1,
    )
    forces = jnp.dot(spread, weights, preferred_element_type=f32).astype(bf16)
    pad = out_ref.shape[0] - forces.shape[0]
    if pad:
        forces = jnp.concatenate([forces, jnp.zeros((pad, lanes), bf16)], axis=0)
    out_ref[...] = forces


def list_kernel(cap, tiles, force_rows, slots_ref, regions_ref, list_ref, run_of):
    parts = slots_ref.shape[0]
    nblk = regions_ref.shape[1]
    shift = cap.bit_length() - 1
    me = lax.axis_index("dom")
    for p in range(3):
        for q in range(nblk // cap):
            run_of[p * parts + regions_ref[p, q * cap]] = p * nblk + q * cap

    def pick(place, filled):
        j = me ^ place
        slots = [slots_ref[j, t] for t in range(tiles)]
        which = [(slot >> shift) - me + 1 for slot in slots]
        kept = [(p >= 0) & (p <= 2) for p in which]
        runs = [run_of[jnp.where(own, p, 0) * parts + j] for own, p in zip(kept, which)]
        places = []
        for own in kept:
            places.append(filled)
            filled = filled + jnp.where(own, 1, 0)
        for t in range(tiles):
            entry = (place * force_rows + t) * code + (slots[t] & (cap - 1)) + runs[t]
            list_ref[0, places[t]] = entry
        return filled

    filled = lax.fori_loop(0, parts, pick, jnp.int32(0))
    for i in range(24):
        list_ref[0, filled + i] = 0
    list_ref[0, list_ref.shape[1] - 1] = filled


def contact_kernel(tiles, list_ref, surf_ref, nodes_ref, part_ref, *refs):
    back_refs, out_ref, back, sums, total = refs[:-4], refs[-4], refs[-3], refs[-2], refs[-1]
    size = back_refs[0].shape[0]
    tops = part_ref.shape[0] // 6
    shared = nodes_ref.shape[0] // 4
    total[...] = part_ref[...]
    for i, ref in enumerate(back_refs):
        back[i * size : (i + 1) * size] = ref[...].astype(f32)
    filled = list_ref[0, list_ref.shape[1] - 1]

    def group(g):
        nodes, values = [], [[], [], []]
        for i in range(8):
            entry = list_ref[0, g * 8 + i]
            row = surf_ref[pl.ds(entry & (code - 1), 1)]
            nodes.append(jnp.where(g * 8 + i < filled, row, -1))
            for c in range(3):
                values[c].append(back[pl.ds((entry >> code_bits) + c * tiles, 1)])
        return node_sums(nodes, values, 3 * tops, 1)

    def spread(g, _):
        sums[...] += group(g)
        return 0

    sums[...] = group(0) + group(1) + group(2)
    lax.fori_loop(3, (filled + 7) // 8, spread, 0)
    pieces = [[sums[(c * 3 + p) * tops : (c * 3 + p + 1) * tops] for c in range(3)] for p in range(3)]
    found = []
    for p in (0, 2):
        at = (2 + p // 2) * shared
        found.append(
            lookup(
                [two_parts(piece) for piece in pieces[p]],
                [nodes_ref[at + k : at + k + 1] for k in range(shared)],
            )
        )
    added = node_sums(
        [nodes_ref[k : k + 1] for k in range(2 * shared)],
        [[near[c][k : k + 1] for near in found for k in range(shared)] for c in range(3)],
        tops,
    )
    added += jnp.concatenate(pieces[1], axis=0)
    for c in range(3):
        add_halves(total, added, c, tops)
    out_ref[...] = total[...].astype(bf16)


def accel_kernel(mass_ref, *refs):
    out_ref = refs[-1]
    terms = [ref[...].astype(f32) for ref in refs[:-1]]
    while len(terms) > 1:
        terms = [a + b for a, b in zip(terms[::2], terms[1::2])]
    size = mass_ref.shape[0]
    for c in range(3):
        at = slice(c * size, (c + 1) * size)
        out_ref[at] = terms[0][at] / mass_ref[...]


def swapped(block, start):
    lows = range(start, lax.axis_size("dom") - 1, 2)
    return lax.ppermute(block, "dom", [(s, s + 1) for s in lows] + [(s + 1, s) for s in lows])


def from_mate(block, distance):
    return lax.ppermute(
        block, "rep", [(i, i ^ distance) for i in range(lax.axis_size("rep"))]
    )


def across(block, distance):
    return lax.ppermute(
        block, "dom", [(s, s ^ distance) for s in range(lax.axis_size("dom"))]
    )


def on_device(
    coords,
    disp,
    mass,
    stiffness,
    elem_nodes,
    modulus,
    surf_nodes,
    block_region,
    face_pos,
    face_normal,
    tile_slot,
    tile_face,
    tile_weight,
    shared_lo,
    shared_hi,
):
    parts = lax.axis_size("dom")
    assert lax.axis_size("rep") == 4
    nodes_all = disp.shape[2]
    nblk = surf_nodes.shape[1]
    tiles = tile_slot.shape[1]
    cap = max(2, 2 * nblk // parts)
    rows = (3 * cap + 1 + 15) // 16 * 16
    force_rows = (3 * tiles + 15) // 16 * 16
    node_array = jax.ShapeDtypeStruct((3 * nodes_all // lanes, lanes), f32)
    mass_array = jax.ShapeDtypeStruct((nodes_all // lanes, lanes), f32)
    coords = coords.reshape(node_array.shape)
    disp = disp.reshape(node_array.shape)
    mass = mass.reshape(mass_array.shape)
    shared_lo = shared_lo.reshape(-1, lanes)
    shared_hi = shared_hi.reshape(-1, lanes)
    shared = shared_lo.shape[0]
    payload = jax.ShapeDtypeStruct((nblk + (shared + 8) // 8 * 8 + 4 * shared, lanes), f32)

    outgoing = call(
        functools.partial(pack_kernel, cap),
        jax.ShapeDtypeStruct((parts, rows, lanes), bf16),
        [hbm] * 5,
        vmem,
        [
            pltpu.VMEM((nblk // cap, rows, lanes), f32),
            pltpu.SMEM(block_region.shape, jnp.int32),
            pltpu.SMEM(tile_slot.shape, jnp.int32),
            pltpu.VMEM(coords.shape, f32),
            pltpu.VMEM(disp.shape, f32),
            pltpu.VMEM(surf_nodes.shape, jnp.int32),
            pltpu.SemaphoreType.DMA((5,)),
        ],
        1 << 30,
        60,
    )(block_region, tile_slot, coords, disp, surf_nodes)
    arrived = lax.all_to_all(outgoing, "dom", split_axis=0, concat_axis=0, tiled=True)

    part, first, second, tile_ids = call(
        element_kernel,
        (node_array, payload, payload, jax.ShapeDtypeStruct((2, tiles), jnp.int32)),
        [vmem] * 11,
        (vmem,) * 4,
        [
            pltpu.VMEM((24, modulus.shape[1]), f32),
            pltpu.VMEM((3 * nodes_all // wide, wide), f32),
        ],
        1 << 32,
    )(
        tile_slot,
        tile_face,
        disp,
        stiffness,
        modulus,
        elem_nodes,
        mass,
        shared_lo,
        shared_hi,
        surf_nodes,
        block_region,
    )
    first = swapped(first, 0)
    arrived, part = lax.optimization_barrier((arrived, part))
    forces, slots = call(
        functools.partial(tile_kernel, cap),
        (
            jax.ShapeDtypeStruct((force_rows, lanes), bf16),
            jax.ShapeDtypeStruct((parts, lanes), jnp.int32),
        ),
        [smem] + [vmem] * 4,
        (vmem, vmem),
        [pltpu.VMEM((parts * rows, lanes), f32)],
        1 << 28,
    )(
        tile_ids,
        arrived,
        jnp.swapaxes(face_pos, 1, 2),
        jnp.swapaxes(face_normal, 1, 2),
        tile_weight,
    )
    forces, second = lax.optimization_barrier((forces, second))
    held, distance = forces, 1
    while 4 * distance < parts:
        held = jnp.concatenate([held, across(held, distance)], axis=0)
        distance *= 2
    back = [held] + [across(held, d) for d in range(distance, parts, distance)]
    second = swapped(second, 1)
    part, mass, surf, nodes, regions = call(
        neighbour_kernel,
        (
            node_array,
            mass_array,
            jax.ShapeDtypeStruct((3 * nblk, lanes), jnp.int32),
            jax.ShapeDtypeStruct((4 * shared, lanes), jnp.int32),
            jax.ShapeDtypeStruct((3, nblk), jnp.int32),
        ),
        [vmem] * 8,
        (vmem,) * 5,
        [],
        1 << 26,
    )(part, mass, shared_lo, shared_hi, surf_nodes, block_region, first, second)
    picks = call(
        functools.partial(list_kernel, cap, tiles, force_rows),
        jax.ShapeDtypeStruct((1, parts * tiles + 32), jnp.int32),
        [smem, smem],
        smem,
        [pltpu.SMEM((3 * parts,), jnp.int32)],
        1 << 24,
    )(slots, regions)
    own = call(
        functools.partial(contact_kernel, tiles),
        jax.ShapeDtypeStruct(node_array.shape, bf16),
        [smem] + [vmem] * (3 + len(back)),
        vmem,
        [
            pltpu.VMEM((parts * force_rows, lanes), f32),
            pltpu.VMEM((9 * nodes_all // wide, wide), f32),
            pltpu.VMEM(node_array.shape, f32),
        ],
        1 << 28,
    )(picks, surf, nodes, part, *back)
    accel = call(accel_kernel, node_array, [vmem] * 5, vmem, [], 1 << 24)(
        mass, own, *[from_mate(own, k) for k in (3, 2, 1)]
    )
    return accel.reshape(1, 3, nodes_all)


def solution(mesh):
    in_specs = (
        P("dom", None, None),
        P("dom", None, None),
        P("dom", None),
        P(),
        P("dom", None, "rep"),
        P("dom", "rep"),
        P("dom", None, None),
        P("dom", None),
        P("dom", None, None, None),
        P("dom", None, None, None),
        P("dom", "rep"),
        P("dom", "rep"),
        P("dom", "rep", None, None),
        P("dom", None),
        P("dom", None),
    )
    out_specs = P("dom", None, None)
    return jax.shard_map(
        on_device, mesh=mesh, in_specs=in_specs, out_specs=out_specs, check_vma=False
    )
```

```python
import functools

import jax
import jax.numpy as jnp
from jax import lax
from jax.experimental import pallas as pl
from jax.experimental.pallas import tpu as pltpu
from jax.sharding import PartitionSpec as P

penalty = 4.0
lanes = 128
wide = 256
code_bits = 12
code = 1 << code_bits
vmem = pl.BlockSpec(memory_space=pltpu.VMEM)
smem = pl.BlockSpec(memory_space=pltpu.SMEM)
hbm = pl.BlockSpec(memory_space=pltpu.HBM)
f32 = jnp.float32
bf16 = jnp.bfloat16


def call(body, out_shape, in_specs, out_specs, scratch, flops, vmem_mib=32):
    return pl.pallas_call(
        body,
        out_shape=out_shape,
        in_specs=in_specs,
        out_specs=out_specs,
        scratch_shapes=scratch,
        compiler_params=pltpu.CompilerParams(vmem_limit_bytes=vmem_mib * 1024 * 1024),
        cost_estimate=pl.CostEstimate(flops=flops, bytes_accessed=1 << 20, transcendentals=0),
    )


def rows_like(count):
    return lax.broadcasted_iota(jnp.int32, (count, lanes), 0).astype(f32).astype(bf16)


def pick(match, values):
    return jnp.where(match, values, jnp.zeros((), bf16))


def upper(nodes):
    return [(row >> 8).astype(f32).astype(bf16) for row in nodes]


def one_hot(nodes):
    line = lax.broadcasted_iota(jnp.int32, (wide, lanes), 0).astype(f32).astype(bf16)
    low = [(row & (wide - 1)).astype(f32).astype(bf16) for row in nodes]
    one, zero = jnp.ones((), bf16), jnp.zeros((), bf16)
    return jnp.concatenate([jnp.where(line == row, one, zero) for row in low], axis=1)


def halves(ref, c, tops):
    at = c * 2 * tops
    return jnp.concatenate(
        [ref[pl.ds(at, tops, stride=2)], ref[pl.ds(at + 1, tops, stride=2)]], axis=1
    )


def two_parts(x):
    coarse = x.astype(bf16)
    return [coarse, (x - coarse.astype(f32)).astype(bf16)]


def row_sums(rows):
    line = lax.broadcasted_iota(jnp.int32, rows[0].shape, 0)
    for step in (4, 2, 1):
        first = (line & step) == 0
        rows = [
            jnp.where(first, a, b)
            + jnp.where(first, pltpu.roll(a, 8 - step, 0), pltpu.roll(b, step, 0))
            for a, b in zip(rows[:step], rows[step:])
        ]
    return rows[0]


def lookup(tables, nodes):
    tops = tables[0][0].shape[0]
    stacked = jnp.concatenate([part for table in tables for part in table], axis=0)
    found = jnp.dot(stacked, one_hot(nodes), preferred_element_type=f32)
    line = lax.broadcasted_iota(jnp.int32, (tops, lanes), 0)
    rows = [[] for _ in tables]
    for i, row in enumerate(nodes):
        match = line == (row >> 8)
        at = 0
        for c, table in enumerate(tables):
            here = found[at : at + tops, i * lanes : (i + 1) * lanes]
            for p in range(1, len(table)):
                here += found[at + p * tops : at + (p + 1) * tops, i * lanes : (i + 1) * lanes]
            at += len(table) * tops
            here = jnp.where(match, here, 0.0)
            rows[c].append(sum(here[k : k + 8] for k in range(8, tops, 8)) + here[:8])
    if len(nodes) == 8:
        return [row_sums(held) for held in rows]
    return [
        jnp.concatenate([jnp.sum(row, axis=0, keepdims=True) for row in held], axis=0) for held in rows
    ]


def node_sums(nodes, values, tops, parts=2):
    line = rows_like(tops)
    comps = len(values)
    left = []
    for i, top in enumerate(upper(nodes)):
        match = line == top
        pieces = [v[i].astype(bf16) for v in values]
        if parts == 2:
            pieces += [(v[i] - w.astype(f32)).astype(bf16) for v, w in zip(values, pieces)]
        left.append(jnp.concatenate([pick(match, piece) for piece in pieces], axis=0))
    both = lax.dot_general(
        jnp.concatenate(left, axis=1),
        one_hot(nodes),
        (((1,), (1,)), ((), ())),
        preferred_element_type=f32,
    )
    return both if parts == 1 else both[: comps * tops] + both[comps * tops :]


def add_halves(ref, sums, c, tops, row=None):
    at = (c if row is None else row) * 2 * tops
    for half in range(2):
        ref[pl.ds(at + half, tops, stride=2)] += sums[
            c * tops : (c + 1) * tops, half * lanes : (half + 1) * lanes
        ]


def pack_kernel(
    cap, region_hbm, slot_hbm, coords_hbm, disp_hbm, surf_hbm, out_ref,
    stage, region_ref, slot_ref, coords_ref, disp_ref, surf_ref, sems,
):
    sources = (coords_hbm, disp_hbm, slot_hbm, surf_hbm, region_hbm)
    places = (coords_ref, disp_ref, slot_ref, surf_ref, region_ref)
    copies = [
        pltpu.make_async_copy(a, b, sems.at[i]) for i, (a, b) in enumerate(zip(sources, places))
    ]
    for copy in copies:
        copy.start()
    parts, rows, _ = out_ref.shape
    nblk = surf_ref.shape[1]
    tiles = slot_ref.shape[1]
    tops = coords_ref.shape[0] // 6
    for copy in copies:
        copy.wait()
    rest = (rows - 3 * cap, lanes)
    lane = lax.broadcasted_iota(jnp.int32, rest, 1)
    line = lax.broadcasted_iota(jnp.int32, rest, 0)
    tail = jnp.zeros(rest, f32)
    for t in range(tiles):
        tail = jnp.where((lane == t) & (line == 0), slot_ref[0, t].astype(f32), tail)
    for q in range(nblk // cap):
        stage[q, 3 * cap :] = tail
    empty = jnp.concatenate([jnp.zeros((3 * cap, lanes), f32), tail], axis=0).astype(bf16)
    for j in range(parts):
        out_ref[j] = empty
    tables = [
        [(halves(coords_ref, c, tops) + halves(disp_ref, c, tops)).astype(bf16)] for c in range(3)
    ]
    size = min(cap, 8)
    for first in range(0, nblk, 8):
        values = lookup(tables, [surf_ref[0, first + i : first + i + 1] for i in range(8)])
        for b in range(first, first + 8, size):
            for c in range(3):
                at = c * cap + b % cap
                stage[b // cap, at : at + size] = values[c][b - first : b - first + size]
    for q in range(nblk // cap):
        out_ref[region_ref[0, q * cap]] = stage[q].astype(bf16)


def element_kernel(
    slot_ref, face_ref, disp_ref, stiff_ref, modulus_ref, nodes_ref, mass_ref, lo_ref, hi_ref, surf_ref, region_ref,
    out_ref, first_ref, second_ref, tiles_ref, local, sums,
):
    tiles_ref[0:1] = slot_ref[...]
    tiles_ref[1:2] = face_ref[...]
    corners, count = nodes_ref.shape[1:]
    tops = disp_ref.shape[0] // 6
    tables = [two_parts(halves(disp_ref, c, tops)) for c in range(3)]
    cuts = [slice(g * lanes, (g + 1) * lanes) for g in range(count // lanes)]
    nodes = [[nodes_ref[0, a : a + 1, cut] for a in range(corners)] for cut in cuts]
    for cut, here in zip(cuts, nodes):
        values = lookup(tables, here)
        for c in range(3):
            local[c * corners : (c + 1) * corners, cut] = values[c]
    force = jnp.dot(
        stiff_ref[...], local[...], precision=lax.Precision.HIGHEST, preferred_element_type=f32
    )
    local[...] = -(force * modulus_ref[...])
    for g, (cut, here) in enumerate(zip(cuts, nodes)):
        values = [
            [local[c * corners + a : c * corners + a + 1, cut] for a in range(corners)]
            for c in range(3)
        ]
        added = node_sums(here, values, tops)
        sums[...] = added if g == 0 else sums[...] + added
    out_ref[...] = jnp.zeros_like(out_ref)
    for c in range(3):
        add_halves(out_ref, sums[...], c, tops)
    even = lax.axis_index("dom") % 2 == 0
    nblk = surf_ref.shape[1]
    shared = lo_ref.shape[0]
    head = first_ref.shape[0] - 4 * shared
    tables = [two_parts(sums[c * tops : (c + 1) * tops]) for c in range(3)]
    tables.append(two_parts(halves(mass_ref, 0, tops)))
    values = lookup(tables, [ref[k : k + 1] for ref in (lo_ref, hi_ref) for k in range(shared)])
    lower_list, upper_list = lo_ref[...].astype(f32), hi_ref[...].astype(f32)
    for ref, up in ((first_ref, even), (second_ref, jnp.logical_not(even))):
        ref[:nblk] = surf_ref[0].astype(f32)
        ref[nblk : nblk + shared] = jnp.where(up, upper_list, lower_list)
        ref[nblk + shared : nblk + shared + 1] = region_ref[...].astype(f32)
        ref[nblk + shared + 1 : head] = jnp.zeros((head - nblk - shared - 1, lanes), f32)
        for c in range(4):
            below, above = values[c][:shared], values[c][shared:]
            ref[head + c * shared : head + (c + 1) * shared] = jnp.where(up, above, below)


def neighbour_kernel(
    part_ref, mass_ref, lo_ref, hi_ref, own_surf_ref, region_ref, first_ref, second_ref,
    out_ref, out_mass_ref, surf_ref, nodes_ref, regions_ref,
):
    even = lax.axis_index("dom") % 2 == 0
    tops = mass_ref.shape[0] // 2
    nblk = own_surf_ref.shape[1]
    nodes_all = mass_ref.shape[0] * lanes
    shared = lo_ref.shape[0]
    head = first_ref.shape[0] - 4 * shared
    out_ref[...] = part_ref[...]
    out_mass_ref[...] = mass_ref[...]
    first, second = first_ref[...], second_ref[...]
    packs = [jnp.where(even, second, first), jnp.where(even, first, second)]
    for i, pack in enumerate(packs):
        surf_ref[2 * i * nblk : (2 * i + 1) * nblk] = pack[:nblk].astype(jnp.int32) + 2 * i * nodes_all
        nodes_ref[(2 + i) * shared : (3 + i) * shared] = pack[nblk : nblk + shared].astype(jnp.int32)
        regions_ref[2 * i : 2 * i + 1] = pack[nblk + shared : nblk + shared + 1].astype(jnp.int32)
    surf_ref[nblk : 2 * nblk] = own_surf_ref[0] + nodes_all
    regions_ref[1:2] = region_ref[...]
    nodes_ref[:shared] = lo_ref[...]
    nodes_ref[shared : 2 * shared] = hi_ref[...]
    nodes = [ref[k : k + 1] for ref in (lo_ref, hi_ref) for k in range(shared)]
    values = [
        [pack[head + c * shared + k : head + c * shared + k + 1] for pack in packs for k in range(shared)]
        for c in range(4)
    ]
    sums = node_sums(nodes, values, tops)
    for c in range(3):
        add_halves(out_ref, sums, c, tops)
    add_halves(out_mass_ref, sums, 3, tops, 0)


def tile_kernel(cap, tiles_ref, got_ref, pos_ref, normal_ref, weight_ref, out_ref, slots_ref, flat):
    parts, rows, _ = got_ref.shape
    tiles = tiles_ref.shape[1]
    shift = cap.bit_length() - 1
    faces = [tiles_ref[1, t] for t in range(tiles)]
    starts = [(tiles_ref[0, t] >> shift) * rows + (tiles_ref[0, t] & (cap - 1)) for t in range(tiles)]
    for j in range(parts):
        flat[j * rows : (j + 1) * rows] = got_ref[j].astype(f32)
    slots_ref[...] = jnp.concatenate(
        [flat[j * rows + 3 * cap : j * rows + 3 * cap + 1] for j in range(parts)], axis=0
    ).astype(jnp.int32)
    x = jnp.concatenate(
        [flat[pl.ds(at + c * cap, 1)] for c in range(3) for at in starts], axis=0
    )
    weights = weight_ref[0].reshape(tiles * lanes, lanes)
    crossed = lax.dot_general(
        x.astype(bf16), weights, (((1,), (1,)), ((), ())), preferred_element_type=f32
    )
    line = lax.broadcasted_iota(jnp.int32, (tiles, lanes), 0)
    gap = jnp.zeros((tiles, lanes), f32)
    normals = []
    for c in range(3):
        interp = jnp.zeros((tiles, lanes), f32)
        for t in range(tiles):
            here = crossed[c * tiles : (c + 1) * tiles, t * lanes : (t + 1) * lanes]
            interp = jnp.where(line == t, here, interp)
        normal = jnp.concatenate([normal_ref[0, c, pl.ds(f, 1)] for f in faces], axis=0)
        pos = jnp.concatenate([pos_ref[0, c, pl.ds(f, 1)] for f in faces], axis=0)
        gap += normal * (interp - pos)
        normals.append(normal)
    pressure = penalty * jnp.maximum(-gap, 0.0)
    push = [pressure * normal for normal in normals]
    spread = jnp.concatenate(
        [
            jnp.concatenate([jnp.where(line == t, p, 0.0) for p in push], axis=0).astype(bf16)
            for t in range(tiles)
        ],
        axis=1,
    )
    forces = jnp.dot(spread, weights, preferred_element_type=f32).astype(bf16)
    pad = out_ref.shape[0] - forces.shape[0]
    if pad:
        forces = jnp.concatenate([forces, jnp.zeros((pad, lanes), bf16)], axis=0)
    out_ref[...] = forces


def list_kernel(cap, tiles, force_rows, slots_ref, regions_ref, list_ref, run_of):
    parts = slots_ref.shape[0]
    nblk = regions_ref.shape[1]
    shift = cap.bit_length() - 1
    me = lax.axis_index("dom")
    for p in range(3):
        for q in range(nblk // cap):
            run_of[p * parts + regions_ref[p, q * cap]] = p * nblk + q * cap

    def pick(place, filled):
        j = me ^ place
        slots = [slots_ref[j, t] for t in range(tiles)]
        which = [(slot >> shift) - me + 1 for slot in slots]
        kept = [(p >= 0) & (p <= 2) for p in which]
        runs = [run_of[jnp.where(own, p, 0) * parts + j] for own, p in zip(kept, which)]
        places = []
        for own in kept:
            places.append(filled)
            filled = filled + jnp.where(own, 1, 0)
        for t in range(tiles):
            entry = (place * force_rows + t) * code + (slots[t] & (cap - 1)) + runs[t]
            list_ref[0, places[t]] = entry
        return filled

    filled = lax.fori_loop(0, parts, pick, jnp.int32(0))
    for i in range(24):
        list_ref[0, filled + i] = 0
    list_ref[0, list_ref.shape[1] - 1] = filled


def contact_kernel(tiles, list_ref, surf_ref, nodes_ref, part_ref, *refs):
    back_refs, out_ref, back, sums, total = refs[:-4], refs[-4], refs[-3], refs[-2], refs[-1]
    size = back_refs[0].shape[0]
    tops = part_ref.shape[0] // 6
    shared = nodes_ref.shape[0] // 4
    total[...] = part_ref[...]
    for i, ref in enumerate(back_refs):
        back[i * size : (i + 1) * size] = ref[...].astype(f32)
    filled = list_ref[0, list_ref.shape[1] - 1]

    def group(g):
        nodes, values = [], [[], [], []]
        for i in range(8):
            entry = list_ref[0, g * 8 + i]
            row = surf_ref[pl.ds(entry & (code - 1), 1)]
            nodes.append(jnp.where(g * 8 + i < filled, row, -1))
            for c in range(3):
                values[c].append(back[pl.ds((entry >> code_bits) + c * tiles, 1)])
        return node_sums(nodes, values, 3 * tops, 1)

    def spread(g, _):
        sums[...] += group(g)
        return 0

    sums[...] = group(0) + group(1) + group(2)
    lax.fori_loop(3, (filled + 7) // 8, spread, 0)
    pieces = [[sums[(c * 3 + p) * tops : (c * 3 + p + 1) * tops] for c in range(3)] for p in range(3)]
    found = []
    for p in (0, 2):
        at = (2 + p // 2) * shared
        found.append(
            lookup(
                [two_parts(piece) for piece in pieces[p]],
                [nodes_ref[at + k : at + k + 1] for k in range(shared)],
            )
        )
    added = node_sums(
        [nodes_ref[k : k + 1] for k in range(2 * shared)],
        [[near[c][k : k + 1] for near in found for k in range(shared)] for c in range(3)],
        tops,
    )
    added += jnp.concatenate(pieces[1], axis=0)
    for c in range(3):
        add_halves(total, added, c, tops)
    out_ref[...] = total[...].astype(bf16)


def accel_kernel(mass_ref, *refs):
    out_ref = refs[-1]
    terms = [ref[...].astype(f32) for ref in refs[:-1]]
    while len(terms) > 1:
        terms = [a + b for a, b in zip(terms[::2], terms[1::2])]
    size = mass_ref.shape[0]
    for c in range(3):
        at = slice(c * size, (c + 1) * size)
        out_ref[at] = terms[0][at] / mass_ref[...]


def swapped(block, start):
    lows = range(start, lax.axis_size("dom") - 1, 2)
    return lax.ppermute(block, "dom", [(s, s + 1) for s in lows] + [(s + 1, s) for s in lows])


def from_mate(block, distance):
    return lax.ppermute(
        block, "rep", [(i, i ^ distance) for i in range(lax.axis_size("rep"))]
    )


def across(block, distance):
    return lax.ppermute(
        block, "dom", [(s, s ^ distance) for s in range(lax.axis_size("dom"))]
    )


def on_device(
    coords,
    disp,
    mass,
    stiffness,
    elem_nodes,
    modulus,
    surf_nodes,
    block_region,
    face_pos,
    face_normal,
    tile_slot,
    tile_face,
    tile_weight,
    shared_lo,
    shared_hi,
):
    parts = lax.axis_size("dom")
    assert lax.axis_size("rep") == 4
    nodes_all = disp.shape[2]
    nblk = surf_nodes.shape[1]
    tiles = tile_slot.shape[1]
    cap = max(2, 2 * nblk // parts)
    rows = (3 * cap + 1 + 15) // 16 * 16
    force_rows = (3 * tiles + 15) // 16 * 16
    node_array = jax.ShapeDtypeStruct((3 * nodes_all // lanes, lanes), f32)
    mass_array = jax.ShapeDtypeStruct((nodes_all // lanes, lanes), f32)
    coords = coords.reshape(node_array.shape)
    disp = disp.reshape(node_array.shape)
    mass = mass.reshape(mass_array.shape)
    shared_lo = shared_lo.reshape(-1, lanes)
    shared_hi = shared_hi.reshape(-1, lanes)
    shared = shared_lo.shape[0]
    payload = jax.ShapeDtypeStruct((nblk + (shared + 8) // 8 * 8 + 4 * shared, lanes), f32)

    outgoing = call(
        functools.partial(pack_kernel, cap),
        jax.ShapeDtypeStruct((parts, rows, lanes), bf16),
        [hbm] * 5,
        vmem,
        [
            pltpu.VMEM((nblk // cap, rows, lanes), f32),
            pltpu.SMEM(block_region.shape, jnp.int32),
            pltpu.SMEM(tile_slot.shape, jnp.int32),
            pltpu.VMEM(coords.shape, f32),
            pltpu.VMEM(disp.shape, f32),
            pltpu.VMEM(surf_nodes.shape, jnp.int32),
            pltpu.SemaphoreType.DMA((5,)),
        ],
        1 << 30,
        60,
    )(block_region, tile_slot, coords, disp, surf_nodes)
    arrived = lax.all_to_all(outgoing, "dom", split_axis=0, concat_axis=0, tiled=True)

    part, first, second, tile_ids = call(
        element_kernel,
        (node_array, payload, payload, jax.ShapeDtypeStruct((2, tiles), jnp.int32)),
        [vmem] * 11,
        (vmem,) * 4,
        [
            pltpu.VMEM((24, modulus.shape[1]), f32),
            pltpu.VMEM((3 * nodes_all // wide, wide), f32),
        ],
        1 << 32,
    )(
        tile_slot,
        tile_face,
        disp,
        stiffness,
        modulus,
        elem_nodes,
        mass,
        shared_lo,
        shared_hi,
        surf_nodes,
        block_region,
    )
    second = swapped(second, 1)
    arrived, part = lax.optimization_barrier((arrived, part))
    forces, slots = call(
        functools.partial(tile_kernel, cap),
        (
            jax.ShapeDtypeStruct((force_rows, lanes), bf16),
            jax.ShapeDtypeStruct((parts, lanes), jnp.int32),
        ),
        [smem] + [vmem] * 4,
        (vmem, vmem),
        [pltpu.VMEM((parts * rows, lanes), f32)],
        1 << 28,
    )(
        tile_ids,
        arrived,
        jnp.swapaxes(face_pos, 1, 2),
        jnp.swapaxes(face_normal, 1, 2),
        tile_weight,
    )
    forces, first = lax.optimization_barrier((forces, first))
    held, distance = forces, 1
    while 4 * distance < parts:
        held = jnp.concatenate([held, across(held, distance)], axis=0)
        distance *= 2
    back = [held] + [across(held, d) for d in range(distance, parts, distance)]
    first = swapped(first, 0)
    part, mass, surf, nodes, regions = call(
        neighbour_kernel,
        (
            node_array,
            mass_array,
            jax.ShapeDtypeStruct((3 * nblk, lanes), jnp.int32),
            jax.ShapeDtypeStruct((4 * shared, lanes), jnp.int32),
            jax.ShapeDtypeStruct((3, nblk), jnp.int32),
        ),
        [vmem] * 8,
        (vmem,) * 5,
        [],
        1 << 26,
    )(part, mass, shared_lo, shared_hi, surf_nodes, block_region, first, second)
    picks = call(
        functools.partial(list_kernel, cap, tiles, force_rows),
        jax.ShapeDtypeStruct((1, parts * tiles + 32), jnp.int32),
        [smem, smem],
        smem,
        [pltpu.SMEM((3 * parts,), jnp.int32)],
        1 << 24,
    )(slots, regions)
    own = call(
        functools.partial(contact_kernel, tiles),
        jax.ShapeDtypeStruct(node_array.shape, bf16),
        [smem] + [vmem] * (3 + len(back)),
        vmem,
        [
            pltpu.VMEM((parts * force_rows, lanes), f32),
            pltpu.VMEM((9 * nodes_all // wide, wide), f32),
            pltpu.VMEM(node_array.shape, f32),
        ],
        1 << 28,
    )(picks, surf, nodes, part, *back)
    accel = call(accel_kernel, node_array, [vmem] * 5, vmem, [], 1 << 24)(
        mass, own, *[from_mate(own, k) for k in (3, 2, 1)]
    )
    return accel.reshape(1, 3, nodes_all)


def solution(mesh):
    in_specs = (
        P("dom", None, None),
        P("dom", None, None),
        P("dom", None),
        P(),
        P("dom", None, "rep"),
        P("dom", "rep"),
        P("dom", None, None),
        P("dom", None),
        P("dom", None, None, None),
        P("dom", None, None, None),
        P("dom", "rep"),
        P("dom", "rep"),
        P("dom", "rep", None, None),
        P("dom", None),
        P("dom", None),
    )
    out_specs = P("dom", None, None)
    return jax.shard_map(
        on_device, mesh=mesh, in_specs=in_specs, out_specs=out_specs, check_vma=False
    )
```
